128 devices in a mesh: lon: 16 (over z, y), lat: 8 (over x, core).
Axes of the slice: x: 4, y: 4, z: 4, core: 2. Of those that a mesh axis runs over, the one named last changes fastest.
Arguments:
- forcing: float32 [2, 8192, 4096], P(None, 'lon', 'lat'), may hold values from -6 to 6
- velocity: float32 [2, 32, 32, 16384], P(None, None, None, ('lon', 'lat')), may hold values from -4 to 4
- stress: float32 [3, 32, 32, 16384], P(None, None, None, ('lon', 'lat')), may hold values from -4 to 4
- mass: float32 [32, 32, 16384], P(None, None, ('lon', 'lat')), may hold values from 0.5 to 4
- strength: float32 [32, 32, 16384], P(None, None, ('lon', 'lat')), may hold values from 0.2 to 2
- owner: int32 [256, 128], replicated, may hold values from -1 to 16383, as said below
Outputs:
- new_velocity: float32 [2, 8192, 4096], P(None, 'lon', 'lat')
- new_stress: float32 [3, 32, 32, 16384], P(None, None, None, ('lon', 'lat'))
The draws below stay inside these ranges and needn't reach their ends.
Inputs may be any that keep to these rules, and one draw needn't show every extreme that they name: `owner`: the ice-covered blocks, taken ocean tile by ocean tile (tiles in the order of lon+lat, each tile the 16 x 16 blocks of one device of the forcing, row by row with latitude fastest) are numbered 0, 1, 2, ... in that order; all other blocks hold -1. There are exactly 16384 ice-covered blocks; a tile holds anywhere from none to all of its blocks, and some tile is fully ice-covered.
All inputs are finite; a program needn't handle non-finite values.
Results may differ from the reference program's by a relative error of at most 0.000073.
Values sent between devices are 32-bit elements; how exact they have to be, the bound alone decides.
No kernel may reach another device: no remote copies, remote signals or barrier semaphores. Data moves between devices by JAX's collectives and lax.ppermute only.
A program may use at most 192 MiB of HBM per device.

```python
import math
import jax
import jax.numpy as jnp

B = 32
BX_DEV = 16
BY_DEV = 16
ITERS = 6
SLOTS = 128
ICE_BLOCKS = 16384
NX = 8192
NY = 4096
N_LON = 16
N_LAT = 8


def shuffle_tile(tile_key):
    return jax.random.permutation(tile_key, BX_DEV * BY_DEV).astype(jnp.int32)


def draw_owner(key, part):
    key = jax.random.fold_in(key, 7)
    tile_count = BX_DEV * BY_DEV
    half_count = tile_count // 2
    pair_key, spot_key, order_key = jax.random.split(key, 3)
    lon_key, lat_key = jax.random.split(spot_key)
    offsets = jax.random.randint(pair_key, (N_LON // 2, N_LAT), -half_count, half_count + 1).astype(jnp.int32)
    spot_lon = jax.random.randint(lon_key, (), 0, N_LON // 2)
    spot_lat = jax.random.randint(lat_key, (), 0, N_LAT)
    offsets = offsets.at[spot_lon, spot_lat].set(half_count)
    counts = jnp.concatenate((half_count + offsets, half_count - offsets), axis=0)
    tile_keys = jax.random.split(order_key, N_LON * N_LAT)
    ranking = jax.vmap(shuffle_tile)(tile_keys)
    iced = ranking < counts.reshape(-1, 1)
    flat_iced = iced.reshape(-1)
    number = jnp.cumsum(flat_iced.astype(jnp.int32)) - 1
    number = jnp.where(flat_iced, number, -1)
    owner = number.reshape(N_LON, N_LAT, BX_DEV, BY_DEV).transpose(0, 2, 1, 3).reshape(BX_DEV * N_LON, BY_DEV * N_LAT)
    return owner.astype(jnp.int32)


def level_of(own_key, shape, cuts, least, largest):
    level, own = 1.0, jax.random.fold_in(own_key, 6)
    for dim, parts in cuts:
        steps = jnp.exp(jax.random.uniform(jax.random.fold_in(own, dim), (parts,), jnp.float32, least / len(cuts), largest / len(cuts)))
        level = level * jnp.repeat(steps, shape[dim] // parts).reshape([-1 if axis == dim else 1 for axis in range(len(shape))])
    return level


def normal_values(own_key, dims, width, most, pieces=(), kind=jnp.bfloat16):
    result = jax.random.normal(own_key, dims, jnp.float32) * width
    if len(pieces) > 0:
        result = level_of(own_key, dims, pieces, -0.22, 0.18) * result
    return jnp.clip(result, min=-most, max=most).astype(kind)


def setup_inputs(seed: int = 0) -> dict:
    streams_of = jax.random.split(jax.random.key(seed), 7)
    return {
        "forcing": normal_values(streams_of[0], (2, NX, NY), 1.0, 6.0, ((1, 16), (2, 8)), jnp.float32),
        "velocity": normal_values(streams_of[1], (2, B, B, ICE_BLOCKS), 0.5, 4.0, ((3, 128),), jnp.float32),
        "stress": normal_values(streams_of[2], (3, B, B, ICE_BLOCKS), 0.5, 4.0, ((3, 128),), jnp.float32),
        "mass": jnp.clip(jnp.exp(math.log(4.0) - 2.0794415 * jax.random.uniform(streams_of[3], (B, B, ICE_BLOCKS), jnp.float32) ** level_of(streams_of[3], (B, B, ICE_BLOCKS), ((2, 128),), -0.2, 0.2)), 0.5, 4.0),
        "strength": jnp.clip(jnp.exp(math.log(2.0) - 2.3025851 * jax.random.uniform(streams_of[4], (B, B, ICE_BLOCKS), jnp.float32) ** level_of(streams_of[4], (B, B, ICE_BLOCKS), ((2, 128),), -0.2, 0.2)), 0.2, 2.0),
        "owner": draw_owner(jax.random.fold_in(streams_of[6], 71), 0),
    }


ECC_SQUARED = 4.0
DELTA_MIN = 0.5
RELAX_RATE = 1.0
TIME_STEP = 0.5
WATER_DRAG = 1.0
CORIOLIS = 0.5

def stress_step(zonal_vel, merid_vel, zonal_east, merid_east, zonal_north, merid_north, stress_sum, stress_diff, stress_shear, strength):
    grad_zonal_x = zonal_east - zonal_vel
    grad_merid_y = merid_north - merid_vel
    grad_zonal_y = zonal_north - zonal_vel
    grad_merid_x = merid_east - merid_vel
    divergence = grad_zonal_x + grad_merid_y
    tension = grad_zonal_x - grad_merid_y
    shearing = grad_zonal_y + grad_merid_x
    spread = jnp.sqrt(divergence * divergence + (tension * tension + shearing * shearing) / ECC_SQUARED + DELTA_MIN * DELTA_MIN)
    weight = strength / spread
    new_sum = (stress_sum + RELAX_RATE * (weight * divergence - strength)) / (1.0 + RELAX_RATE)
    new_diff = (stress_diff + RELAX_RATE * weight * tension / ECC_SQUARED) / (1.0 + RELAX_RATE)
    new_shear = (stress_shear + RELAX_RATE * 0.5 * weight * shearing / ECC_SQUARED) / (1.0 + RELAX_RATE)
    return (new_sum, new_diff, new_shear)

def momentum_step(zonal_vel, merid_vel, stress_sum, stress_diff, stress_shear, west_sum, west_diff, west_shear, south_sum, south_diff, south_shear, mass, force_zonal, force_merid, coriolis):
    normal_xx = 0.5 * (stress_sum + stress_diff)
    normal_xx_west = 0.5 * (west_sum + west_diff)
    normal_yy = 0.5 * (stress_sum - stress_diff)
    normal_yy_south = 0.5 * (south_sum - south_diff)
    push_zonal = normal_xx - normal_xx_west + (stress_shear - south_shear)
    push_merid = stress_shear - west_shear + (normal_yy - normal_yy_south)
    damping = mass + TIME_STEP * WATER_DRAG
    new_zonal = (mass * zonal_vel + TIME_STEP * (push_zonal + force_zonal) + TIME_STEP * mass * coriolis * merid_vel) / damping
    new_merid = (mass * merid_vel + TIME_STEP * (push_merid + force_merid) - TIME_STEP * mass * coriolis * zonal_vel) / damping
    return (new_zonal, new_merid)

def reference(forcing, velocity, stress, mass, strength, owner):
    devices = N_LON * N_LAT
    block_x = owner.shape[0]
    block_y = owner.shape[1]
    iced = owner >= 0
    slot_index = jnp.where(iced, owner % devices * SLOTS + owner // devices, 0).astype(jnp.int32).reshape(-1)
    block_mask = iced.astype(jnp.float32).reshape(-1)

    def to_grid(blocks):
        picked = jnp.take(blocks, slot_index, axis=2) * block_mask
        return picked.reshape(B, B, block_x, block_y).transpose(2, 0, 3, 1).reshape(NX, NY)

    def north_of(field):
        return jnp.concatenate((field[:, 1:], jnp.zeros((NX, 1), jnp.float32)), axis=1)

    def south_of(field):
        return jnp.concatenate((jnp.zeros((NX, 1), jnp.float32), field[:, :-1]), axis=1)
    cell_mask = jnp.repeat(jnp.repeat(iced.astype(jnp.float32), B, axis=0), B, axis=1)
    coriolis = CORIOLIS * (2.0 * (jnp.arange(NY, dtype=jnp.float32) + 0.5) / NY - 1.0)
    zonal = to_grid(velocity[0])
    merid = to_grid(velocity[1])
    stress_sum = to_grid(stress[0])
    stress_diff = to_grid(stress[1])
    stress_shear = to_grid(stress[2])
    mass_grid = to_grid(mass)
    strength_grid = to_grid(strength)
    for step in range(ITERS):
        new_sum, new_diff, new_shear = stress_step(zonal, merid, jnp.roll(zonal, -1, axis=0), jnp.roll(merid, -1, axis=0), north_of(zonal), north_of(merid), stress_sum, stress_diff, stress_shear, strength_grid)
        stress_sum = new_sum * cell_mask
        stress_diff = new_diff * cell_mask
        stress_shear = new_shear * cell_mask
        new_zonal, new_merid = momentum_step(zonal, merid, stress_sum, stress_diff, stress_shear, jnp.roll(stress_sum, 1, axis=0), jnp.roll(stress_diff, 1, axis=0), jnp.roll(stress_shear, 1, axis=0), south_of(stress_sum), south_of(stress_diff), south_of(stress_shear), mass_grid, forcing[0], forcing[1], coriolis)
        zonal = new_zonal * cell_mask
        merid = new_merid * cell_mask
    inverse = jnp.zeros((ICE_BLOCKS,), jnp.int32).at[jnp.where(iced.reshape(-1), slot_index, ICE_BLOCKS)].set(jnp.arange(block_x * block_y, dtype=jnp.int32), mode='drop')

    def to_slots(grid):
        blocks = grid.reshape(block_x, B, block_y, B).transpose(1, 3, 0, 2).reshape(B, B, block_x * block_y)
        return jnp.take(blocks, inverse, axis=2)
    return (jnp.stack((zonal, merid)), jnp.stack((to_slots(stress_sum), to_slots(stress_diff), to_slots(stress_shear))))
```

```python
import jax
import jax.numpy as jnp
from jax import lax
from jax.experimental import pallas as pl
from jax.experimental.pallas import tpu as pltpu
from jax.sharding import PartitionSpec as P

B = 32
BX_DEV = 16
BY_DEV = 16
ITERS = 6
LANES = 128
CORIOLIS = 0.5
HALO = 6
FIELDS = 7
ROWS = BX_DEV * B
COLS = BY_DEV * B
WIDE = COLS + LANES
RIM = 4 * (FIELDS + 2)
GROUPS = ROWS // 8 + 2
CHUNK = 24
TAIL = CHUNK + 8


def lane_ids(shape):
    return lax.broadcasted_iota(jnp.int32, shape, len(shape) - 1)


def row_ids(shape):
    return lax.broadcasted_iota(jnp.int32, shape, len(shape) - 2)


def swap_groups(parts):
    lane = lane_ids((8, LANES))
    low = lane < 64
    even = (lane // 32) % 2 == 0
    lo, hi = [], []
    for p in range(2):
        lo.append(jnp.where(low, parts[p], pltpu.roll(parts[p + 2], 64, 1)))
        hi.append(jnp.where(low, pltpu.roll(parts[p], 64, 1), parts[p + 2]))
    out = []
    for pair in (lo, hi):
        out.append(jnp.where(even, pair[0], pltpu.roll(pair[1], 32, 1)))
        out.append(jnp.where(even, pltpu.roll(pair[0], 96, 1), pair[1]))
    return out


def pack_kernel(pos_ref, vel_ref, str_ref, mass_ref, strength_ref, out_ref, scr_ref):
    slots = vel_ref.shape[-1]

    def turn(field, load):
        for s in range(8):
            rows = jnp.concatenate([load(8 * q + s) for q in range(4)], axis=0)
            scr_ref[field, pl.ds(s, slots, stride=8), :] = rows.T

    for c in range(2):
        turn(c, lambda ci, c=c: vel_ref[c, ci])
    for c in range(3):
        turn(2 + c, lambda ci, c=c: str_ref[c, ci])
    turn(5, lambda ci: mass_ref[ci])
    turn(6, lambda ci: strength_ref[ci])

    def scatter(slot, carry):
        place = pos_ref[slot]
        for field in range(FIELDS):
            out_ref[place, field] = scr_ref[field, pl.ds(pl.multiple_of(slot * 8, 8), 8), :]
        return carry

    lax.fori_loop(0, slots, scatter, 0, unroll=4)


def block_of(tile_ref, recv_ref, bx, by, half, field):
    number = tile_ref[bx, by]
    source = number & (recv_ref.shape[0] // 2 - 1)
    value = recv_ref[source * 2 + half, field]
    return jnp.where(number >= 0, value, 0.0)


def strips_kernel(tile_ref, recv_ref, force_ref, north_ref, south_ref, east_ref, west_ref):
    lane = lane_ids((8, LANES))
    in_group = lane % 32

    for bx, ref, group in ((0, east_ref, 0), (BX_DEV - 1, west_ref, 3)):
        for part in range(4):
            cols = pl.ds(part * LANES, LANES)
            for field in range(FIELDS):
                total = jnp.zeros((8, LANES), jnp.float32)
                for p in range(4):
                    got = block_of(tile_ref, recv_ref, bx, part * 4 + p, int(bx >= 8), field)
                    turned = pltpu.roll(got, ((p - group) * 32) % LANES, 1) if p != group else got
                    total = jnp.where(lane // 32 == p, turned, total)
                ref[field * 4 + part] = total
            for c in range(2):
                ref[(FIELDS + c) * 4 + part] = force_ref[c, pl.ds(bx * B + group * 8, 8), cols]

    def lat_rims(half):
        def body(bx, carry):
            for by, ref, first in ((0, north_ref, 0), (BY_DEV - 1, south_ref, B - HALO)):
                for v in range(2):
                    total = jnp.zeros((8, LANES), jnp.float32)
                    for k in range(5):
                        field = v * 5 + k
                        if field >= FIELDS + 2:
                            continue
                        mine = (in_group >= HALO * k) & (in_group < HALO * (k + 1))
                        if field < FIELDS:
                            got = block_of(tile_ref, recv_ref, bx, by, half, field)
                            got = pltpu.roll(got, (HALO * k - first) % LANES, 1)
                            total = jnp.where(mine, got, total)
                        else:
                            col = (by // 4) * LANES
                            lead = (by % 4) * 32 + first
                            for q in range(4):
                                rows = pl.ds(pl.multiple_of(bx * B + q * 8, 8), 8)
                                got = force_ref[field - FIELDS, rows, pl.ds(col, LANES)]
                                got = pltpu.roll(got, (q * 32 + HALO * k - lead) % LANES, 1)
                                total = jnp.where(mine & (lane // 32 == q), got, total)
                    ref[bx, v] = total
            return carry

        return body

    lax.fori_loop(0, BX_DEV // 2, lat_rims(0), 0)
    lax.fori_loop(BX_DEV // 2, BX_DEV, lat_rims(1), 0)


def tile_kernel(
    tile_ref,
    lat_ref,
    recv_ref,
    force_ref,
    north_ref,
    south_ref,
    east_ref,
    west_ref,
    vel_out_ref,
    send_out_ref,
    z_ref,
    m_ref,
    p_ref,
    q_ref,
    s_ref,
    a_ref,
    b_ref,
    fx_ref,
    fy_ref,
    w_ref,
    send_ref,
    sems,
):
    lane = lane_ids((8, LANES))
    count = recv_ref.shape[0] // 2
    states = (z_ref, m_ref, p_ref, q_ref, s_ref)

    def prepare(row, cols, zonal, merid, total, diff, shear, mass, strength, fzonal, fmerid):
        drag = jnp.where(mass > 0.0, 0.5 / (mass + 0.5), 0.0)
        rows = pl.ds(row, 8)
        z_ref[rows, cols] = zonal
        m_ref[rows, cols] = merid
        p_ref[rows, cols] = 0.5 * (total + diff)
        q_ref[rows, cols] = 0.5 * (total - diff)
        s_ref[rows, cols] = shear
        a_ref[rows, cols] = 2.0 * mass * drag
        b_ref[rows, cols] = drag
        fx_ref[rows, cols] = drag * fzonal
        fy_ref[rows, cols] = drag * fmerid
        w_ref[rows, cols] = 0.25 * strength

    def unpack(half):
        def body(bx, carry):
            for part in range(4):
                cols = pl.ds(part * LANES, LANES)
                numbers = [tile_ref[bx, part * 4 + p] for p in range(4)]
                sources = [(n & (count - 1)) * 2 + half for n in numbers]
                fields = []
                for field in range(FIELDS):
                    got = [
                        jnp.where(numbers[p] >= 0, recv_ref[sources[p], field], 0.0)
                        for p in range(4)
                    ]
                    fields.append(swap_groups(got))
                for q in range(4):
                    row = pl.multiple_of(bx * B + q * 8, 8)
                    force = [force_ref[c, pl.ds(row, 8), cols] for c in range(2)]
                    prepare(
                        pl.multiple_of(row + 16, 8), cols, *[field[q] for field in fields], *force
                    )
            return carry

        return body

    lax.fori_loop(0, BX_DEV // 2, unpack(0), 0)
    lax.fori_loop(BX_DEV // 2, BX_DEV, unpack(1), 0)

    side = pl.ds(COLS, LANES)
    is_north = lane < HALO
    is_south = lane >= LANES - HALO

    def side_columns(bx, carry):
        for q in range(4):
            fields = []
            for field in range(FIELDS + 2):
                v, k = divmod(field, 5)
                lead = q * 32 + HALO * k
                north = pltpu.roll(north_ref[bx, v], (-lead) % LANES, 1)
                south = pltpu.roll(south_ref[bx, v], (LANES - HALO - lead) % LANES, 1)
                fields.append(jnp.where(is_north, north, jnp.where(is_south, south, 0.0)))
            prepare(pl.multiple_of(bx * B + q * 8 + 16, 8), side, *fields)
        return carry

    lax.fori_loop(0, BX_DEV, side_columns, 0)

    for ref, row, group in ((west_ref, 8, 3), (east_ref, ROWS + 16, 0)):
        for part in range(4):
            cols = pl.ds(part * LANES, LANES)
            prepare(row, cols, *[ref[field * 4 + part] for field in range(FIELDS + 2)])
        fields = []
        for field in range(FIELDS + 2):
            v, k = divmod(field, 5)
            lead = group * 32 + HALO * k
            north = pltpu.roll(ref[RIM + v], (-lead) % LANES, 1)
            south = pltpu.roll(ref[RIM + 2 + v], (LANES - HALO - lead) % LANES, 1)
            fields.append(jnp.where(is_north, north, jnp.where(is_south, south, 0.0)))
        prepare(row, side, *fields)

    for ref in states + (w_ref,):
        ref[pl.ds(0, 8), :] = jnp.zeros((8, WIDE), jnp.float32)
        ref[pl.ds(ROWS + 24, TAIL), :] = jnp.zeros((TAIL, WIDE), jnp.float32)

    wide_lane = lane_ids((1, WIDE))
    cell = jnp.where(wide_lane < COLS + 8, wide_lane, wide_lane - WIDE) + lat_ref[0] * COLS
    half_coriolis = (0.5 * CORIOLIS) * (
        2.0 * (cell.astype(jnp.float32) + 0.5) / (lat_ref[1] * COLS).astype(jnp.float32) - 1.0
    )
    sub = row_ids((CHUNK, WIDE))
    first_row = sub == 0
    last_row = sub == CHUNK - 1

    def stress_part(row):
        here = pl.ds(row, CHUNK)
        after = pl.ds(pl.multiple_of(row + CHUNK, 8), 8)
        z, m, w = z_ref[here, :], m_ref[here, :], w_ref[here, :]
        p, q, s = p_ref[here, :], q_ref[here, :], s_ref[here, :]
        z_next, m_next = z_ref[after, :], m_ref[after, :]

        def east(x, follow):
            return pltpu.roll(jnp.where(first_row, jnp.broadcast_to(follow[:1], x.shape), x), CHUNK - 1, 0)

        def run():
            gx = east(z, z_next) - z
            hx = east(m, m_next) - m
            gy = pltpu.roll(m, WIDE - 1, 1) - m
            hy = pltpu.roll(z, WIDE - 1, 1) - z
            div = gx + gy
            ten = gx - gy
            she = hy + hx
            weight = w * lax.rsqrt(div * div + 0.25 * (ten * ten + she * she) + 0.25)
            quarter = 0.25 * weight
            mean = weight * div - w
            dev = quarter * ten
            return 0.5 * p + (mean + dev), 0.5 * q + (mean - dev), 0.5 * s + quarter * she

        def keep(values):
            p_ref[here, :], q_ref[here, :], s_ref[here, :] = values

        return run, keep

    def momentum_part(row):
        here = pl.ds(row, CHUNK)
        before = pl.ds(pl.multiple_of(row - 8, 8), 8)
        z, m, a, b = z_ref[here, :], m_ref[here, :], a_ref[here, :], b_ref[here, :]
        p, q, s = p_ref[here, :], q_ref[here, :], s_ref[here, :]
        fx, fy = fx_ref[here, :], fy_ref[here, :]
        p_last, s_last = p_ref[before, :], s_ref[before, :]

        def west(x, lead):
            return pltpu.roll(jnp.where(last_row, jnp.broadcast_to(lead[7:], x.shape), x), 1, 0)

        def run():
            push_x = (p - west(p, p_last)) + (s - pltpu.roll(s, 1, 1))
            push_y = (s - west(s, s_last)) + (q - pltpu.roll(q, 1, 1))
            turn = a * half_coriolis
            return a * z + b * push_x + fx + turn * m, a * m + b * push_y + fy - turn * z

        def keep(values):
            z_ref[here, :], m_ref[here, :] = values

        return run, keep

    def sweep(step, carry):
        run, keep = stress_part(8)
        keep(run())

        def body(c, carry):
            row = pl.multiple_of(8 + c * CHUNK, 8)
            run_stress, keep_stress = stress_part(pl.multiple_of(row + CHUNK, 8))
            run_momentum, keep_momentum = momentum_part(row)
            stresses = run_stress()
            velocities = run_momentum()
            keep_stress(stresses)
            keep_momentum(velocities)
            return carry

        return lax.fori_loop(0, 8 * GROUPS // CHUNK, body, carry)

    lax.fori_loop(0, ITERS, sweep, 0)

    copies = [
        pltpu.make_async_copy(
            ref.at[pl.ds(16, ROWS), pl.ds(0, COLS)], vel_out_ref.at[c], sems.at[c]
        )
        for c, ref in enumerate((z_ref, m_ref))
    ]
    for copy in copies:
        copy.start()

    def repack(half):
        def body(bx, carry):
            for part in range(4):
                cols = pl.ds(part * LANES, LANES)
                fields = ([], [], [])
                for q in range(4):
                    rows = pl.ds(pl.multiple_of(bx * B + q * 8 + 16, 8), 8)
                    pv, qv = p_ref[rows, cols], q_ref[rows, cols]
                    fields[0].append(pv + qv)
                    fields[1].append(pv - qv)
                    fields[2].append(s_ref[rows, cols])
                fields = [swap_groups(field) for field in fields]
                for p in range(4):
                    number = tile_ref[bx, part * 4 + p]
                    place = jnp.where(number >= 0, (number & (count - 1)) * 2 + half, 2 * count)
                    for c in range(3):
                        send_ref[place, c] = fields[c][p]
            return carry

        return body

    lax.fori_loop(0, BX_DEV // 2, repack(0), 0)
    lax.fori_loop(BX_DEV // 2, BX_DEV, repack(1), 0)
    last = pltpu.make_async_copy(send_ref.at[pl.ds(0, 2 * count)], send_out_ref, sems.at[2])
    last.start()
    for copy in copies + [last]:
        copy.wait()


def unpack_kernel(pos_ref, recv_ref, out_ref, scr_ref):
    slots = out_ref.shape[-1]

    def gather(slot, carry):
        place = pos_ref[slot]
        for c in range(3):
            scr_ref[c, pl.ds(pl.multiple_of(slot * 8, 8), 8), :] = recv_ref[place, c]
        return carry

    lax.fori_loop(0, slots, gather, 0, unroll=4)
    for c in range(3):
        for s in range(8):
            turned = scr_ref[c, pl.ds(s, slots, stride=8), :].T
            for q in range(4):
                out_ref[c, 8 * q + s] = turned[q * B : (q + 1) * B]


VMEM = pl.BlockSpec(memory_space=pltpu.VMEM)
SMEM = pl.BlockSpec(memory_space=pltpu.SMEM)
ANY = pl.BlockSpec(memory_space=pl.ANY)


def params(mebibytes):
    return pltpu.CompilerParams(vmem_limit_bytes=mebibytes * 1024 * 1024)


def f32(*shape):
    return jax.ShapeDtypeStruct(shape, jnp.float32)


def on_device(forcing, velocity, stress, mass, strength, owner):
    lon_count = lax.axis_size("lon")
    lat_count = lax.axis_size("lat")
    devices = lon_count * lat_count
    lat_index = lax.axis_index("lat")
    lon_index = lax.axis_index("lon")
    own_index = lon_index * lat_count + lat_index
    slots = velocity.shape[-1]

    iced = (owner >= 0).astype(jnp.int32)
    counts = jnp.sum(iced.reshape(lon_count, 2, BX_DEV // 2, lat_count, BY_DEV), axis=(2, 4))
    ends = jnp.cumsum(counts.transpose(0, 2, 1).reshape(-1))
    numbers = jnp.arange(slots, dtype=jnp.int32) * devices + own_index
    pos = jnp.sum((ends[None, :] <= numbers[:, None]).astype(jnp.int32), axis=1)
    my_tile = lax.dynamic_slice(owner, (lon_index * BX_DEV, lat_index * BY_DEV), (BX_DEV, BY_DEV))

    send = pl.pallas_call(
        pack_kernel,
        out_shape=f32(devices * 2, FIELDS, 8, LANES),
        in_specs=[SMEM] + [VMEM] * 4,
        out_specs=VMEM,
        scratch_shapes=[pltpu.VMEM((FIELDS, slots * 8, LANES), jnp.float32)],
        compiler_params=params(24),
    )(pos, velocity, stress, mass, strength)
    recv = lax.all_to_all(
        send.reshape(devices, 2 * FIELDS, 8, LANES), ("lon", "lat"), 0, 0, tiled=True
    ).reshape(devices * 2, FIELDS, 8, LANES)

    north, south, east, west = pl.pallas_call(
        strips_kernel,
        out_shape=(f32(BX_DEV, 2, 8, LANES),) * 2 + (f32(RIM, 8, LANES),) * 2,
        in_specs=[SMEM, VMEM, VMEM],
        out_specs=(VMEM,) * 4,
        compiler_params=params(16),
    )(my_tile, recv, forcing)

    ahead = [(j, j + 1) for j in range(lat_count - 1)]
    got_north = lax.ppermute(north, "lat", [(k, j) for j, k in ahead])
    got_south = lax.ppermute(south, "lat", ahead)
    ring = [(i, (i + 1) % lon_count) for i in range(lon_count)]
    east = jnp.concatenate((east, got_north[0], got_south[0]), axis=0)
    west = jnp.concatenate((west, got_north[-1], got_south[-1]), axis=0)
    got_east = lax.ppermute(east, "lon", [(k, i) for i, k in ring])
    got_west = lax.ppermute(west, "lon", ring)
    work = pltpu.VMEM((ROWS + 24 + TAIL, WIDE), jnp.float32)
    new_velocity, back = pl.pallas_call(
        tile_kernel,
        out_shape=(f32(2, ROWS, COLS), f32(devices * 2, 3, 8, LANES)),
        in_specs=[SMEM, SMEM] + [VMEM] * 6,
        out_specs=(ANY, ANY),
        scratch_shapes=[work] * 10
        + [
            pltpu.VMEM((devices * 2 + 1, 3, 8, LANES), jnp.float32),
            pltpu.SemaphoreType.DMA((3,)),
        ],
        compiler_params=params(40),
    )(
        my_tile,
        jnp.stack((lat_index, lat_count)).astype(jnp.int32),
        recv,
        forcing,
        got_north,
        got_south,
        got_east,
        got_west,
    )
    returned = lax.all_to_all(
        back.reshape(devices, 6, 8, LANES), ("lon", "lat"), 0, 0, tiled=True
    ).reshape(devices * 2, 3, 8, LANES)
    new_stress = pl.pallas_call(
        unpack_kernel,
        out_shape=f32(3, B, B, slots),
        in_specs=[SMEM, VMEM],
        out_specs=VMEM,
        scratch_shapes=[pltpu.VMEM((3, slots * 8, LANES), jnp.float32)],
        compiler_params=params(16),
    )(pos, returned)
    return (new_velocity, new_stress)


def solution(mesh):
    in_specs = (
        P(None, "lon", "lat"),
        P(None, None, None, ("lon", "lat")),
        P(None, None, None, ("lon", "lat")),
        P(None, None, ("lon", "lat")),
        P(None, None, ("lon", "lat")),
        P(),
    )
    out_specs = (P(None, "lon", "lat"), P(None, None, None, ("lon", "lat")))
    return jax.shard_map(
        on_device, mesh=mesh, in_specs=in_specs, out_specs=out_specs, check_vma=False
    )
```

```python
import jax
import jax.numpy as jnp
import numpy as np
from jax import lax
from jax.experimental import pallas as pl
from jax.experimental.pallas import tpu as pltpu
from jax.sharding import PartitionSpec as P

B = 32
BX_DEV = 16
BY_DEV = 16
ITERS = 6
LANES = 128
CORIOLIS = 0.5
HALO = 6
FIELDS = 7
ROWS = BX_DEV * B
COLS = BY_DEV * B
RIM = 4 * (FIELDS + 2)
SIDE = BX_DEV + 2
GRID_LANES = -(-SIDE * SIDE // LANES) * LANES


def lane_ids(shape):
    return lax.broadcasted_iota(jnp.int32, shape, len(shape) - 1)


def row_ids(shape):
    return lax.broadcasted_iota(jnp.int32, shape, len(shape) - 2)


def swap_groups(parts):
    lane = lane_ids((8, LANES))
    low = lane < 64
    even = (lane // 32) % 2 == 0
    lo, hi = [], []
    for p in range(2):
        lo.append(jnp.where(low, parts[p], pltpu.roll(parts[p + 2], 64, 1)))
        hi.append(jnp.where(low, pltpu.roll(parts[p], 64, 1), parts[p + 2]))
    out = []
    for pair in (lo, hi):
        out.append(jnp.where(even, pair[0], pltpu.roll(pair[1], 32, 1)))
        out.append(jnp.where(even, pltpu.roll(pair[0], 96, 1), pair[1]))
    return out


def grid_rows(bx, by):
    return pl.ds(pl.multiple_of(((bx + 1) * SIDE + by + 1) * 8, 8), 8)


def pack_kernel(
    own_ref,
    owner_ref,
    vel_hbm,
    str_hbm,
    mass_hbm,
    strength_hbm,
    send_ref,
    pos_ref,
    vel_ref,
    str_ref,
    mass_ref,
    strength_ref,
    scr_ref,
    place_ref,
    sems,
):
    slots = vel_ref.shape[-1]
    lon_count = owner_ref.shape[0] // BX_DEV
    lat_count = owner_ref.shape[1] // BY_DEV
    devices = lon_count * lat_count
    fetches = [
        pltpu.make_async_copy(src, dst, sems.at[i])
        for i, (src, dst) in enumerate(
            (
                (vel_hbm, vel_ref),
                (str_hbm, str_ref),
                (mass_hbm, mass_ref),
                (strength_hbm, strength_ref),
            )
        )
    ]
    for fetch in fetches:
        fetch.start()

    half_rows = BX_DEV // 2
    columns = owner_ref.shape[1]

    def dot(x, y):
        return jnp.dot(
            x.astype(jnp.bfloat16), y.astype(jnp.bfloat16), preferred_element_type=jnp.float32
        )

    def square(rows, cols):
        return (
            lax.broadcasted_iota(jnp.int32, (rows, cols), 0),
            lax.broadcasted_iota(jnp.int32, (rows, cols), 1),
        )

    row, col = square(columns, devices)
    of_lat = jnp.where(row // BY_DEV == col % lat_count, 1.0, 0.0)
    iced = jnp.where(owner_ref[...] >= 0, 1.0, 0.0)
    row, col = square(2 * lon_count, owner_ref.shape[0])
    of_half = jnp.where(col // half_rows == row, 1.0, 0.0)
    per_tile = dot(dot(of_half, iced), of_lat)
    row, col = square(2 * lon_count, devices)
    mine = row // 2 == col // lat_count
    counts = [
        jnp.sum(jnp.where(mine & (row % 2 == h), per_tile, 0.0), axis=0, keepdims=True)
        for h in range(2)
    ]
    row, col = square(devices, devices)
    upto = jnp.where(row <= col, 1.0, 0.0)
    both = jnp.broadcast_to(counts[0] + counts[1], (8, devices))
    end_second = dot(both, upto)[:1]
    end_first = end_second - counts[1]
    number = (lax.broadcasted_iota(jnp.int32, (devices, slots), 1) * devices + own_ref[0]).astype(
        jnp.float32
    )
    place = jnp.zeros((1, slots), jnp.float32)
    for end in (end_first, end_second):
        column = jnp.broadcast_to(end, (devices, devices)).T[:, :1]
        place = place + jnp.sum(jnp.where(column <= number, 1.0, 0.0), axis=0, keepdims=True)
    pos_ref[...] = place.astype(jnp.int32)
    to_scalar = pltpu.make_async_copy(pos_ref, place_ref, sems.at[4])
    to_scalar.start()

    def turn(field, load):
        for s in range(8):
            rows = jnp.concatenate([load(8 * q + s) for q in range(4)], axis=0)
            scr_ref[field, pl.ds(s, slots, stride=8), :] = rows.T

    fetches[0].wait()
    for c in range(2):
        turn(c, lambda ci, c=c: vel_ref[c, ci])
    fetches[1].wait()
    for c in range(3):
        turn(2 + c, lambda ci, c=c: str_ref[c, ci])
    fetches[2].wait()
    turn(5, lambda ci: mass_ref[ci])
    fetches[3].wait()
    turn(6, lambda ci: strength_ref[ci])
    to_scalar.wait()

    def scatter(slot, carry):
        spot = place_ref[0, slot]
        rows = pl.ds(pl.multiple_of(slot * 8, 8), 8)
        pltpu.make_async_copy(scr_ref.at[:, rows, :], send_ref.at[spot], sems.at[5]).start()
        return carry

    lax.fori_loop(0, slots, scatter, 0, unroll=4)
    pltpu.make_async_copy(send_ref.at[pl.ds(0, slots)], send_ref.at[pl.ds(0, slots)], sems.at[5]).wait()


def strips_kernel(
    tile_ref,
    recv_hbm,
    force_ref,
    north_ref,
    south_ref,
    east_ref,
    west_ref,
    edge_ref,
    sem,
):
    lane = lane_ids((8, LANES))
    in_group = lane % 32
    count = recv_hbm.shape[0] // 2
    half = BX_DEV // 2

    def fetch(i, carry):
        for side, (bx, by) in enumerate(((i, 0), (i, BY_DEV - 1), (0, i), (BX_DEV - 1, i))):
            source = (tile_ref[bx, by] & (count - 1)) * 2 + jnp.int32(bx >= half)
            pltpu.make_async_copy(recv_hbm.at[source], edge_ref.at[side * BX_DEV + i], sem).start()
        return carry

    lax.fori_loop(0, BX_DEV, fetch, 0)
    pltpu.make_async_copy(recv_hbm.at[pl.ds(0, 4 * BX_DEV)], edge_ref, sem).wait()

    def block_of(side, bx, by, field):
        if field >= FIELDS:
            return force_ref[bx * BY_DEV + by, field - FIELDS]
        value = edge_ref[side * BX_DEV + (bx if side < 2 else by), field]
        return jnp.where(tile_ref[bx, by] >= 0, value, 0.0)

    for side, bx, ref, group in ((2, 0, east_ref, 0), (3, BX_DEV - 1, west_ref, 3)):
        for part in range(4):
            for field in range(FIELDS + 2):
                total = jnp.zeros((8, LANES), jnp.float32)
                for p in range(4):
                    got = block_of(side, bx, part * 4 + p, field)
                    turned = pltpu.roll(got, ((p - group) * 32) % LANES, 1) if p != group else got
                    total = jnp.where(lane // 32 == p, turned, total)
                ref[field * 4 + part] = total

    def lat_rims(bx, carry):
        for side, by, ref, first in (
            (0, 0, north_ref, 0),
            (1, BY_DEV - 1, south_ref, B - HALO),
        ):
            for v in range(2):
                total = jnp.zeros((8, LANES), jnp.float32)
                for k in range(min(5, FIELDS + 2 - v * 5)):
                    mine = (in_group >= HALO * k) & (in_group < HALO * (k + 1))
                    got = block_of(side, bx, by, v * 5 + k)
                    got = pltpu.roll(got, (HALO * k - first) % LANES, 1)
                    total = jnp.where(mine, got, total)
                ref[bx, v] = total
        return carry

    lax.fori_loop(0, BX_DEV, lat_rims, 0)


def collect_kernel(tile_ref, recv_ref, force_ref, scr_ref):
    count = recv_ref.shape[0] // 2
    rest = SIDE * SIDE * 8
    for field in range(FIELDS + 2):
        scr_ref[field, pl.ds(rest, GRID_LANES * 8 - rest), :] = jnp.zeros(
            (GRID_LANES * 8 - rest, LANES), jnp.float32
        )

    def collect(bx, carry):
        half = jnp.int32(bx >= BX_DEV // 2)
        for by in range(BY_DEV):
            number = tile_ref[bx, by]
            source = (number & (count - 1)) * 2 + half
            iced = number >= 0
            for field in range(FIELDS):
                scr_ref[field, grid_rows(bx, by), :] = jnp.where(
                    iced, recv_ref[source, field], 0.0
                )
            for c in range(2):
                scr_ref[FIELDS + c, grid_rows(bx, by), :] = force_ref[bx * BY_DEV + by, c]
        return carry

    lax.fori_loop(0, BX_DEV, collect, 0)


def force_kernel(force_ref, out_ref):
    def body(bx, carry):
        for part in range(4):
            for c in range(2):
                rows = [
                    force_ref[
                        c,
                        pl.ds(pl.multiple_of(bx * B + 8 * q, 8), 8),
                        pl.ds(part * LANES, LANES),
                    ]
                    for q in range(4)
                ]
                for p, block in enumerate(swap_groups(rows)):
                    out_ref[bx * BY_DEV + part * 4 + p, c] = block
        return carry

    lax.fori_loop(0, BX_DEV, body, 0)


def velocity_kernel(vel_ref, out_ref, scr_ref):
    for c in range(2):
        for t in range(GRID_LANES // LANES):
            for s in range(8):
                cells = [vel_ref[c, 8 * q + s, :, pl.ds(t * LANES, LANES)] for q in range(4)]
                scr_ref[c, pl.ds(t * 8 * LANES + s, LANES, stride=8), :] = jnp.concatenate(
                    cells, axis=0
                ).T

    def body(bx, carry):
        for part in range(4):
            for c in range(2):
                blocks = [
                    scr_ref[
                        c,
                        pl.ds(pl.multiple_of(((bx + 1) * SIDE + part * 4 + p + 1) * 8, 8), 8),
                        :,
                    ]
                    for p in range(4)
                ]
                for q, rows in enumerate(swap_groups(blocks)):
                    out_ref[
                        c,
                        pl.ds(pl.multiple_of(bx * B + 8 * q, 8), 8),
                        pl.ds(part * LANES, LANES),
                    ] = rows
        return carry

    lax.fori_loop(0, BX_DEV, body, 0)


def tile_kernel(
    tile_ref,
    lat_ref,
    blocks_ref,
    cell_ref,
    north_ref,
    south_ref,
    east_ref,
    west_ref,
    scr_ref,
    vel_out_ref,
    send_out_ref,
    z_ref,
    m_ref,
    p_ref,
    q_ref,
    s_ref,
    a_ref,
    b_ref,
    fx_ref,
    fy_ref,
    w_ref,
    turn_ref,
    send_ref,
    sems,
):
    del blocks_ref
    lane = lane_ids((8, LANES))
    count = send_out_ref.shape[0] // 2
    tiles = GRID_LANES // LANES
    fields = FIELDS + 2
    spot = grid_rows
    in_group = lane % 32

    def lat_rim(bx, north, south):
        for field in range(fields):
            v, k = divmod(field, 5)
            got = pltpu.roll(north(v), (-HALO * k) % LANES, 1)
            scr_ref[field, spot(bx, BY_DEV), :] = jnp.where(in_group < HALO, got, 0.0)
            got = pltpu.roll(south(v), (B - HALO - HALO * k) % LANES, 1)
            scr_ref[field, spot(bx, -1), :] = jnp.where(in_group >= B - HALO, got, 0.0)

    def lat_rims(bx, carry):
        lat_rim(bx, lambda v: north_ref[bx, v], lambda v: south_ref[bx, v])
        return carry

    lax.fori_loop(0, BX_DEV, lat_rims, 0)
    for ref, bx, group in ((west_ref, -1, 3), (east_ref, BX_DEV, 0)):
        for field in range(fields):
            for part in range(4):
                for p in range(4):
                    got = ref[field * 4 + part]
                    got = pltpu.roll(got, ((group - p) * 32) % LANES, 1)
                    scr_ref[field, spot(bx, part * 4 + p), :] = jnp.where(
                        lane // 32 == group, got, 0.0
                    )
        lat_rim(bx, lambda v: ref[RIM + v], lambda v: ref[RIM + 2 + v])

    def prepare(t, carry):
        cols = pl.ds(pl.multiple_of(t * LANES, LANES), LANES)
        for s in range(8):
            start = pl.multiple_of(t * 8 * LANES, 8 * LANES) + s
            turned = [
                scr_ref[field, pl.ds(start, LANES, stride=8), :].T for field in range(fields)
            ]
            for q in range(4):
                plane = 8 * q + s
                zonal, merid, total, diff, shear, mass, strength, fzonal, fmerid = [
                    x[q * B : (q + 1) * B] for x in turned
                ]
                drag = jnp.where(mass > 0.0, 0.5 / (mass + 0.5), 0.0)
                z_ref[plane + 1, :, cols] = zonal
                m_ref[plane + 1, :, cols] = merid
                p_ref[plane + 1, :, cols] = 0.5 * (total + diff)
                q_ref[plane + 1, :, cols] = 0.5 * (total - diff)
                s_ref[plane + 1, :, cols] = shear
                a_ref[plane, :, cols] = 2.0 * mass * drag
                b_ref[plane, :, cols] = drag
                fx_ref[plane, :, cols] = drag * fzonal
                fy_ref[plane, :, cols] = drag * fmerid
                w_ref[plane, :, cols] = 0.25 * strength
        return carry

    lax.fori_loop(0, tiles, prepare, 0)

    cell = cell_ref[...] + lat_ref[0] * COLS
    turn_ref[...] = (0.5 * CORIOLIS) * (
        2.0 * (cell.astype(jnp.float32) + 0.5) / (lat_ref[1] * COLS).astype(jnp.float32) - 1.0
    )

    sub = row_ids((8, LANES))
    first_row = sub == 0
    last_row = sub == 7

    def north_of(x, edge):
        top = jnp.where(first_row, edge, x[:8])
        return pltpu.roll(jnp.concatenate((top, x[8:]), axis=0), B - 1, 0)

    def south_of(x, edge):
        bottom = jnp.where(last_row, edge, x[B - 8 :])
        return pltpu.roll(jnp.concatenate((x[: B - 8], bottom), axis=0), 1, 0)

    def stress_plane(k):
        z_edge = pltpu.roll(z_ref[k, pl.ds(0, 8), :], GRID_LANES - 1, 1)
        m_edge = pltpu.roll(m_ref[k, pl.ds(0, 8), :], GRID_LANES - 1, 1)
        for t in range(tiles):
            cols = slice(t * LANES, (t + 1) * LANES)
            z, m, w = z_ref[k, :, cols], m_ref[k, :, cols], w_ref[k - 1, :, cols]
            gx = z_ref[k + 1, :, cols] - z
            hx = m_ref[k + 1, :, cols] - m
            gy = north_of(m, m_edge[:, cols]) - m
            hy = north_of(z, z_edge[:, cols]) - z
            div = gx + gy
            ten = gx - gy
            she = hy + hx
            weight = w * lax.rsqrt(div * div + 0.25 * (ten * ten + she * she) + 0.25)
            quarter = 0.25 * weight
            mean = weight * div - w
            dev = quarter * ten
            p_ref[k, :, cols] = 0.5 * p_ref[k, :, cols] + (mean + dev)
            q_ref[k, :, cols] = 0.5 * q_ref[k, :, cols] + (mean - dev)
            s_ref[k, :, cols] = 0.5 * s_ref[k, :, cols] + quarter * she

    def momentum_plane(k):
        s_edge = pltpu.roll(s_ref[k, pl.ds(B - 8, 8), :], 1, 1)
        q_edge = pltpu.roll(q_ref[k, pl.ds(B - 8, 8), :], 1, 1)
        for t in range(tiles):
            cols = slice(t * LANES, (t + 1) * LANES)
            z, m = z_ref[k, :, cols], m_ref[k, :, cols]
            a, b = a_ref[k - 1, :, cols], b_ref[k - 1, :, cols]
            s, q = s_ref[k, :, cols], q_ref[k, :, cols]
            push_x = (p_ref[k, :, cols] - p_ref[k - 1, :, cols]) + (
                s - south_of(s, s_edge[:, cols])
            )
            push_y = (s - s_ref[k - 1, :, cols]) + (q - south_of(q, q_edge[:, cols]))
            turn = a * turn_ref[:, cols]
            z_ref[k, :, cols] = a * z + b * push_x + fx_ref[k - 1, :, cols] + turn * m
            m_ref[k, :, cols] = a * m + b * push_y + fy_ref[k - 1, :, cols] - turn * z

    def sweep(step, carry):
        for ref in (z_ref, m_ref):
            ref[B + 1] = pltpu.roll(ref[1], GRID_LANES - SIDE, 1)
        stress_plane(B)
        for ref in (p_ref, s_ref):
            ref[0] = pltpu.roll(ref[B], SIDE, 1)
        stress_plane(1)

        def body(k, carry):
            stress_plane(k + 1)
            momentum_plane(k)
            return carry

        lax.fori_loop(1, B - 1, body, 0, unroll=True)
        for k in (B - 1, B):
            momentum_plane(k)
        return carry

    lax.fori_loop(0, ITERS, sweep, 0)
    copies = [
        pltpu.make_async_copy(ref.at[pl.ds(1, B)], vel_out_ref.at[c], sems.at[c])
        for c, ref in enumerate((z_ref, m_ref))
    ]
    for copy in copies:
        copy.start()

    def turn_back(t, carry):
        cols = pl.ds(pl.multiple_of(t * LANES, LANES), LANES)
        for s in range(8):
            rows = pl.ds(pl.multiple_of(t * 8 * LANES, 8 * LANES) + s, LANES, stride=8)
            planes = [8 * q + s + 1 for q in range(4)]
            p_all = jnp.concatenate([p_ref[k, :, cols] for k in planes], axis=0)
            q_all = jnp.concatenate([q_ref[k, :, cols] for k in planes], axis=0)
            s_all = jnp.concatenate([s_ref[k, :, cols] for k in planes], axis=0)
            scr_ref[0, rows, :] = (p_all + q_all).T
            scr_ref[1, rows, :] = (p_all - q_all).T
            scr_ref[2, rows, :] = s_all.T
        return carry

    lax.fori_loop(0, tiles, turn_back, 0)

    def deal(half):
        def body(bx, carry):
            for by in range(BY_DEV):
                number = tile_ref[bx, by]
                place = jnp.where(number >= 0, (number & (count - 1)) * 2 + half, 2 * count)
                for c in range(3):
                    send_ref[place, c] = scr_ref[c, spot(bx, by), :]
            return carry

        return body

    lax.fori_loop(0, BX_DEV // 2, deal(0), 0)
    lax.fori_loop(BX_DEV // 2, BX_DEV, deal(1), 0)
    copies.append(
        pltpu.make_async_copy(send_ref.at[pl.ds(0, 2 * count)], send_out_ref, sems.at[2])
    )
    copies[2].start()
    for copy in copies:
        copy.wait()


def unpack_kernel(pos_ref, recv_ref, out_ref, scr_ref):
    slots = out_ref.shape[-1]

    def gather(slot, carry):
        place = pos_ref[0, slot]
        for c in range(3):
            scr_ref[c, pl.ds(pl.multiple_of(slot * 8, 8), 8), :] = recv_ref[place, c]
        return carry

    lax.fori_loop(0, slots, gather, 0, unroll=4)
    for c in range(3):
        for s in range(8):
            turned = scr_ref[c, pl.ds(s, slots, stride=8), :].T
            for q in range(4):
                out_ref[c, 8 * q + s] = turned[q * B : (q + 1) * B]


VMEM = pl.BlockSpec(memory_space=pltpu.VMEM)
SMEM = pl.BlockSpec(memory_space=pltpu.SMEM)
ANY = pl.BlockSpec(memory_space=pl.ANY)
HBM = pl.BlockSpec(memory_space=pltpu.HBM)


def params(mebibytes):
    return pltpu.CompilerParams(vmem_limit_bytes=mebibytes * 1024 * 1024)


def cost(mebibytes):
    return pl.CostEstimate(flops=10**7, bytes_accessed=mebibytes * 2**20, transcendentals=0)


def f32(*shape):
    return jax.ShapeDtypeStruct(shape, jnp.float32)


def on_device(forcing, velocity, stress, mass, strength, owner):
    lon_count = lax.axis_size("lon")
    lat_count = lax.axis_size("lat")
    devices = lon_count * lat_count
    lat_index = lax.axis_index("lat")
    lon_index = lax.axis_index("lon")
    own_index = lon_index * lat_count + lat_index
    slots = velocity.shape[-1]

    my_tile = lax.dynamic_slice(owner, (lon_index * BX_DEV, lat_index * BY_DEV), (BX_DEV, BY_DEV))

    block = (B, B, slots)
    send, pos = pl.pallas_call(
        pack_kernel,
        out_shape=(
            f32(devices * 2, FIELDS, 8, LANES),
            jax.ShapeDtypeStruct((1, slots), jnp.int32),
        ),
        in_specs=[SMEM, VMEM] + [HBM] * 4,
        out_specs=(HBM, VMEM),
        scratch_shapes=[
            pltpu.VMEM((2,) + block, jnp.float32),
            pltpu.VMEM((3,) + block, jnp.float32),
            pltpu.VMEM(block, jnp.float32),
            pltpu.VMEM(block, jnp.float32),
            pltpu.VMEM((FIELDS, slots * 8, LANES), jnp.float32),
            pltpu.SMEM((1, slots), jnp.int32),
            pltpu.SemaphoreType.DMA((6,)),
        ],
        compiler_params=params(61),
    )(own_index.reshape(1).astype(jnp.int32), owner, velocity, stress, mass, strength)
    recv = lax.all_to_all(
        send.reshape(devices, 2 * FIELDS, 8, LANES), ("lon", "lat"), 0, 0, tiled=True
    ).reshape(devices * 2, FIELDS, 8, LANES)

    force_blocks = pl.pallas_call(
        force_kernel,
        out_shape=f32(BX_DEV * BY_DEV, 2, 8, LANES),
        in_specs=[VMEM],
        out_specs=VMEM,
        cost_estimate=cost(4),
        compiler_params=params(12),
    )(forcing)
    north, south, east, west = pl.pallas_call(
        strips_kernel,
        out_shape=(f32(BX_DEV, 2, 8, LANES),) * 2 + (f32(RIM, 8, LANES),) * 2,
        in_specs=[SMEM, HBM, VMEM],
        out_specs=(VMEM,) * 4,
        scratch_shapes=[
            pltpu.VMEM((4 * BX_DEV, FIELDS, 8, LANES), jnp.float32),
            pltpu.SemaphoreType.DMA(()),
        ],
        cost_estimate=cost(4),
        compiler_params=params(10),
    )(my_tile, recv, force_blocks)
    blocks = pl.pallas_call(
        collect_kernel,
        out_shape=f32(FIELDS + 2, GRID_LANES * 8, LANES),
        in_specs=[SMEM, VMEM, VMEM],
        out_specs=VMEM,
        cost_estimate=cost(24),
        compiler_params=params(12),
    )(my_tile, recv, force_blocks)

    ahead = [(j, j + 1) for j in range(lat_count - 1)]
    got_north = lax.ppermute(north, "lat", [(k, j) for j, k in ahead])
    got_south = lax.ppermute(south, "lat", ahead)
    ring = [(i, (i + 1) % lon_count) for i in range(lon_count)]
    east = jnp.concatenate((east, got_north[0], got_south[0]), axis=0)
    west = jnp.concatenate((west, got_north[-1], got_south[-1]), axis=0)
    got_east = lax.ppermute(east, "lon", [(k, i) for i, k in ring])
    got_west = lax.ppermute(west, "lon", ring)
    grid = np.arange(GRID_LANES) % SIDE - 1
    cells = jnp.asarray(grid[None, :] * B + np.arange(B)[:, None], jnp.int32)
    state = (B + 2, B, GRID_LANES)
    constant = (B, B, GRID_LANES)
    _, cell_velocity, back = pl.pallas_call(
        tile_kernel,
        out_shape=(
            f32(FIELDS + 2, GRID_LANES * 8, LANES),
            f32(2, B, B, GRID_LANES),
            f32(devices * 2, 3, 8, LANES),
        ),
        in_specs=[SMEM, SMEM] + [VMEM] * 6,
        out_specs=(VMEM, HBM, ANY),
        input_output_aliases={2: 0},
        scratch_shapes=[pltpu.VMEM(state, jnp.float32)] * 5
        + [pltpu.VMEM(constant, jnp.float32)] * 5
        + [
            pltpu.VMEM((B, GRID_LANES), jnp.float32),
            pltpu.VMEM((devices * 2 + 1, 3, 8, LANES), jnp.float32),
            pltpu.SemaphoreType.DMA((3,)),
        ],
        compiler_params=params(26),
    )(
        my_tile,
        jnp.stack((lat_index, lat_count)).astype(jnp.int32),
        blocks,
        cells,
        got_north,
        got_south,
        got_east,
        got_west,
    )
    returned = lax.all_to_all(
        back.reshape(devices, 6, 8, LANES), ("lon", "lat"), 0, 0, tiled=True
    ).reshape(devices * 2, 3, 8, LANES)
    new_velocity = pl.pallas_call(
        velocity_kernel,
        out_shape=f32(2, ROWS, COLS),
        in_specs=[VMEM],
        out_specs=VMEM,
        scratch_shapes=[pltpu.VMEM((2, GRID_LANES * 8, LANES), jnp.float32)],
        cost_estimate=cost(6),
        compiler_params=params(16),
    )(cell_velocity)
    new_stress = pl.pallas_call(
        unpack_kernel,
        out_shape=f32(3, B, B, slots),
        in_specs=[SMEM, VMEM],
        out_specs=VMEM,
        scratch_shapes=[pltpu.VMEM((3, slots * 8, LANES), jnp.float32)],
        compiler_params=params(16),
    )(pos, returned)
    return (new_velocity, new_stress)


def solution(mesh):
    in_specs = (
        P(None, "lon", "lat"),
        P(None, None, None, ("lon", "lat")),
        P(None, None, None, ("lon", "lat")),
        P(None, None, ("lon", "lat")),
        P(None, None, ("lon", "lat")),
        P(),
    )
    out_specs = (P(None, "lon", "lat"), P(None, None, None, ("lon", "lat")))
    return jax.shard_map(
        on_device, mesh=mesh, in_specs=in_specs, out_specs=out_specs, check_vma=False
    )
```

```python
import jax
import jax.numpy as jnp
import numpy as np
from jax import lax
from jax.experimental import pallas as pl
from jax.experimental.pallas import tpu as pltpu
from jax.sharding import PartitionSpec as P

B = 32
BX_DEV = 16
BY_DEV = 16
ITERS = 6
LANES = 128
CORIOLIS = 0.5
HALO = 6
FIELDS = 7
ROWS = BX_DEV * B
COLS = BY_DEV * B
RIM = 4 * (FIELDS + 2)
SIDE = BX_DEV + 2
GRID_LANES = -(-SIDE * SIDE // LANES) * LANES


def lane_ids(shape):
    return lax.broadcasted_iota(jnp.int32, shape, len(shape) - 1)


def row_ids(shape):
    return lax.broadcasted_iota(jnp.int32, shape, len(shape) - 2)


def swap_groups(parts):
    lane = lane_ids((8, LANES))
    low = lane < 64
    even = (lane // 32) % 2 == 0
    lo, hi = [], []
    for p in range(2):
        lo.append(jnp.where(low, parts[p], pltpu.roll(parts[p + 2], 64, 1)))
        hi.append(jnp.where(low, pltpu.roll(parts[p], 64, 1), parts[p + 2]))
    out = []
    for pair in (lo, hi):
        out.append(jnp.where(even, pair[0], pltpu.roll(pair[1], 32, 1)))
        out.append(jnp.where(even, pltpu.roll(pair[0], 96, 1), pair[1]))
    return out


def grid_rows(bx, by):
    return pl.ds(pl.multiple_of(((bx + 1) * SIDE + by + 1) * 8, 8), 8)


def pack_kernel(
    own_ref,
    owner_ref,
    vel_hbm,
    str_hbm,
    mass_hbm,
    strength_hbm,
    send_ref,
    pos_ref,
    vel_ref,
    str_ref,
    mass_ref,
    strength_ref,
    scr_ref,
    place_ref,
    sems,
):
    slots = vel_ref.shape[-1]
    lon_count = owner_ref.shape[0] // BX_DEV
    lat_count = owner_ref.shape[1] // BY_DEV
    devices = lon_count * lat_count
    fetches = [
        pltpu.make_async_copy(src, dst, sems.at[i])
        for i, (src, dst) in enumerate(
            (
                (vel_hbm, vel_ref),
                (str_hbm, str_ref),
                (mass_hbm, mass_ref),
                (strength_hbm, strength_ref),
            )
        )
    ]
    for fetch in fetches:
        fetch.start()

    half_rows = BX_DEV // 2
    columns = owner_ref.shape[1]

    def dot(x, y):
        return jnp.dot(
            x.astype(jnp.bfloat16), y.astype(jnp.bfloat16), preferred_element_type=jnp.float32
        )

    def square(rows, cols):
        return (
            lax.broadcasted_iota(jnp.int32, (rows, cols), 0),
            lax.broadcasted_iota(jnp.int32, (rows, cols), 1),
        )

    row, col = square(columns, devices)
    of_lat = jnp.where(row // BY_DEV == col % lat_count, 1.0, 0.0)
    iced = jnp.where(owner_ref[...] >= 0, 1.0, 0.0)
    row, col = square(2 * lon_count, owner_ref.shape[0])
    of_half = jnp.where(col // half_rows == row, 1.0, 0.0)
    per_tile = dot(dot(of_half, iced), of_lat)
    row, col = square(2 * lon_count, devices)
    mine = row // 2 == col // lat_count
    counts = [
        jnp.sum(jnp.where(mine & (row % 2 == h), per_tile, 0.0), axis=0, keepdims=True)
        for h in range(2)
    ]
    row, col = square(devices, devices)
    upto = jnp.where(row <= col, 1.0, 0.0)
    both = jnp.broadcast_to(counts[0] + counts[1], (8, devices))
    end_second = dot(both, upto)[:1]
    end_first = end_second - counts[1]
    number = (lax.broadcasted_iota(jnp.int32, (devices, slots), 1) * devices + own_ref[0]).astype(
        jnp.float32
    )
    place = jnp.zeros((1, slots), jnp.float32)
    for end in (end_first, end_second):
        column = jnp.broadcast_to(end, (devices, devices)).T[:, :1]
        place = place + jnp.sum(jnp.where(column <= number, 1.0, 0.0), axis=0, keepdims=True)
    pos_ref[...] = place.astype(jnp.int32)
    to_scalar = pltpu.make_async_copy(pos_ref, place_ref, sems.at[4])
    to_scalar.start()

    def turn(field, load):
        for s in range(8):
            rows = jnp.concatenate([load(8 * q + s) for q in range(4)], axis=0)
            scr_ref[field, pl.ds(s, slots, stride=8), :] = rows.T

    def scatter(first, fields, sem):
        def body(slot, carry):
            rows = pl.ds(pl.multiple_of(slot * 8, 8), 8)
            pltpu.make_async_copy(
                scr_ref.at[pl.ds(first, fields), rows, :],
                send_ref.at[place_ref[0, slot], pl.ds(first, fields)],
                sem,
            ).start()
            return carry

        lax.fori_loop(0, slots, body, 0, unroll=8)
        everything = send_ref.at[pl.ds(0, slots), pl.ds(first, fields)]
        return pltpu.make_async_copy(everything, everything, sem)

    fetches[0].wait()
    for c in range(2):
        turn(c, lambda ci, c=c: vel_ref[c, ci])
    fetches[1].wait()
    for c in range(3):
        turn(2 + c, lambda ci, c=c: str_ref[c, ci])
    to_scalar.wait()
    early = scatter(0, 5, sems.at[5])
    fetches[2].wait()
    turn(5, lambda ci: mass_ref[ci])
    fetches[3].wait()
    turn(6, lambda ci: strength_ref[ci])
    late = scatter(5, 2, sems.at[6])
    early.wait()
    late.wait()


def fetch_edges(tile_ref, recv_hbm, edge_ref, sem, places):
    count = recv_hbm.shape[0] // 2

    def fetch(i, carry):
        for side, (bx, by) in enumerate(places(i)):
            source = (tile_ref[bx, by] & (count - 1)) * 2 + jnp.int32(bx >= BX_DEV // 2)
            pltpu.make_async_copy(recv_hbm.at[source], edge_ref.at[side * BX_DEV + i], sem).start()
        return carry

    lax.fori_loop(0, BX_DEV, fetch, 0, unroll=4)
    pltpu.make_async_copy(recv_hbm.at[pl.ds(0, 2 * BX_DEV)], edge_ref, sem).wait()


def lat_kernel(tile_ref, recv_hbm, force_ref, north_ref, south_ref, edge_ref, sem):
    in_group = lane_ids((8, LANES)) % 32
    edges = (0, BY_DEV - 1)
    fetch_edges(tile_ref, recv_hbm, edge_ref, sem, lambda i: [(i, by) for by in edges])

    def lat_rims(bx, carry):
        for side, (by, ref, first) in enumerate(
            zip(edges, (north_ref, south_ref), (0, B - HALO))
        ):
            for v in range(2):
                total = jnp.zeros((8, LANES), jnp.float32)
                for k in range(min(5, FIELDS + 2 - v * 5)):
                    field = v * 5 + k
                    if field >= FIELDS:
                        got = force_ref[bx * BY_DEV + by, field - FIELDS]
                    else:
                        got = edge_ref[side * BX_DEV + bx, field]
                        got = jnp.where(tile_ref[bx, by] >= 0, got, 0.0)
                    mine = (in_group >= HALO * k) & (in_group < HALO * (k + 1))
                    got = pltpu.roll(got, (HALO * k - first) % LANES, 1)
                    total = jnp.where(mine, got, total)
                ref[bx, v] = total
        return carry

    lax.fori_loop(0, BX_DEV, lat_rims, 0, unroll=2)


def lon_kernel(tile_ref, recv_hbm, force_ref, east_ref, west_ref, edge_ref, sem):
    group_of = lane_ids((8, LANES)) // 32
    edges = (0, BX_DEV - 1)
    fetch_edges(tile_ref, recv_hbm, edge_ref, sem, lambda i: [(bx, i) for bx in edges])
    for side, (bx, ref, group) in enumerate(zip(edges, (east_ref, west_ref), (0, 3))):
        for part in range(4):
            for field in range(FIELDS + 2):
                total = jnp.zeros((8, LANES), jnp.float32)
                for p in range(4):
                    by = part * 4 + p
                    if field >= FIELDS:
                        got = force_ref[bx * BY_DEV + by, field - FIELDS]
                    else:
                        got = edge_ref[side * BX_DEV + by, field]
                        got = jnp.where(tile_ref[bx, by] >= 0, got, 0.0)
                    turned = pltpu.roll(got, ((p - group) * 32) % LANES, 1) if p != group else got
                    total = jnp.where(group_of == p, turned, total)
                ref[field * 4 + part] = total


def collect_kernel(tile_ref, recv_ref, force_ref, scr_ref):
    count = recv_ref.shape[0] // 2
    rest = SIDE * SIDE * 8
    for field in range(FIELDS + 2):
        scr_ref[field, pl.ds(rest, GRID_LANES * 8 - rest), :] = jnp.zeros(
            (GRID_LANES * 8 - rest, LANES), jnp.float32
        )

    def collect(bx, carry):
        half = jnp.int32(bx >= BX_DEV // 2)
        for by in range(BY_DEV):
            number = tile_ref[bx, by]
            source = (number & (count - 1)) * 2 + half
            iced = number >= 0
            for field in range(FIELDS):
                scr_ref[field, grid_rows(bx, by), :] = jnp.where(
                    iced, recv_ref[source, field], 0.0
                )
            for c in range(2):
                scr_ref[FIELDS + c, grid_rows(bx, by), :] = force_ref[bx * BY_DEV + by, c]
        return carry

    lax.fori_loop(0, BX_DEV, collect, 0)


def force_kernel(force_ref, out_ref):
    def body(bx, carry):
        for part in range(4):
            for c in range(2):
                rows = [
                    force_ref[
                        c,
                        pl.ds(pl.multiple_of(bx * B + 8 * q, 8), 8),
                        pl.ds(part * LANES, LANES),
                    ]
                    for q in range(4)
                ]
                for p, block in enumerate(swap_groups(rows)):
                    out_ref[bx * BY_DEV + part * 4 + p, c] = block
        return carry

    lax.fori_loop(0, BX_DEV, body, 0)


def velocity_kernel(vel_ref, out_ref, scr_ref):
    for c in range(2):
        for t in range(GRID_LANES // LANES):
            for s in range(8):
                cells = [vel_ref[c, 8 * q + s, :, pl.ds(t * LANES, LANES)] for q in range(4)]
                scr_ref[c, pl.ds(t * 8 * LANES + s, LANES, stride=8), :] = jnp.concatenate(
                    cells, axis=0
                ).T

    def body(bx, carry):
        for part in range(4):
            for c in range(2):
                blocks = [
                    scr_ref[
                        c,
                        pl.ds(pl.multiple_of(((bx + 1) * SIDE + part * 4 + p + 1) * 8, 8), 8),
                        :,
                    ]
                    for p in range(4)
                ]
                for q, rows in enumerate(swap_groups(blocks)):
                    out_ref[
                        c,
                        pl.ds(pl.multiple_of(bx * B + 8 * q, 8), 8),
                        pl.ds(part * LANES, LANES),
                    ] = rows
        return carry

    lax.fori_loop(0, BX_DEV, body, 0)


def tile_kernel(
    tile_ref,
    lat_ref,
    blocks_ref,
    cell_ref,
    north_ref,
    south_ref,
    east_ref,
    west_ref,
    scr_ref,
    vel_out_ref,
    send_out_ref,
    z_ref,
    m_ref,
    p_ref,
    q_ref,
    s_ref,
    a_ref,
    b_ref,
    fx_ref,
    fy_ref,
    w_ref,
    turn_ref,
    send_ref,
    sems,
):
    del blocks_ref
    lane = lane_ids((8, LANES))
    count = send_out_ref.shape[0] // 2
    tiles = GRID_LANES // LANES
    fields = FIELDS + 2
    spot = grid_rows
    in_group = lane % 32

    def lat_rim(bx, north, south):
        for field in range(fields):
            v, k = divmod(field, 5)
            got = pltpu.roll(north(v), (-HALO * k) % LANES, 1)
            scr_ref[field, spot(bx, BY_DEV), :] = jnp.where(in_group < HALO, got, 0.0)
            got = pltpu.roll(south(v), (B - HALO - HALO * k) % LANES, 1)
            scr_ref[field, spot(bx, -1), :] = jnp.where(in_group >= B - HALO, got, 0.0)

    def lat_rims(bx, carry):
        lat_rim(bx, lambda v: north_ref[bx, v], lambda v: south_ref[bx, v])
        return carry

    lax.fori_loop(0, BX_DEV, lat_rims, 0)
    for ref, bx, group in ((west_ref, -1, 3), (east_ref, BX_DEV, 0)):
        for field in range(fields):
            for part in range(4):
                for p in range(4):
                    got = ref[field * 4 + part]
                    got = pltpu.roll(got, ((group - p) * 32) % LANES, 1)
                    scr_ref[field, spot(bx, part * 4 + p), :] = jnp.where(
                        lane // 32 == group, got, 0.0
                    )
        lat_rim(bx, lambda v: ref[RIM + v], lambda v: ref[RIM + 2 + v])

    def prepare(t, carry):
        cols = pl.ds(pl.multiple_of(t * LANES, LANES), LANES)
        for s in range(8):
            start = pl.multiple_of(t * 8 * LANES, 8 * LANES) + s
            turned = [
                scr_ref[field, pl.ds(start, LANES, stride=8), :].T for field in range(fields)
            ]
            for q in range(4):
                plane = 8 * q + s
                zonal, merid, total, diff, shear, mass, strength, fzonal, fmerid = [
                    x[q * B : (q + 1) * B] for x in turned
                ]
                drag = jnp.where(mass > 0.0, 0.5 / (mass + 0.5), 0.0)
                z_ref[plane + 1, :, cols] = zonal
                m_ref[plane + 1, :, cols] = merid
                p_ref[plane + 1, :, cols] = 0.5 * (total + diff)
                q_ref[plane + 1, :, cols] = 0.5 * (total - diff)
                s_ref[plane + 1, :, cols] = shear
                a_ref[plane, :, cols] = 2.0 * mass * drag
                b_ref[plane, :, cols] = drag
                fx_ref[plane, :, cols] = drag * fzonal
                fy_ref[plane, :, cols] = drag * fmerid
                w_ref[plane, :, cols] = 0.25 * strength
        return carry

    lax.fori_loop(0, tiles, prepare, 0)

    cell = cell_ref[...] + lat_ref[0] * COLS
    turn_ref[...] = (0.5 * CORIOLIS) * (
        2.0 * (cell.astype(jnp.float32) + 0.5) / (lat_ref[1] * COLS).astype(jnp.float32) - 1.0
    )

    sub = row_ids((8, LANES))
    first_row = sub == 0
    last_row = sub == 7

    def north_of(x, edge):
        top = jnp.where(first_row, edge, x[:8])
        return pltpu.roll(jnp.concatenate((top, x[8:]), axis=0), B - 1, 0)

    def south_of(x, edge):
        bottom = jnp.where(last_row, edge, x[B - 8 :])
        return pltpu.roll(jnp.concatenate((x[: B - 8], bottom), axis=0), 1, 0)

    def stress_plane(k):
        z_edge = pltpu.roll(z_ref[k, pl.ds(0, 8), :], GRID_LANES - 1, 1)
        m_edge = pltpu.roll(m_ref[k, pl.ds(0, 8), :], GRID_LANES - 1, 1)
        for t in range(tiles):
            cols = slice(t * LANES, (t + 1) * LANES)
            z, m, w = z_ref[k, :, cols], m_ref[k, :, cols], w_ref[k - 1, :, cols]
            gx = z_ref[k + 1, :, cols] - z
            hx = m_ref[k + 1, :, cols] - m
            gy = north_of(m, m_edge[:, cols]) - m
            hy = north_of(z, z_edge[:, cols]) - z
            div = gx + gy
            ten = gx - gy
            she = hy + hx
            weight = w * lax.rsqrt(div * div + 0.25 * (ten * ten + she * she) + 0.25)
            quarter = 0.25 * weight
            mean = weight * div - w
            dev = quarter * ten
            p_ref[k, :, cols] = 0.5 * p_ref[k, :, cols] + (mean + dev)
            q_ref[k, :, cols] = 0.5 * q_ref[k, :, cols] + (mean - dev)
            s_ref[k, :, cols] = 0.5 * s_ref[k, :, cols] + quarter * she

    def momentum_plane(k):
        s_edge = pltpu.roll(s_ref[k, pl.ds(B - 8, 8), :], 1, 1)
        q_edge = pltpu.roll(q_ref[k, pl.ds(B - 8, 8), :], 1, 1)
        for t in range(tiles):
            cols = slice(t * LANES, (t + 1) * LANES)
            z, m = z_ref[k, :, cols], m_ref[k, :, cols]
            a, b = a_ref[k - 1, :, cols], b_ref[k - 1, :, cols]
            s, q = s_ref[k, :, cols], q_ref[k, :, cols]
            push_x = (p_ref[k, :, cols] - p_ref[k - 1, :, cols]) + (
                s - south_of(s, s_edge[:, cols])
            )
            push_y = (s - s_ref[k - 1, :, cols]) + (q - south_of(q, q_edge[:, cols]))
            turn = a * turn_ref[:, cols]
            z_ref[k, :, cols] = a * z + b * push_x + fx_ref[k - 1, :, cols] + turn * m
            m_ref[k, :, cols] = a * m + b * push_y + fy_ref[k - 1, :, cols] - turn * z

    def sweep(step, carry):
        for ref in (z_ref, m_ref):
            ref[B + 1] = pltpu.roll(ref[1], GRID_LANES - SIDE, 1)
        stress_plane(B)
        for ref in (p_ref, s_ref):
            ref[0] = pltpu.roll(ref[B], SIDE, 1)
        stress_plane(1)

        def body(k, carry):
            stress_plane(k + 1)
            momentum_plane(k)
            return carry

        lax.fori_loop(1, B - 1, body, 0, unroll=True)
        for k in (B - 1, B):
            momentum_plane(k)
        return carry

    lax.fori_loop(0, ITERS, sweep, 0)
    copies = [
        pltpu.make_async_copy(ref.at[pl.ds(1, B)], vel_out_ref.at[c], sems.at[c])
        for c, ref in enumerate((z_ref, m_ref))
    ]
    for copy in copies:
        copy.start()

    def turn_back(t, carry):
        cols = pl.ds(pl.multiple_of(t * LANES, LANES), LANES)
        for s in range(8):
            rows = pl.ds(pl.multiple_of(t * 8 * LANES, 8 * LANES) + s, LANES, stride=8)
            planes = [8 * q + s + 1 for q in range(4)]
            p_all = jnp.concatenate([p_ref[k, :, cols] for k in planes], axis=0)
            q_all = jnp.concatenate([q_ref[k, :, cols] for k in planes], axis=0)
            s_all = jnp.concatenate([s_ref[k, :, cols] for k in planes], axis=0)
            scr_ref[0, rows, :] = (p_all + q_all).T
            scr_ref[1, rows, :] = (p_all - q_all).T
            scr_ref[2, rows, :] = s_all.T
        return carry

    lax.fori_loop(0, tiles, turn_back, 0)

    def deal(half):
        def body(bx, carry):
            for by in range(BY_DEV):
                number = tile_ref[bx, by]
                place = jnp.where(number >= 0, (number & (count - 1)) * 2 + half, 2 * count)
                for c in range(3):
                    send_ref[place, c] = scr_ref[c, spot(bx, by), :]
            return carry

        return body

    lax.fori_loop(0, BX_DEV // 2, deal(0), 0)
    lax.fori_loop(BX_DEV // 2, BX_DEV, deal(1), 0)
    copies.append(
        pltpu.make_async_copy(send_ref.at[pl.ds(0, 2 * count)], send_out_ref, sems.at[2])
    )
    copies[2].start()
    for copy in copies:
        copy.wait()


def unpack_kernel(pos_ref, recv_ref, out_ref, scr_ref):
    slots = out_ref.shape[-1]

    def gather(slot, carry):
        place = pos_ref[0, slot]
        for c in range(3):
            scr_ref[c, pl.ds(pl.multiple_of(slot * 8, 8), 8), :] = recv_ref[place, c]
        return carry

    lax.fori_loop(0, slots, gather, 0, unroll=4)
    for c in range(3):
        for s in range(8):
            turned = scr_ref[c, pl.ds(s, slots, stride=8), :].T
            for q in range(4):
                out_ref[c, 8 * q + s] = turned[q * B : (q + 1) * B]


VMEM = pl.BlockSpec(memory_space=pltpu.VMEM)
SMEM = pl.BlockSpec(memory_space=pltpu.SMEM)
HBM = pl.BlockSpec(memory_space=pltpu.HBM)


def params(mebibytes):
    return pltpu.CompilerParams(vmem_limit_bytes=mebibytes * 1024 * 1024)


def cost(mebibytes):
    return pl.CostEstimate(flops=10**7, bytes_accessed=mebibytes * 2**20, transcendentals=0)


def f32(*shape):
    return jax.ShapeDtypeStruct(shape, jnp.float32)


def on_device(forcing, velocity, stress, mass, strength, owner):
    lon_count = lax.axis_size("lon")
    lat_count = lax.axis_size("lat")
    devices = lon_count * lat_count
    lat_index = lax.axis_index("lat")
    lon_index = lax.axis_index("lon")
    own_index = lon_index * lat_count + lat_index
    slots = velocity.shape[-1]

    my_tile = lax.dynamic_slice(owner, (lon_index * BX_DEV, lat_index * BY_DEV), (BX_DEV, BY_DEV))

    block = (B, B, slots)
    send, pos = pl.pallas_call(
        pack_kernel,
        out_shape=(
            pltpu.HBM((devices * 2, FIELDS, 8, LANES), jnp.float32),
            jax.ShapeDtypeStruct((1, slots), jnp.int32),
        ),
        in_specs=[SMEM, VMEM] + [HBM] * 4,
        out_specs=(HBM, VMEM),
        scratch_shapes=[
            pltpu.VMEM((2,) + block, jnp.float32),
            pltpu.VMEM((3,) + block, jnp.float32),
            pltpu.VMEM(block, jnp.float32),
            pltpu.VMEM(block, jnp.float32),
            pltpu.VMEM((FIELDS, slots * 8, LANES), jnp.float32),
            pltpu.SMEM((1, slots), jnp.int32),
            pltpu.SemaphoreType.DMA((7,)),
        ],
        compiler_params=params(61),
    )(own_index.reshape(1).astype(jnp.int32), owner, velocity, stress, mass, strength)
    recv = lax.all_to_all(
        send.reshape(devices, 2 * FIELDS, 8, LANES), ("lon", "lat"), 0, 0, tiled=True
    ).reshape(devices * 2, FIELDS, 8, LANES)

    force_blocks = pl.pallas_call(
        force_kernel,
        out_shape=f32(BX_DEV * BY_DEV, 2, 8, LANES),
        in_specs=[VMEM],
        out_specs=VMEM,
        cost_estimate=cost(4),
        compiler_params=params(12),
    )(forcing)
    edge_scratch = [
        pltpu.VMEM((2 * BX_DEV, FIELDS, 8, LANES), jnp.float32),
        pltpu.SemaphoreType.DMA(()),
    ]
    north, south = pl.pallas_call(
        lat_kernel,
        out_shape=(f32(BX_DEV, 2, 8, LANES),) * 2,
        in_specs=[SMEM, HBM, VMEM],
        out_specs=(VMEM,) * 2,
        scratch_shapes=edge_scratch,
        cost_estimate=cost(4),
        compiler_params=params(8),
    )(my_tile, recv, force_blocks)
    east, west = pl.pallas_call(
        lon_kernel,
        out_shape=(f32(RIM, 8, LANES),) * 2,
        in_specs=[SMEM, HBM, VMEM],
        out_specs=(VMEM,) * 2,
        scratch_shapes=edge_scratch,
        cost_estimate=cost(6),
        compiler_params=params(8),
    )(my_tile, recv, force_blocks)
    blocks = pl.pallas_call(
        collect_kernel,
        out_shape=pltpu.VMEM((FIELDS + 2, GRID_LANES * 8, LANES), jnp.float32),
        in_specs=[SMEM, VMEM, VMEM],
        out_specs=VMEM,
        cost_estimate=cost(24),
        compiler_params=params(12),
    )(my_tile, recv, force_blocks)

    ahead = [(j, j + 1) for j in range(lat_count - 1)]
    got_north = lax.ppermute(north, "lat", [(k, j) for j, k in ahead])
    got_south = lax.ppermute(south, "lat", ahead)
    ring = [(i, (i + 1) % lon_count) for i in range(lon_count)]
    east = jnp.concatenate((east, got_north[0], got_south[0]), axis=0)
    west = jnp.concatenate((west, got_north[-1], got_south[-1]), axis=0)
    got_east = lax.ppermute(east, "lon", [(k, i) for i, k in ring])
    got_west = lax.ppermute(west, "lon", ring)
    grid = np.arange(GRID_LANES) % SIDE - 1
    cells = jnp.asarray(grid[None, :] * B + np.arange(B)[:, None], jnp.int32)
    state = (B + 2, B, GRID_LANES)
    constant = (B, B, GRID_LANES)
    _, cell_velocity, back = pl.pallas_call(
        tile_kernel,
        out_shape=(
            pltpu.VMEM((FIELDS + 2, GRID_LANES * 8, LANES), jnp.float32),
            pltpu.HBM((2, B, B, GRID_LANES), jnp.float32),
            pltpu.HBM((devices * 2, 3, 8, LANES), jnp.float32),
        ),
        in_specs=[SMEM, SMEM] + [VMEM] * 6,
        out_specs=(VMEM, HBM, HBM),
        input_output_aliases={2: 0},
        scratch_shapes=[pltpu.VMEM(state, jnp.float32)] * 5
        + [pltpu.VMEM(constant, jnp.float32)] * 5
        + [
            pltpu.VMEM((B, GRID_LANES), jnp.float32),
            pltpu.VMEM((devices * 2 + 1, 3, 8, LANES), jnp.float32),
            pltpu.SemaphoreType.DMA((3,)),
        ],
        compiler_params=params(26),
    )(
        my_tile,
        jnp.stack((lat_index, lat_count)).astype(jnp.int32),
        blocks,
        cells,
        got_north,
        got_south,
        got_east,
        got_west,
    )
    returned = lax.all_to_all(
        back.reshape(devices, 6, 8, LANES), ("lon", "lat"), 0, 0, tiled=True
    ).reshape(devices * 2, 3, 8, LANES)
    new_velocity = pl.pallas_call(
        velocity_kernel,
        out_shape=f32(2, ROWS, COLS),
        in_specs=[VMEM],
        out_specs=VMEM,
        scratch_shapes=[pltpu.VMEM((2, GRID_LANES * 8, LANES), jnp.float32)],
        cost_estimate=cost(6),
        compiler_params=params(16),
    )(cell_velocity)
    new_stress = pl.pallas_call(
        unpack_kernel,
        out_shape=f32(3, B, B, slots),
        in_specs=[SMEM, VMEM],
        out_specs=VMEM,
        scratch_shapes=[pltpu.VMEM((3, slots * 8, LANES), jnp.float32)],
        compiler_params=params(16),
    )(pos, returned)
    return (new_velocity, new_stress)


def solution(mesh):
    in_specs = (
        P(None, "lon", "lat"),
        P(None, None, None, ("lon", "lat")),
        P(None, None, None, ("lon", "lat")),
        P(None, None, ("lon", "lat")),
        P(None, None, ("lon", "lat")),
        P(),
    )
    out_specs = (P(None, "lon", "lat"), P(None, None, None, ("lon", "lat")))
    return jax.shard_map(
        on_device, mesh=mesh, in_specs=in_specs, out_specs=out_specs, check_vma=False
    )
```

```python
import jax
import jax.numpy as jnp
import numpy as np
from jax import lax
from jax.experimental import pallas as pl
from jax.experimental.pallas import tpu as pltpu
from jax.sharding import PartitionSpec as P

B = 32
BX_DEV = 16
BY_DEV = 16
ITERS = 6
LANES = 128
CORIOLIS = 0.5
HALO = 6
FIELDS = 6
MESSAGE = 2 * FIELDS + 1
EDGE = FIELDS + 2
PER_RIM = 4
ROWS = BX_DEV * B
COLS = BY_DEV * B
LAT_RIM = BX_DEV * 2 + BX_DEV // 8
LON_RIM = 4 * (FIELDS + 2) + BY_DEV // 8
SIDE = BX_DEV + 2
GRID_LANES = -(-SIDE * SIDE // LANES) * LANES


def lane_ids(shape):
    return lax.broadcasted_iota(jnp.int32, shape, len(shape) - 1)


def row_ids(shape):
    return lax.broadcasted_iota(jnp.int32, shape, len(shape) - 2)


def swap_groups(parts):
    lane = lane_ids((8, LANES))
    low = lane < 64
    even = (lane // 32) % 2 == 0
    lo, hi = [], []
    for p in range(2):
        lo.append(jnp.where(low, parts[p], pltpu.roll(parts[p + 2], 64, 1)))
        hi.append(jnp.where(low, pltpu.roll(parts[p], 64, 1), parts[p + 2]))
    out = []
    for pair in (lo, hi):
        out.append(jnp.where(even, pair[0], pltpu.roll(pair[1], 32, 1)))
        out.append(jnp.where(even, pltpu.roll(pair[0], 96, 1), pair[1]))
    return out


def grid_rows(bx, by):
    return pl.ds(pl.multiple_of(((bx + 1) * SIDE + by + 1) * 8, 8), 8)


def grid_row(bx, by):
    return pl.ds(pl.multiple_of(((bx + 1) * SIDE + by + 1) * 8, 8), 1)


def pack_kernel(
    own_ref,
    owner_ref,
    vel_hbm,
    str_hbm,
    mass_hbm,
    strength_hbm,
    send_ref,
    pos_ref,
    vel_ref,
    str_ref,
    mass_ref,
    strength_ref,
    scr_ref,
    edge_ref,
    stage_ref,
    place_ref,
    sems,
):
    slots = vel_ref.shape[-1]
    lon_count = owner_ref.shape[0] // BX_DEV
    lat_count = owner_ref.shape[1] // BY_DEV
    devices = lon_count * lat_count
    fetches = [
        pltpu.make_async_copy(src, dst, sems.at[i])
        for i, (src, dst) in enumerate(
            (
                (vel_hbm, vel_ref),
                (str_hbm, str_ref),
                (mass_hbm, mass_ref),
                (strength_hbm, strength_ref),
            )
        )
    ]
    for fetch in fetches:
        fetch.start()

    half_rows = BX_DEV // 2
    columns = owner_ref.shape[1]

    def dot(x, y):
        return jnp.dot(
            x.astype(jnp.bfloat16), y.astype(jnp.bfloat16), preferred_element_type=jnp.float32
        )

    def square(rows, cols):
        return (
            lax.broadcasted_iota(jnp.int32, (rows, cols), 0),
            lax.broadcasted_iota(jnp.int32, (rows, cols), 1),
        )

    row, col = square(columns, devices)
    of_lat = jnp.where(row // BY_DEV == col % lat_count, 1.0, 0.0)
    iced = jnp.where(owner_ref[...] >= 0, 1.0, 0.0)
    row, col = square(2 * lon_count, owner_ref.shape[0])
    of_half = jnp.where(col // half_rows == row, 1.0, 0.0)
    per_tile = dot(dot(of_half, iced), of_lat)
    row, col = square(2 * lon_count, devices)
    mine = row // 2 == col // lat_count
    counts = [
        jnp.sum(jnp.where(mine & (row % 2 == h), per_tile, 0.0), axis=0, keepdims=True)
        for h in range(2)
    ]
    row, col = square(devices, devices)
    upto = jnp.where(row <= col, 1.0, 0.0)
    both = jnp.broadcast_to(counts[0] + counts[1], (8, devices))
    end_second = dot(both, upto)[:1]
    end_first = end_second - counts[1]
    number = (lax.broadcasted_iota(jnp.int32, (devices, slots), 1) * devices + own_ref[0]).astype(
        jnp.float32
    )
    place = jnp.zeros((1, slots), jnp.float32)
    for end in (end_first, end_second):
        column = jnp.broadcast_to(end, (devices, devices)).T[:, :1]
        place = place + jnp.sum(jnp.where(column <= number, 1.0, 0.0), axis=0, keepdims=True)
    pos_ref[...] = place.astype(jnp.int32)
    to_scalar = pltpu.make_async_copy(pos_ref, place_ref, sems.at[4])
    to_scalar.start()

    def turn(field, planes):
        scr_ref[field, pl.ds(planes[0], slots, stride=8), :] = jnp.concatenate(planes[1], axis=0).T

    def scatter(first, fields, sem):
        def body(slot, carry):
            rows = pl.ds(pl.multiple_of(slot * 8, 8), 8)
            place = place_ref[0, slot]
            pltpu.make_async_copy(
                scr_ref.at[pl.ds(first, fields), rows, :],
                send_ref.at[place >> 1, pl.ds((place & 1) * (FIELDS + 1) + first, fields)],
                sem,
            ).start()
            return carry

        lax.fori_loop(0, slots, body, 0, unroll=8)
        everything = send_ref.at[pl.ds(0, slots), pl.ds(0, fields)]
        return pltpu.make_async_copy(everything, everything, sem)

    first_row = row_ids((B, slots)) == 0

    def south(x):
        return jnp.where(first_row, 0.0, pltpu.roll(x, 1, 0))

    def stresses(ci):
        total, diff = str_ref[0, ci], str_ref[1, ci]
        return 0.5 * (total + diff), 0.5 * (total - diff), str_ref[2, ci]

    fetches[0].wait()
    for c in range(2):
        for s in range(8):
            turn(c, (s, [vel_ref[c, 8 * q + s] for q in range(4)]))
    fetches[1].wait()
    for s in range(8):
        push_x, push_y = [], []
        for q in range(4):
            p, n, shear = stresses(8 * q + s)
            gx = p + (shear - south(shear))
            gy = shear + (n - south(n))
            if q or s:
                p_west, _, shear_west = stresses(8 * q + s - 1)
                gx, gy = gx - p_west, gy - shear_west
            push_x.append(gx)
            push_y.append(gy)
        turn(2, (s, push_x))
        turn(3, (s, push_y))
    p, _, shear = stresses(B - 1)
    shear_top = str_ref[2, :, B - 1, :]
    n_top = 0.5 * (str_ref[0, :, B - 1, :] - str_ref[1, :, B - 1, :])
    edge_ref[...] = jnp.concatenate((p, shear, shear_top, n_top), axis=0).T
    to_scalar.wait()
    waits = [scatter(0, 4, sems.at[5])]

    def stage(slot, carry):
        place = place_ref[0, slot]
        stage_ref[place >> 1, pl.ds(place & 1, 1), :] = edge_ref[pl.ds(slot, 1), :]
        return carry

    lax.fori_loop(0, slots, stage, 0, unroll=8)
    edges = pltpu.make_async_copy(stage_ref, send_ref.at[:, FIELDS], sems.at[7])
    edges.start()
    for field, ref in ((4, mass_ref), (5, strength_ref)):
        fetches[field - 2].wait()
        for s in range(8):
            turn(field, (s, [ref[8 * q + s] for q in range(4)]))
    waits.append(scatter(4, 2, sems.at[6]))
    for wait in waits:
        wait.wait()
    edges.wait()


def fetch_edges(tile_ref, recv_hbm, edge_ref, sem, places):
    count = recv_hbm.shape[0]

    def fetch(i, carry):
        for side, (bx, by) in enumerate(places(i)):
            first = jnp.int32(bx >= BX_DEV // 2) * FIELDS
            block = recv_hbm.at[tile_ref[bx, by] & (count - 1), pl.ds(first, FIELDS + 1)]
            pltpu.make_async_copy(block, edge_ref.at[side * BX_DEV + i], sem).start()
        return carry

    lax.fori_loop(0, BX_DEV, fetch, 0, unroll=4)
    pltpu.make_async_copy(edge_ref, edge_ref, sem).wait()


def lat_kernel(tile_ref, recv_hbm, force_ref, north_ref, south_ref, edge_ref, sem):
    in_group = lane_ids((8, LANES)) % 32
    edges = (0, BY_DEV - 1)
    fetch_edges(tile_ref, recv_hbm, edge_ref, sem, lambda i: [(i, by) for by in edges])

    def lat_rims(half):
        def body(bx, carry):
            for side, (by, ref, first) in enumerate(
                zip(edges, (north_ref, south_ref), (0, B - HALO))
            ):
                place = side * BX_DEV + bx
                iced = tile_ref[bx, by] >= 0
                for v in range(2):
                    total = jnp.zeros((8, LANES), jnp.float32)
                    for k in range(PER_RIM):
                        field = v * PER_RIM + k
                        if field >= FIELDS:
                            got = force_ref[bx * BY_DEV + by, field - FIELDS]
                        else:
                            got = jnp.where(iced, edge_ref[place, half + field], 0.0)
                        mine = (in_group >= HALO * k) & (in_group < HALO * (k + 1))
                        got = pltpu.roll(got, (HALO * k - first) % LANES, 1)
                        total = jnp.where(mine, got, total)
                    ref[bx * 2 + v] = total
                row = edge_ref[place, FIELDS * (1 - half), half : half + 1, :]
                ref[BX_DEV * 2 + half, pl.ds(bx % 8, 1), :] = jnp.where(iced, row, 0.0)
            return carry

        return body

    lax.fori_loop(0, BX_DEV // 2, lat_rims(0), 0, unroll=2)
    lax.fori_loop(BX_DEV // 2, BX_DEV, lat_rims(1), 0, unroll=2)


def lon_kernel(tile_ref, recv_hbm, force_ref, east_ref, west_ref, edge_ref, sem):
    group_of = lane_ids((8, LANES)) // 32
    edges = (0, BX_DEV - 1)
    fetch_edges(tile_ref, recv_hbm, edge_ref, sem, lambda i: [(bx, i) for bx in edges])
    for side, (bx, ref, group) in enumerate(zip(edges, (east_ref, west_ref), (0, 3))):
        half = int(bx >= BX_DEV // 2)
        for part in range(4):
            for field in range(FIELDS + 2):
                total = jnp.zeros((8, LANES), jnp.float32)
                for p in range(4):
                    by = part * 4 + p
                    if field >= FIELDS:
                        got = force_ref[bx * BY_DEV + by, field - FIELDS]
                    else:
                        got = edge_ref[side * BX_DEV + by, half + field]
                        got = jnp.where(tile_ref[bx, by] >= 0, got, 0.0)
                    turned = pltpu.roll(got, ((p - group) * 32) % LANES, 1) if p != group else got
                    total = jnp.where(group_of == p, turned, total)
                ref[field * 4 + part] = total
        for by in range(BY_DEV):
            row = edge_ref[side * BX_DEV + by, FIELDS * (1 - half), half : half + 1, :]
            ref[4 * (FIELDS + 2) + by // 8, by % 8 : by % 8 + 1, :] = jnp.where(
                tile_ref[bx, by] >= 0, row, 0.0
            )


def collect_kernel(tile_ref, recv_ref, force_ref, scr_ref):
    count = recv_ref.shape[0]
    rest = SIDE * SIDE * 8
    for field in range(FIELDS + 3):
        scr_ref[field, pl.ds(rest, GRID_LANES * 8 - rest), :] = jnp.zeros(
            (GRID_LANES * 8 - rest, LANES), jnp.float32
        )

    def collect(half):
        def body(bx, carry):
            for by in range(BY_DEV):
                number = tile_ref[bx, by]
                source = number & (count - 1)
                iced = number >= 0
                for field in range(FIELDS):
                    scr_ref[field, grid_rows(bx, by), :] = jnp.where(
                        iced, recv_ref[source, half * (FIELDS + 1) + field], 0.0
                    )
                for c in range(2):
                    scr_ref[FIELDS + c, grid_rows(bx, by), :] = force_ref[bx * BY_DEV + by, c]
                row = recv_ref[source, FIELDS, half : half + 1, :]
                scr_ref[EDGE, grid_row(bx, by), :] = jnp.where(iced, row, 0.0)
            return carry

        return body

    lax.fori_loop(0, BX_DEV // 2, collect(0), 0)
    lax.fori_loop(BX_DEV // 2, BX_DEV, collect(1), 0)


def force_kernel(force_ref, out_ref):
    def body(bx, carry):
        for part in range(4):
            for c in range(2):
                rows = [
                    force_ref[
                        c,
                        pl.ds(pl.multiple_of(bx * B + 8 * q, 8), 8),
                        pl.ds(part * LANES, LANES),
                    ]
                    for q in range(4)
                ]
                for p, block in enumerate(swap_groups(rows)):
                    out_ref[bx * BY_DEV + part * 4 + p, c] = block
        return carry

    lax.fori_loop(0, BX_DEV, body, 0)


def velocity_kernel(vel_ref, out_ref, scr_ref):
    for c in range(2):
        for t in range(GRID_LANES // LANES):
            for s in range(8):
                cells = [vel_ref[c, 8 * q + s, :, pl.ds(t * LANES, LANES)] for q in range(4)]
                scr_ref[c, pl.ds(t * 8 * LANES + s, LANES, stride=8), :] = jnp.concatenate(
                    cells, axis=0
                ).T

    def body(bx, carry):
        for part in range(4):
            for c in range(2):
                blocks = [
                    scr_ref[
                        c,
                        pl.ds(pl.multiple_of(((bx + 1) * SIDE + part * 4 + p + 1) * 8, 8), 8),
                        :,
                    ]
                    for p in range(4)
                ]
                for q, rows in enumerate(swap_groups(blocks)):
                    out_ref[
                        c,
                        pl.ds(pl.multiple_of(bx * B + 8 * q, 8), 8),
                        pl.ds(part * LANES, LANES),
                    ] = rows
        return carry

    lax.fori_loop(0, BX_DEV, body, 0)


def tile_kernel(
    place_ref,
    lat_ref,
    blocks_ref,
    cell_ref,
    north_ref,
    south_ref,
    east_ref,
    west_ref,
    scr_ref,
    vel_out_ref,
    send_out_ref,
    z_ref,
    m_ref,
    p_ref,
    q_ref,
    s_ref,
    a_ref,
    b_ref,
    fx_ref,
    fy_ref,
    w_ref,
    gx_ref,
    gy_ref,
    turn_ref,
    edge_ref,
    send_ref,
    sems,
):
    del blocks_ref
    lane = lane_ids((8, LANES))
    tiles = GRID_LANES // LANES
    fields = FIELDS + 2
    spot = grid_rows
    in_group = lane % 32

    def lat_rim(bx, north, south, north_row, south_row):
        for field in range(fields):
            v, k = divmod(field, PER_RIM)
            got = pltpu.roll(north(v), (-HALO * k) % LANES, 1)
            scr_ref[field, spot(bx, BY_DEV), :] = jnp.where(in_group < HALO, got, 0.0)
            got = pltpu.roll(south(v), (B - HALO - HALO * k) % LANES, 1)
            scr_ref[field, spot(bx, -1), :] = jnp.where(in_group >= B - HALO, got, 0.0)
        scr_ref[EDGE, grid_row(bx, BY_DEV), :] = north_row
        scr_ref[EDGE, grid_row(bx, -1), :] = south_row

    def lat_rims(bx, carry):
        lat_rim(
            bx,
            lambda v: north_ref[bx * 2 + v],
            lambda v: south_ref[bx * 2 + v],
            north_ref[BX_DEV * 2 + bx // 8, pl.ds(bx % 8, 1), :],
            south_ref[BX_DEV * 2 + bx // 8, pl.ds(bx % 8, 1), :],
        )
        return carry

    lax.fori_loop(0, BX_DEV, lat_rims, 0)
    for ref, bx, group, row in ((west_ref, -1, 3, 7), (east_ref, BX_DEV, 0, 0)):
        for field in range(fields):
            for part in range(4):
                for p in range(4):
                    got = ref[field * 4 + part]
                    got = pltpu.roll(got, ((group - p) * 32) % LANES, 1)
                    scr_ref[field, spot(bx, part * 4 + p), :] = jnp.where(
                        lane // 32 == group, got, 0.0
                    )
        for by in range(BY_DEV):
            scr_ref[EDGE, grid_row(bx, by), :] = ref[
                fields * 4 + by // 8, by % 8 : by % 8 + 1, :
            ]
        lat_rim(
            bx,
            lambda v: ref[LON_RIM + v],
            lambda v: ref[LON_RIM + 2 + v],
            ref[LON_RIM + 4, row : row + 1, :],
            ref[LON_RIM + 5, row : row + 1, :],
        )

    def turn_edges(t, carry):
        start = pl.multiple_of(t * 8 * LANES, 8 * LANES)
        edge_ref[:, pl.ds(pl.multiple_of(t * LANES, LANES), LANES)] = scr_ref[
            EDGE, pl.ds(start, LANES, stride=8), :
        ].T
        return carry

    lax.fori_loop(0, tiles, turn_edges, 0)
    edge_ref[: 2 * B, :] = pltpu.roll(edge_ref[: 2 * B, :], SIDE, 1)
    edge_ref[2 * B :, :] = pltpu.roll(edge_ref[2 * B :, :], 1, 1)
    top_row = row_ids((8, LANES)) == 0

    def prepare(t, carry):
        cols = pl.ds(pl.multiple_of(t * LANES, LANES), LANES)
        for s in range(8):
            start = pl.multiple_of(t * 8 * LANES, 8 * LANES) + s
            turned = [
                scr_ref[field, pl.ds(start, LANES, stride=8), :].T for field in range(fields)
            ]
            for q in range(4):
                plane = 8 * q + s
                zonal, merid, push_x, push_y, mass, strength, fzonal, fmerid = [
                    x[q * B : (q + 1) * B] for x in turned
                ]

                def less(push, base):
                    row = edge_ref[base + plane : base + plane + 1, cols]
                    top = push[:8] - jnp.where(top_row, row, 0.0)
                    return jnp.concatenate((top, push[8:]), axis=0)

                push_x, push_y = less(push_x, 2 * B), less(push_y, 3 * B)
                if plane == 0:
                    push_x = push_x - edge_ref[:B, cols]
                    push_y = push_y - edge_ref[B : 2 * B, cols]
                drag = jnp.where(mass > 0.0, 0.5 / (mass + 0.5), 0.0)
                z_ref[plane + 1, :, cols] = zonal
                m_ref[plane + 1, :, cols] = merid
                for ref in (p_ref, q_ref, s_ref):
                    ref[plane + 1, :, cols] = jnp.zeros((B, LANES), jnp.float32)
                a_ref[plane, :, cols] = 2.0 * mass * drag
                b_ref[plane, :, cols] = drag
                fx_ref[plane, :, cols] = drag * fzonal
                fy_ref[plane, :, cols] = drag * fmerid
                gx_ref[plane, :, cols] = drag * push_x
                gy_ref[plane, :, cols] = drag * push_y
                w_ref[plane, :, cols] = 0.25 * strength
        return carry

    lax.fori_loop(0, tiles, prepare, 0)

    cell = cell_ref[...] + lat_ref[0] * COLS
    turn_ref[...] = (0.5 * CORIOLIS) * (
        2.0 * (cell.astype(jnp.float32) + 0.5) / (lat_ref[1] * COLS).astype(jnp.float32) - 1.0
    )

    sub = row_ids((8, LANES))
    first_row = sub == 0
    last_row = sub == 7

    def north_of(x, edge):
        top = jnp.where(first_row, edge, x[:8])
        return pltpu.roll(jnp.concatenate((top, x[8:]), axis=0), B - 1, 0)

    def south_of(x, edge):
        bottom = jnp.where(last_row, edge, x[B - 8 :])
        return pltpu.roll(jnp.concatenate((x[: B - 8], bottom), axis=0), 1, 0)

    def stress_plane(k):
        z_edge = pltpu.roll(z_ref[k, pl.ds(0, 8), :], GRID_LANES - 1, 1)
        m_edge = pltpu.roll(m_ref[k, pl.ds(0, 8), :], GRID_LANES - 1, 1)
        for t in range(tiles):
            cols = slice(t * LANES, (t + 1) * LANES)
            z, m, w = z_ref[k, :, cols], m_ref[k, :, cols], w_ref[k - 1, :, cols]
            gx = z_ref[k + 1, :, cols] - z
            hx = m_ref[k + 1, :, cols] - m
            gy = north_of(m, m_edge[:, cols]) - m
            hy = north_of(z, z_edge[:, cols]) - z
            div = gx + gy
            ten = gx - gy
            she = hy + hx
            weight = w * lax.rsqrt(div * div + 0.25 * (ten * ten + she * she) + 0.25)
            quarter = 0.25 * weight
            mean = weight * div - w
            dev = quarter * ten
            p_ref[k, :, cols] = 0.5 * p_ref[k, :, cols] + (mean + dev)
            q_ref[k, :, cols] = 0.5 * q_ref[k, :, cols] + (mean - dev)
            s_ref[k, :, cols] = 0.5 * s_ref[k, :, cols] + quarter * she

    def momentum_plane(k, share):
        s_edge = pltpu.roll(s_ref[k, pl.ds(B - 8, 8), :], 1, 1)
        q_edge = pltpu.roll(q_ref[k, pl.ds(B - 8, 8), :], 1, 1)
        for t in range(tiles):
            cols = slice(t * LANES, (t + 1) * LANES)
            z, m = z_ref[k, :, cols], m_ref[k, :, cols]
            a, b = a_ref[k - 1, :, cols], b_ref[k - 1, :, cols]
            s, q = s_ref[k, :, cols], q_ref[k, :, cols]
            push_x = (p_ref[k, :, cols] - p_ref[k - 1, :, cols]) + (
                s - south_of(s, s_edge[:, cols])
            )
            push_y = (s - s_ref[k - 1, :, cols]) + (q - south_of(q, q_edge[:, cols]))
            turn = a * turn_ref[:, cols]
            z_ref[k, :, cols] = (
                a * z + b * push_x + (fx_ref[k - 1, :, cols] + share * gx_ref[k - 1, :, cols]) + turn * m
            )
            m_ref[k, :, cols] = (
                a * m + b * push_y + (fy_ref[k - 1, :, cols] + share * gy_ref[k - 1, :, cols]) - turn * z
            )

    def sweep(step, share):
        for ref in (z_ref, m_ref):
            ref[B + 1] = pltpu.roll(ref[1], GRID_LANES - SIDE, 1)
        stress_plane(B)
        for ref in (p_ref, s_ref):
            ref[0] = pltpu.roll(ref[B], SIDE, 1)
        stress_plane(1)

        def body(k, carry):
            stress_plane(k + 1)
            momentum_plane(k, share)
            return carry

        lax.fori_loop(1, B - 1, body, 0, unroll=True)
        for k in (B - 1, B):
            momentum_plane(k, share)
        return 0.5 * share

    lax.fori_loop(0, ITERS, sweep, jnp.float32(0.5))
    copies = [
        pltpu.make_async_copy(ref.at[pl.ds(1, B)], vel_out_ref.at[c], sems.at[c])
        for c, ref in enumerate((z_ref, m_ref))
    ]
    for copy in copies:
        copy.start()

    def total(k, cols):
        return p_ref[k, :, cols] + q_ref[k, :, cols]

    def difference(k, cols):
        return p_ref[k, :, cols] - q_ref[k, :, cols]

    def shear(k, cols):
        return s_ref[k, :, cols]

    for c, value in enumerate((total, difference, shear)):
        for t in range(tiles):
            cols = slice(t * LANES, (t + 1) * LANES)
            for s in range(8):
                cells = [value(8 * q + s + 1, cols) for q in range(4)]
                scr_ref[c, pl.ds(t * 8 * LANES + s, LANES, stride=8), :] = jnp.concatenate(
                    cells, axis=0
                ).T

        def deal(bx, carry, c=c):
            for by in range(BY_DEV):
                send_ref[place_ref[bx, by], c] = scr_ref[c, spot(bx, by), :]
            return carry

        lax.fori_loop(0, BX_DEV, deal, 0, unroll=2)
        copies.append(
            pltpu.make_async_copy(
                send_ref.at[pl.ds(0, send_out_ref.shape[0]), c],
                send_out_ref.at[:, c],
                sems.at[2 + c],
            )
        )
        copies[-1].start()
    for copy in copies:
        copy.wait()


def unpack_kernel(pos_ref, recv_ref, stress_hbm, out_hbm, out_ref, stress_ref, scr_ref, sems):
    slots = out_ref.shape[-1]
    old, done = [], []
    for c in range(3):
        old.append(pltpu.make_async_copy(stress_hbm.at[c], stress_ref.at[c], sems.at[c]))
        done.append(pltpu.make_async_copy(out_ref.at[c], out_hbm.at[c], sems.at[3 + c]))
        old[c].start()

    def gather(slot, carry):
        place = pos_ref[0, slot]
        rows = pl.ds(pl.multiple_of(slot * 8, 8), 8)
        for c in range(3):
            scr_ref[c, rows, :] = recv_ref[place, c]
        return carry

    lax.fori_loop(0, slots, gather, 0, unroll=8)
    for c in range(3):
        old[c].wait()
        for s in range(8):
            turned = scr_ref[c, pl.ds(s, slots, stride=8), :].T
            for q in range(4):
                ci = 8 * q + s
                out_ref[c, ci] = turned[q * B : (q + 1) * B] + 0.5**ITERS * stress_ref[c, ci]
        done[c].start()
    for copy in done:
        copy.wait()


VMEM = pl.BlockSpec(memory_space=pltpu.VMEM)
SMEM = pl.BlockSpec(memory_space=pltpu.SMEM)
HBM = pl.BlockSpec(memory_space=pltpu.HBM)


def params(mebibytes):
    return pltpu.CompilerParams(vmem_limit_bytes=mebibytes * 1024 * 1024)


def cost(mebibytes):
    return pl.CostEstimate(flops=10**7, bytes_accessed=mebibytes * 2**20, transcendentals=0)


def f32(*shape):
    return jax.ShapeDtypeStruct(shape, jnp.float32)


def on_device(forcing, velocity, stress, mass, strength, owner):
    lon_count = lax.axis_size("lon")
    lat_count = lax.axis_size("lat")
    devices = lon_count * lat_count
    lat_index = lax.axis_index("lat")
    lon_index = lax.axis_index("lon")
    own_index = lon_index * lat_count + lat_index
    slots = velocity.shape[-1]

    my_tile = lax.dynamic_slice(owner, (lon_index * BX_DEV, lat_index * BY_DEV), (BX_DEV, BY_DEV))

    block = (B, B, slots)
    send, pos = pl.pallas_call(
        pack_kernel,
        out_shape=(
            pltpu.HBM((devices, MESSAGE, 8, LANES), jnp.float32),
            jax.ShapeDtypeStruct((1, slots), jnp.int32),
        ),
        in_specs=[SMEM, VMEM] + [HBM] * 4,
        out_specs=(HBM, VMEM),
        scratch_shapes=[
            pltpu.VMEM((2,) + block, jnp.float32),
            pltpu.VMEM((3,) + block, jnp.float32),
            pltpu.VMEM(block, jnp.float32),
            pltpu.VMEM(block, jnp.float32),
            pltpu.VMEM((FIELDS, slots * 8, LANES), jnp.float32),
            pltpu.VMEM((slots, LANES), jnp.float32),
            pltpu.VMEM((devices, 8, LANES), jnp.float32),
            pltpu.SMEM((1, slots), jnp.int32),
            pltpu.SemaphoreType.DMA((8,)),
        ],
        compiler_params=params(61),
    )(own_index.reshape(1).astype(jnp.int32), owner, velocity, stress, mass, strength)
    recv = lax.all_to_all(send, ("lon", "lat"), 0, 0, tiled=True)

    force_blocks = pl.pallas_call(
        force_kernel,
        out_shape=f32(BX_DEV * BY_DEV, 2, 8, LANES),
        in_specs=[VMEM],
        out_specs=VMEM,
        cost_estimate=cost(4),
        compiler_params=params(12),
    )(forcing)
    edge_scratch = [
        pltpu.VMEM((2 * BX_DEV, FIELDS + 1, 8, LANES), jnp.float32),
        pltpu.SemaphoreType.DMA(()),
    ]
    north, south = pl.pallas_call(
        lat_kernel,
        out_shape=(f32(LAT_RIM, 8, LANES),) * 2,
        in_specs=[SMEM, HBM, VMEM],
        out_specs=(VMEM,) * 2,
        scratch_shapes=edge_scratch,
        cost_estimate=cost(4),
        compiler_params=params(8),
    )(my_tile, recv, force_blocks)
    east, west = pl.pallas_call(
        lon_kernel,
        out_shape=(f32(LON_RIM, 8, LANES),) * 2,
        in_specs=[SMEM, HBM, VMEM],
        out_specs=(VMEM,) * 2,
        scratch_shapes=edge_scratch,
        cost_estimate=cost(6),
        compiler_params=params(8),
    )(my_tile, recv, force_blocks)
    blocks = pl.pallas_call(
        collect_kernel,
        out_shape=pltpu.VMEM((FIELDS + 3, GRID_LANES * 8, LANES), jnp.float32),
        in_specs=[SMEM, VMEM, VMEM],
        out_specs=VMEM,
        cost_estimate=cost(24),
        compiler_params=params(12),
    )(my_tile, recv, force_blocks)

    ahead = [(j, j + 1) for j in range(lat_count - 1)]
    got_north = lax.ppermute(north, "lat", [(k, j) for j, k in ahead])
    got_south = lax.ppermute(south, "lat", ahead)
    ring = [(i, (i + 1) % lon_count) for i in range(lon_count)]
    end = BX_DEV * 2

    def with_corners(rim, bx):
        pairs = [x[bx * 2 : bx * 2 + 2] for x in (got_north, got_south)]
        rows = [x[end + bx // 8 : end + bx // 8 + 1] for x in (got_north, got_south)]
        return jnp.concatenate([rim] + pairs + rows, axis=0)

    east = with_corners(east, 0)
    west = with_corners(west, BX_DEV - 1)
    got_east = lax.ppermute(east, "lon", [(k, i) for i, k in ring])
    got_west = lax.ppermute(west, "lon", ring)
    grid = np.arange(GRID_LANES) % SIDE - 1
    cells = jnp.asarray(grid[None, :] * B + np.arange(B)[:, None], jnp.int32)
    state = (B + 2, B, GRID_LANES)
    constant = (B, B, GRID_LANES)
    half = (jnp.arange(BX_DEV, dtype=jnp.int32) // (BX_DEV // 2))[:, None]
    places = jnp.where(my_tile >= 0, (my_tile & (devices - 1)) * 2 + half, 2 * devices)
    _, cell_velocity, back = pl.pallas_call(
        tile_kernel,
        out_shape=(
            pltpu.VMEM((FIELDS + 3, GRID_LANES * 8, LANES), jnp.float32),
            pltpu.HBM((2, B, B, GRID_LANES), jnp.float32),
            pltpu.HBM((devices * 2, 3, 8, LANES), jnp.float32),
        ),
        in_specs=[SMEM, SMEM] + [VMEM] * 6,
        out_specs=(VMEM, HBM, HBM),
        input_output_aliases={2: 0},
        scratch_shapes=[pltpu.VMEM(state, jnp.float32)] * 5
        + [pltpu.VMEM(constant, jnp.float32)] * 7
        + [
            pltpu.VMEM((B, GRID_LANES), jnp.float32),
            pltpu.VMEM((4 * B, GRID_LANES), jnp.float32),
            pltpu.VMEM((devices * 2 + 1, 3, 8, LANES), jnp.float32),
            pltpu.SemaphoreType.DMA((5,)),
        ],
        compiler_params=params(26),
    )(
        places,
        jnp.stack((lat_index, lat_count)).astype(jnp.int32),
        blocks,
        cells,
        got_north,
        got_south,
        got_east,
        got_west,
    )
    returned = lax.all_to_all(
        back.reshape(devices, 6, 8, LANES), ("lon", "lat"), 0, 0, tiled=True
    ).reshape(devices * 2, 3, 8, LANES)
    new_velocity = pl.pallas_call(
        velocity_kernel,
        out_shape=f32(2, ROWS, COLS),
        in_specs=[VMEM],
        out_specs=VMEM,
        scratch_shapes=[pltpu.VMEM((2, GRID_LANES * 8, LANES), jnp.float32)],
        cost_estimate=cost(6),
        compiler_params=params(16),
    )(cell_velocity)
    new_stress = pl.pallas_call(
        unpack_kernel,
        out_shape=pltpu.HBM((3,) + block, jnp.float32),
        in_specs=[SMEM, VMEM, HBM],
        out_specs=HBM,
        scratch_shapes=[
            pltpu.VMEM((3,) + block, jnp.float32),
            pltpu.VMEM((3,) + block, jnp.float32),
            pltpu.VMEM((3, slots * 8, LANES), jnp.float32),
            pltpu.SemaphoreType.DMA((6,)),
        ],
        compiler_params=params(16),
    )(pos, returned, pltpu.with_memory_space_constraint(stress, pltpu.HBM))
    return (new_velocity, new_stress)


def solution(mesh):
    in_specs = (
        P(None, "lon", "lat"),
        P(None, None, None, ("lon", "lat")),
        P(None, None, None, ("lon", "lat")),
        P(None, None, ("lon", "lat")),
        P(None, None, ("lon", "lat")),
        P(),
    )
    out_specs = (P(None, "lon", "lat"), P(None, None, None, ("lon", "lat")))
    return jax.shard_map(
        on_device, mesh=mesh, in_specs=in_specs, out_specs=out_specs, check_vma=False
    )
```

```python
import jax
import jax.numpy as jnp
import numpy as np
from jax import lax
from jax.experimental import pallas as pl
from jax.experimental.pallas import tpu as pltpu
from jax.sharding import PartitionSpec as P

B = 32
BX_DEV = 16
BY_DEV = 16
ITERS = 6
LANES = 128
CORIOLIS = 0.5
HALO = 6
FIELDS = 6
MESSAGE = 2 * FIELDS + 1
EDGE = FIELDS + 2
PER_RIM = 4
ROWS = BX_DEV * B
COLS = BY_DEV * B
LAT_RIM = BX_DEV * 2 + BX_DEV // 8
LON_RIM = 4 * (FIELDS + 2) + BY_DEV // 8
SIDE = BX_DEV + 2
GRID_LANES = -(-SIDE * SIDE // LANES) * LANES


def lane_ids(shape):
    return lax.broadcasted_iota(jnp.int32, shape, len(shape) - 1)


def row_ids(shape):
    return lax.broadcasted_iota(jnp.int32, shape, len(shape) - 2)


def swap_groups(parts):
    lane = lane_ids((8, LANES))
    low = lane < 64
    even = (lane // 32) % 2 == 0
    lo, hi = [], []
    for p in range(2):
        lo.append(jnp.where(low, parts[p], pltpu.roll(parts[p + 2], 64, 1)))
        hi.append(jnp.where(low, pltpu.roll(parts[p], 64, 1), parts[p + 2]))
    out = []
    for pair in (lo, hi):
        out.append(jnp.where(even, pair[0], pltpu.roll(pair[1], 32, 1)))
        out.append(jnp.where(even, pltpu.roll(pair[0], 96, 1), pair[1]))
    return out


def grid_rows(bx, by):
    return pl.ds(pl.multiple_of(((bx + 1) * SIDE + by + 1) * 8, 8), 8)


def grid_row(bx, by):
    return pl.ds(pl.multiple_of(((bx + 1) * SIDE + by + 1) * 8, 8), 1)


def pack_kernel(
    own_ref,
    owner_ref,
    vel_hbm,
    str_hbm,
    mass_hbm,
    strength_hbm,
    send_ref,
    pos_ref,
    vel_ref,
    str_ref,
    mass_ref,
    strength_ref,
    scr_ref,
    edge_ref,
    stage_ref,
    place_ref,
    sems,
):
    slots = vel_ref.shape[-1]
    lon_count = owner_ref.shape[0] // BX_DEV
    lat_count = owner_ref.shape[1] // BY_DEV
    devices = lon_count * lat_count
    fetches = [
        pltpu.make_async_copy(src, dst, sems.at[i])
        for i, (src, dst) in enumerate(
            (
                (vel_hbm, vel_ref),
                (str_hbm, str_ref),
                (mass_hbm, mass_ref),
                (strength_hbm, strength_ref),
            )
        )
    ]
    for fetch in fetches:
        fetch.start()

    half_rows = BX_DEV // 2
    columns = owner_ref.shape[1]

    def dot(x, y):
        return jnp.dot(
            x.astype(jnp.bfloat16), y.astype(jnp.bfloat16), preferred_element_type=jnp.float32
        )

    def square(rows, cols):
        return (
            lax.broadcasted_iota(jnp.int32, (rows, cols), 0),
            lax.broadcasted_iota(jnp.int32, (rows, cols), 1),
        )

    row, col = square(columns, devices)
    of_lat = jnp.where(row // BY_DEV == col % lat_count, 1.0, 0.0)
    iced = jnp.where(owner_ref[...] >= 0, 1.0, 0.0)
    row, col = square(2 * lon_count, owner_ref.shape[0])
    of_half = jnp.where(col // half_rows == row, 1.0, 0.0)
    per_tile = dot(dot(of_half, iced), of_lat)
    row, col = square(2 * lon_count, devices)
    mine = row // 2 == col // lat_count
    counts = [
        jnp.sum(jnp.where(mine & (row % 2 == h), per_tile, 0.0), axis=0, keepdims=True)
        for h in range(2)
    ]
    row, col = square(devices, devices)
    upto = jnp.where(row <= col, 1.0, 0.0)
    both = jnp.broadcast_to(counts[0] + counts[1], (8, devices))
    end_second = dot(both, upto)[:1]
    end_first = end_second - counts[1]
    number = (lax.broadcasted_iota(jnp.int32, (devices, slots), 1) * devices + own_ref[0]).astype(
        jnp.float32
    )
    place = jnp.zeros((1, slots), jnp.float32)
    for end in (end_first, end_second):
        column = jnp.broadcast_to(end, (devices, devices)).T[:, :1]
        place = place + jnp.sum(jnp.where(column <= number, 1.0, 0.0), axis=0, keepdims=True)
    pos_ref[...] = place.astype(jnp.int32)
    to_scalar = pltpu.make_async_copy(pos_ref, place_ref, sems.at[4])
    to_scalar.start()

    def turn(field, planes):
        scr_ref[field, pl.ds(planes[0], slots, stride=8), :] = jnp.concatenate(planes[1], axis=0).T

    def scatter(first, fields, sem):
        def body(slot, carry):
            rows = pl.ds(pl.multiple_of(slot * 8, 8), 8)
            place = place_ref[0, slot]
            pltpu.make_async_copy(
                scr_ref.at[pl.ds(first, fields), rows, :],
                send_ref.at[place >> 1, pl.ds((place & 1) * (FIELDS + 1) + first, fields)],
                sem,
            ).start()
            return carry

        lax.fori_loop(0, slots, body, 0, unroll=8)
        everything = send_ref.at[pl.ds(0, slots), pl.ds(0, fields)]
        return pltpu.make_async_copy(everything, everything, sem)

    first_row = row_ids((B, slots)) == 0

    def south(x):
        return jnp.where(first_row, 0.0, pltpu.roll(x, 1, 0))

    def stresses(ci):
        total, diff = str_ref[0, ci], str_ref[1, ci]
        return 0.5 * (total + diff), 0.5 * (total - diff), str_ref[2, ci]

    fetches[0].wait()
    for c in range(2):
        for s in range(8):
            turn(c, (s, [vel_ref[c, 8 * q + s] for q in range(4)]))
    fetches[1].wait()
    for s in range(8):
        push_x, push_y = [], []
        for q in range(4):
            p, n, shear = stresses(8 * q + s)
            gx = p + (shear - south(shear))
            gy = shear + (n - south(n))
            if q or s:
                p_west, _, shear_west = stresses(8 * q + s - 1)
                gx, gy = gx - p_west, gy - shear_west
            push_x.append(gx)
            push_y.append(gy)
        turn(2, (s, push_x))
        turn(3, (s, push_y))
    p, _, shear = stresses(B - 1)
    shear_top = str_ref[2, :, B - 1, :]
    n_top = 0.5 * (str_ref[0, :, B - 1, :] - str_ref[1, :, B - 1, :])
    edge_ref[...] = jnp.concatenate((p, shear, shear_top, n_top), axis=0).T
    to_scalar.wait()
    waits = [scatter(0, 4, sems.at[5])]

    def stage(slot, carry):
        place = place_ref[0, slot]
        stage_ref[place >> 1, pl.ds(place & 1, 1), :] = edge_ref[pl.ds(slot, 1), :]
        return carry

    lax.fori_loop(0, slots, stage, 0, unroll=8)
    edges = pltpu.make_async_copy(stage_ref, send_ref.at[:, FIELDS], sems.at[7])
    edges.start()
    for field, ref in ((4, mass_ref), (5, strength_ref)):
        fetches[field - 2].wait()
        for s in range(8):
            turn(field, (s, [ref[8 * q + s] for q in range(4)]))
    waits.append(scatter(4, 2, sems.at[6]))
    for wait in waits:
        wait.wait()
    edges.wait()


def fetch_edges(tile_ref, recv_hbm, edge_ref, sem, places):
    count = recv_hbm.shape[0]

    def fetch(i, carry):
        for side, (bx, by) in enumerate(places(i)):
            first = jnp.int32(bx >= BX_DEV // 2) * FIELDS
            block = recv_hbm.at[tile_ref[bx, by] & (count - 1), pl.ds(first, FIELDS + 1)]
            pltpu.make_async_copy(block, edge_ref.at[side * BX_DEV + i], sem).start()
        return carry

    lax.fori_loop(0, BX_DEV, fetch, 0, unroll=4)
    pltpu.make_async_copy(edge_ref, edge_ref, sem).wait()


def lat_kernel(tile_ref, even_ref, recv_hbm, force_ref, near_ref, far_ref, edge_ref, sem):
    in_group = lane_ids((8, LANES)) % 32
    edges = (0, BY_DEV - 1)
    fetch_edges(tile_ref, recv_hbm, edge_ref, sem, lambda i: [(i, by) for by in edges])

    def lat_rims(half):
        def body(bx, carry):
            found = []
            for side, (by, first) in enumerate(zip(edges, (0, B - HALO))):
                place = side * BX_DEV + bx
                iced = tile_ref[bx, by] >= 0
                vectors = []
                for v in range(2):
                    total = jnp.zeros((8, LANES), jnp.float32)
                    for k in range(PER_RIM):
                        field = v * PER_RIM + k
                        if field >= FIELDS:
                            got = force_ref[bx * BY_DEV + by, field - FIELDS]
                        else:
                            got = jnp.where(iced, edge_ref[place, half + field], 0.0)
                        mine = (in_group >= HALO * k) & (in_group < HALO * (k + 1))
                        got = pltpu.roll(got, (HALO * k - first) % LANES, 1)
                        total = jnp.where(mine, got, total)
                    vectors.append(total)
                row = edge_ref[place, FIELDS * (1 - half), half : half + 1, :]
                found.append(vectors + [jnp.where(iced, row, 0.0)])
            even = even_ref[0] == 1
            for ref, kept in ((near_ref, even), (far_ref, jnp.logical_not(even))):
                first_v, second_v, row = [jnp.where(kept, y, x) for x, y in zip(*found)]
                ref[bx * 2] = first_v
                ref[bx * 2 + 1] = second_v
                ref[BX_DEV * 2 + half, pl.ds(bx % 8, 1), :] = row
            return carry

        return body

    lax.fori_loop(0, BX_DEV // 2, lat_rims(0), 0, unroll=2)
    lax.fori_loop(BX_DEV // 2, BX_DEV, lat_rims(1), 0, unroll=2)


def lon_kernel(tile_ref, recv_hbm, force_ref, east_ref, west_ref, edge_ref, sem):
    group_of = lane_ids((8, LANES)) // 32
    edges = (0, BX_DEV - 1)
    fetch_edges(tile_ref, recv_hbm, edge_ref, sem, lambda i: [(bx, i) for bx in edges])
    for side, (bx, ref, group) in enumerate(zip(edges, (east_ref, west_ref), (0, 3))):
        half = int(bx >= BX_DEV // 2)
        for part in range(4):
            for field in range(FIELDS + 2):
                total = jnp.zeros((8, LANES), jnp.float32)
                for p in range(4):
                    by = part * 4 + p
                    if field >= FIELDS:
                        got = force_ref[bx * BY_DEV + by, field - FIELDS]
                    else:
                        got = edge_ref[side * BX_DEV + by, half + field]
                        got = jnp.where(tile_ref[bx, by] >= 0, got, 0.0)
                    turned = pltpu.roll(got, ((p - group) * 32) % LANES, 1) if p != group else got
                    total = jnp.where(group_of == p, turned, total)
                ref[field * 4 + part] = total
        for by in range(BY_DEV):
            row = edge_ref[side * BX_DEV + by, FIELDS * (1 - half), half : half + 1, :]
            ref[4 * (FIELDS + 2) + by // 8, by % 8 : by % 8 + 1, :] = jnp.where(
                tile_ref[bx, by] >= 0, row, 0.0
            )


def collect_kernel(tile_ref, recv_ref, force_ref, scr_ref):
    count = recv_ref.shape[0]
    rest = SIDE * SIDE * 8
    for field in range(FIELDS + 3):
        scr_ref[field, pl.ds(rest, GRID_LANES * 8 - rest), :] = jnp.zeros(
            (GRID_LANES * 8 - rest, LANES), jnp.float32
        )

    def collect(half):
        def body(bx, carry):
            for by in range(BY_DEV):
                number = tile_ref[bx, by]
                source = number & (count - 1)
                iced = number >= 0
                for field in range(FIELDS):
                    scr_ref[field, grid_rows(bx, by), :] = jnp.where(
                        iced, recv_ref[source, half * (FIELDS + 1) + field], 0.0
                    )
                for c in range(2):
                    scr_ref[FIELDS + c, grid_rows(bx, by), :] = force_ref[bx * BY_DEV + by, c]
                row = recv_ref[source, FIELDS, half : half + 1, :]
                scr_ref[EDGE, grid_row(bx, by), :] = jnp.where(iced, row, 0.0)
            return carry

        return body

    lax.fori_loop(0, BX_DEV // 2, collect(0), 0)
    lax.fori_loop(BX_DEV // 2, BX_DEV, collect(1), 0)


def force_kernel(force_ref, out_ref):
    def body(bx, carry):
        for part in range(4):
            for c in range(2):
                rows = [
                    force_ref[
                        c,
                        pl.ds(pl.multiple_of(bx * B + 8 * q, 8), 8),
                        pl.ds(part * LANES, LANES),
                    ]
                    for q in range(4)
                ]
                for p, block in enumerate(swap_groups(rows)):
                    out_ref[bx * BY_DEV + part * 4 + p, c] = block
        return carry

    lax.fori_loop(0, BX_DEV, body, 0)


def velocity_kernel(vel_ref, out_ref, scr_ref):
    for c in range(2):
        for t in range(GRID_LANES // LANES):
            for s in range(8):
                cells = [vel_ref[c, 8 * q + s, :, pl.ds(t * LANES, LANES)] for q in range(4)]
                scr_ref[c, pl.ds(t * 8 * LANES + s, LANES, stride=8), :] = jnp.concatenate(
                    cells, axis=0
                ).T

    def body(bx, carry):
        for part in range(4):
            for c in range(2):
                blocks = [
                    scr_ref[
                        c,
                        pl.ds(pl.multiple_of(((bx + 1) * SIDE + part * 4 + p + 1) * 8, 8), 8),
                        :,
                    ]
                    for p in range(4)
                ]
                for q, rows in enumerate(swap_groups(blocks)):
                    out_ref[
                        c,
                        pl.ds(pl.multiple_of(bx * B + 8 * q, 8), 8),
                        pl.ds(part * LANES, LANES),
                    ] = rows
        return carry

    lax.fori_loop(0, BX_DEV, body, 0)


def tile_kernel(
    place_ref,
    lat_ref,
    blocks_ref,
    cell_ref,
    near_ref,
    far_ref,
    east_ref,
    west_ref,
    scr_ref,
    vel_out_ref,
    send_out_ref,
    z_ref,
    m_ref,
    p_ref,
    q_ref,
    s_ref,
    a_ref,
    b_ref,
    fx_ref,
    fy_ref,
    w_ref,
    gx_ref,
    gy_ref,
    turn_ref,
    edge_ref,
    send_ref,
    sems,
):
    del blocks_ref
    lane = lane_ids((8, LANES))
    tiles = GRID_LANES // LANES
    fields = FIELDS + 2
    spot = grid_rows
    in_group = lane % 32

    even = lat_ref[2] == 1

    def either(x, y):
        return jnp.where(even, x, y), jnp.where(even, y, x)

    def lat_rim(bx, near, far, near_row, far_row):
        north_row, south_row = either(near_row, far_row)
        for field in range(fields):
            v, k = divmod(field, PER_RIM)
            north, south = either(near(v), far(v))
            got = pltpu.roll(north, (-HALO * k) % LANES, 1)
            scr_ref[field, spot(bx, BY_DEV), :] = jnp.where(in_group < HALO, got, 0.0)
            got = pltpu.roll(south, (B - HALO - HALO * k) % LANES, 1)
            scr_ref[field, spot(bx, -1), :] = jnp.where(in_group >= B - HALO, got, 0.0)
        scr_ref[EDGE, grid_row(bx, BY_DEV), :] = north_row
        scr_ref[EDGE, grid_row(bx, -1), :] = south_row

    def lat_rims(bx, carry):
        lat_rim(
            bx,
            lambda v: near_ref[bx * 2 + v],
            lambda v: far_ref[bx * 2 + v],
            near_ref[BX_DEV * 2 + bx // 8, pl.ds(bx % 8, 1), :],
            far_ref[BX_DEV * 2 + bx // 8, pl.ds(bx % 8, 1), :],
        )
        return carry

    lax.fori_loop(0, BX_DEV, lat_rims, 0)
    for ref, bx, group, row in ((west_ref, -1, 3, 7), (east_ref, BX_DEV, 0, 0)):
        for field in range(fields):
            for part in range(4):
                for p in range(4):
                    got = ref[field * 4 + part]
                    got = pltpu.roll(got, ((group - p) * 32) % LANES, 1)
                    scr_ref[field, spot(bx, part * 4 + p), :] = jnp.where(
                        lane // 32 == group, got, 0.0
                    )
        for by in range(BY_DEV):
            scr_ref[EDGE, grid_row(bx, by), :] = ref[
                fields * 4 + by // 8, by % 8 : by % 8 + 1, :
            ]
        lat_rim(
            bx,
            lambda v: ref[LON_RIM + v],
            lambda v: ref[LON_RIM + 2 + v],
            ref[LON_RIM + 4, row : row + 1, :],
            ref[LON_RIM + 5, row : row + 1, :],
        )

    def turn_edges(t, carry):
        start = pl.multiple_of(t * 8 * LANES, 8 * LANES)
        edge_ref[:, pl.ds(pl.multiple_of(t * LANES, LANES), LANES)] = scr_ref[
            EDGE, pl.ds(start, LANES, stride=8), :
        ].T
        return carry

    lax.fori_loop(0, tiles, turn_edges, 0)
    edge_ref[: 2 * B, :] = pltpu.roll(edge_ref[: 2 * B, :], SIDE, 1)
    edge_ref[2 * B :, :] = pltpu.roll(edge_ref[2 * B :, :], 1, 1)
    top_row = row_ids((8, LANES)) == 0

    def prepare(t, carry):
        cols = pl.ds(pl.multiple_of(t * LANES, LANES), LANES)
        for s in range(8):
            start = pl.multiple_of(t * 8 * LANES, 8 * LANES) + s
            turned = [
                scr_ref[field, pl.ds(start, LANES, stride=8), :].T for field in range(fields)
            ]
            for q in range(4):
                plane = 8 * q + s
                zonal, merid, push_x, push_y, mass, strength, fzonal, fmerid = [
                    x[q * B : (q + 1) * B] for x in turned
                ]

                def less(push, base):
                    row = edge_ref[base + plane : base + plane + 1, cols]
                    top = push[:8] - jnp.where(top_row, row, 0.0)
                    return jnp.concatenate((top, push[8:]), axis=0)

                push_x, push_y = less(push_x, 2 * B), less(push_y, 3 * B)
                if plane == 0:
                    push_x = push_x - edge_ref[:B, cols]
                    push_y = push_y - edge_ref[B : 2 * B, cols]
                drag = jnp.where(mass > 0.0, 0.5 / (mass + 0.5), 0.0)
                z_ref[plane + 1, :, cols] = zonal
                m_ref[plane + 1, :, cols] = merid
                for ref in (p_ref, q_ref, s_ref):
                    ref[plane + 1, :, cols] = jnp.zeros((B, LANES), jnp.float32)
                a_ref[plane, :, cols] = 2.0 * mass * drag
                b_ref[plane, :, cols] = drag
                fx_ref[plane, :, cols] = drag * fzonal
                fy_ref[plane, :, cols] = drag * fmerid
                gx_ref[plane, :, cols] = drag * push_x
                gy_ref[plane, :, cols] = drag * push_y
                w_ref[plane, :, cols] = 0.25 * strength
        return carry

    lax.fori_loop(0, tiles, prepare, 0)

    cell = cell_ref[...] + lat_ref[0] * COLS
    turn_ref[...] = (0.5 * CORIOLIS) * (
        2.0 * (cell.astype(jnp.float32) + 0.5) / (lat_ref[1] * COLS).astype(jnp.float32) - 1.0
    )

    sub = row_ids((8, LANES))
    first_row = sub == 0
    last_row = sub == 7

    def north_of(x, edge):
        top = jnp.where(first_row, edge, x[:8])
        return pltpu.roll(jnp.concatenate((top, x[8:]), axis=0), B - 1, 0)

    def south_of(x, edge):
        bottom = jnp.where(last_row, edge, x[B - 8 :])
        return pltpu.roll(jnp.concatenate((x[: B - 8], bottom), axis=0), 1, 0)

    def stress_plane(k):
        z_edge = pltpu.roll(z_ref[k, pl.ds(0, 8), :], GRID_LANES - 1, 1)
        m_edge = pltpu.roll(m_ref[k, pl.ds(0, 8), :], GRID_LANES - 1, 1)
        for t in range(tiles):
            cols = slice(t * LANES, (t + 1) * LANES)
            z, m, w = z_ref[k, :, cols], m_ref[k, :, cols], w_ref[k - 1, :, cols]
            gx = z_ref[k + 1, :, cols] - z
            hx = m_ref[k + 1, :, cols] - m
            gy = north_of(m, m_edge[:, cols]) - m
            hy = north_of(z, z_edge[:, cols]) - z
            div = gx + gy
            ten = gx - gy
            she = hy + hx
            weight = w * lax.rsqrt(div * div + 0.25 * (ten * ten + she * she) + 0.25)
            quarter = 0.25 * weight
            mean = weight * div - w
            dev = quarter * ten
            p_ref[k, :, cols] = 0.5 * p_ref[k, :, cols] + (mean + dev)
            q_ref[k, :, cols] = 0.5 * q_ref[k, :, cols] + (mean - dev)
            s_ref[k, :, cols] = 0.5 * s_ref[k, :, cols] + quarter * she

    def momentum_plane(k, share):
        s_edge = pltpu.roll(s_ref[k, pl.ds(B - 8, 8), :], 1, 1)
        q_edge = pltpu.roll(q_ref[k, pl.ds(B - 8, 8), :], 1, 1)
        for t in range(tiles):
            cols = slice(t * LANES, (t + 1) * LANES)
            z, m = z_ref[k, :, cols], m_ref[k, :, cols]
            a, b = a_ref[k - 1, :, cols], b_ref[k - 1, :, cols]
            s, q = s_ref[k, :, cols], q_ref[k, :, cols]
            push_x = (p_ref[k, :, cols] - p_ref[k - 1, :, cols]) + (
                s - south_of(s, s_edge[:, cols])
            )
            push_y = (s - s_ref[k - 1, :, cols]) + (q - south_of(q, q_edge[:, cols]))
            turn = turn_ref[:, cols]
            z_ref[k, :, cols] = (
                a * (z + turn * m) + b * push_x + (fx_ref[k - 1, :, cols] + share * gx_ref[k - 1, :, cols])
            )
            m_ref[k, :, cols] = (
                a * (m - turn * z) + b * push_y + (fy_ref[k - 1, :, cols] + share * gy_ref[k - 1, :, cols])
            )

    def sweep(step, share):
        for ref in (z_ref, m_ref):
            ref[B + 1] = pltpu.roll(ref[1], GRID_LANES - SIDE, 1)
        stress_plane(B)
        for ref in (p_ref, s_ref):
            ref[0] = pltpu.roll(ref[B], SIDE, 1)
        stress_plane(1)

        def body(k, carry):
            stress_plane(k + 1)
            momentum_plane(k, share)
            return carry

        lax.fori_loop(1, B - 1, body, 0, unroll=True)
        for k in (B - 1, B):
            momentum_plane(k, share)
        return 0.5 * share

    lax.fori_loop(0, ITERS, sweep, jnp.float32(0.5))
    copies = [
        pltpu.make_async_copy(ref.at[pl.ds(1, B)], vel_out_ref.at[c], sems.at[c])
        for c, ref in enumerate((z_ref, m_ref))
    ]
    for copy in copies:
        copy.start()

    def total(k, cols):
        return p_ref[k, :, cols] + q_ref[k, :, cols]

    def difference(k, cols):
        return p_ref[k, :, cols] - q_ref[k, :, cols]

    def shear(k, cols):
        return s_ref[k, :, cols]

    for c, value in enumerate((total, difference, shear)):
        for t in range(tiles):
            cols = slice(t * LANES, (t + 1) * LANES)
            for s in range(8):
                cells = [value(8 * q + s + 1, cols) for q in range(4)]
                scr_ref[c, pl.ds(t * 8 * LANES + s, LANES, stride=8), :] = jnp.concatenate(
                    cells, axis=0
                ).T

        def deal(bx, carry, c=c):
            for by in range(BY_DEV):
                send_ref[place_ref[bx, by], c] = scr_ref[c, spot(bx, by), :]
            return carry

        lax.fori_loop(0, BX_DEV, deal, 0, unroll=2)
        copies.append(
            pltpu.make_async_copy(
                send_ref.at[pl.ds(0, send_out_ref.shape[0]), c],
                send_out_ref.at[:, c],
                sems.at[2 + c],
            )
        )
        copies[-1].start()
    for copy in copies:
        copy.wait()


def unpack_kernel(pos_ref, recv_ref, stress_hbm, out_hbm, out_ref, stress_ref, scr_ref, sems):
    slots = out_ref.shape[-1]
    old, done = [], []
    for c in range(3):
        old.append(pltpu.make_async_copy(stress_hbm.at[c], stress_ref.at[c], sems.at[c]))
        done.append(pltpu.make_async_copy(out_ref.at[c], out_hbm.at[c], sems.at[3 + c]))
        old[c].start()

    def gather(slot, carry):
        place = pos_ref[0, slot]
        rows = pl.ds(pl.multiple_of(slot * 8, 8), 8)
        for c in range(3):
            scr_ref[c, rows, :] = recv_ref[place, c]
        return carry

    lax.fori_loop(0, slots, gather, 0, unroll=8)
    for c in range(3):
        old[c].wait()
        for s in range(8):
            turned = scr_ref[c, pl.ds(s, slots, stride=8), :].T
            for q in range(4):
                ci = 8 * q + s
                out_ref[c, ci] = turned[q * B : (q + 1) * B] + 0.5**ITERS * stress_ref[c, ci]
        done[c].start()
    for copy in done:
        copy.wait()


VMEM = pl.BlockSpec(memory_space=pltpu.VMEM)
SMEM = pl.BlockSpec(memory_space=pltpu.SMEM)
HBM = pl.BlockSpec(memory_space=pltpu.HBM)


def params(mebibytes):
    return pltpu.CompilerParams(vmem_limit_bytes=mebibytes * 1024 * 1024)


def cost(mebibytes):
    return pl.CostEstimate(flops=10**7, bytes_accessed=mebibytes * 2**20, transcendentals=0)


def f32(*shape):
    return jax.ShapeDtypeStruct(shape, jnp.float32)


def on_device(forcing, velocity, stress, mass, strength, owner):
    lon_count = lax.axis_size("lon")
    lat_count = lax.axis_size("lat")
    devices = lon_count * lat_count
    lat_index = lax.axis_index("lat")
    lon_index = lax.axis_index("lon")
    own_index = lon_index * lat_count + lat_index
    slots = velocity.shape[-1]

    my_tile = lax.dynamic_slice(owner, (lon_index * BX_DEV, lat_index * BY_DEV), (BX_DEV, BY_DEV))

    block = (B, B, slots)
    send, pos = pl.pallas_call(
        pack_kernel,
        out_shape=(
            pltpu.HBM((devices, MESSAGE, 8, LANES), jnp.float32),
            jax.ShapeDtypeStruct((1, slots), jnp.int32),
        ),
        in_specs=[SMEM, VMEM] + [HBM] * 4,
        out_specs=(HBM, VMEM),
        scratch_shapes=[
            pltpu.VMEM((2,) + block, jnp.float32),
            pltpu.VMEM((3,) + block, jnp.float32),
            pltpu.VMEM(block, jnp.float32),
            pltpu.VMEM(block, jnp.float32),
            pltpu.VMEM((FIELDS, slots * 8, LANES), jnp.float32),
            pltpu.VMEM((slots, LANES), jnp.float32),
            pltpu.VMEM((devices, 8, LANES), jnp.float32),
            pltpu.SMEM((1, slots), jnp.int32),
            pltpu.SemaphoreType.DMA((8,)),
        ],
        compiler_params=params(61),
    )(own_index.reshape(1).astype(jnp.int32), owner, velocity, stress, mass, strength)
    recv = lax.all_to_all(send, ("lon", "lat"), 0, 0, tiled=True)

    force_blocks = pl.pallas_call(
        force_kernel,
        out_shape=f32(BX_DEV * BY_DEV, 2, 8, LANES),
        in_specs=[VMEM],
        out_specs=VMEM,
        cost_estimate=cost(4),
        compiler_params=params(12),
    )(forcing)
    edge_scratch = [
        pltpu.VMEM((2 * BX_DEV, FIELDS + 1, 8, LANES), jnp.float32),
        pltpu.SemaphoreType.DMA(()),
    ]
    even = 1 - lat_index % 2
    near, far = pl.pallas_call(
        lat_kernel,
        out_shape=(f32(LAT_RIM, 8, LANES),) * 2,
        in_specs=[SMEM, SMEM, HBM, VMEM],
        out_specs=(VMEM,) * 2,
        scratch_shapes=edge_scratch,
        cost_estimate=cost(4),
        compiler_params=params(8),
    )(my_tile, even.reshape(1).astype(jnp.int32), recv, force_blocks)
    east, west = pl.pallas_call(
        lon_kernel,
        out_shape=(f32(LON_RIM, 8, LANES),) * 2,
        in_specs=[SMEM, HBM, VMEM],
        out_specs=(VMEM,) * 2,
        scratch_shapes=edge_scratch,
        cost_estimate=cost(6),
        compiler_params=params(8),
    )(my_tile, recv, force_blocks)
    blocks = pl.pallas_call(
        collect_kernel,
        out_shape=pltpu.VMEM((FIELDS + 3, GRID_LANES * 8, LANES), jnp.float32),
        in_specs=[SMEM, VMEM, VMEM],
        out_specs=VMEM,
        cost_estimate=cost(24),
        compiler_params=params(12),
    )(my_tile, recv, force_blocks)

    def exchange(rim, first):
        pairs = [(j, j + 1) for j in range(first, lat_count - 1, 2)]
        return lax.ppermute(rim, "lat", pairs + [(k, j) for j, k in pairs])

    got_near = exchange(near, 0)
    got_far = exchange(far, 1)
    ring = [(i, (i + 1) % lon_count) for i in range(lon_count)]
    end = BX_DEV * 2

    def with_corners(rim, bx):
        pairs = [x[bx * 2 : bx * 2 + 2] for x in (got_near, got_far)]
        rows = [x[end + bx // 8 : end + bx // 8 + 1] for x in (got_near, got_far)]
        return jnp.concatenate([rim] + pairs + rows, axis=0)

    east = with_corners(east, 0)
    west = with_corners(west, BX_DEV - 1)
    got_east = lax.ppermute(east, "lon", [(k, i) for i, k in ring])
    got_west = lax.ppermute(west, "lon", ring)
    grid = np.arange(GRID_LANES) % SIDE - 1
    cells = jnp.asarray(grid[None, :] * B + np.arange(B)[:, None], jnp.int32)
    state = (B + 2, B, GRID_LANES)
    constant = (B, B, GRID_LANES)
    half = (jnp.arange(BX_DEV, dtype=jnp.int32) // (BX_DEV // 2))[:, None]
    places = jnp.where(my_tile >= 0, (my_tile & (devices - 1)) * 2 + half, 2 * devices)
    _, cell_velocity, back = pl.pallas_call(
        tile_kernel,
        out_shape=(
            pltpu.VMEM((FIELDS + 3, GRID_LANES * 8, LANES), jnp.float32),
            pltpu.HBM((2, B, B, GRID_LANES), jnp.float32),
            pltpu.HBM((devices * 2, 3, 8, LANES), jnp.float32),
        ),
        in_specs=[SMEM, SMEM] + [VMEM] * 6,
        out_specs=(VMEM, HBM, HBM),
        input_output_aliases={2: 0},
        scratch_shapes=[pltpu.VMEM(state, jnp.float32)] * 5
        + [pltpu.VMEM(constant, jnp.float32)] * 7
        + [
            pltpu.VMEM((B, GRID_LANES), jnp.float32),
            pltpu.VMEM((4 * B, GRID_LANES), jnp.float32),
            pltpu.VMEM((devices * 2 + 1, 3, 8, LANES), jnp.float32),
            pltpu.SemaphoreType.DMA((5,)),
        ],
        compiler_params=params(26),
    )(
        places,
        jnp.stack((lat_index, lat_count, even)).astype(jnp.int32),
        blocks,
        cells,
        got_near,
        got_far,
        got_east,
        got_west,
    )
    returned = lax.all_to_all(
        back.reshape(devices, 6, 8, LANES), ("lon", "lat"), 0, 0, tiled=True
    ).reshape(devices * 2, 3, 8, LANES)
    new_velocity = pl.pallas_call(
        velocity_kernel,
        out_shape=f32(2, ROWS, COLS),
        in_specs=[VMEM],
        out_specs=VMEM,
        scratch_shapes=[pltpu.VMEM((2, GRID_LANES * 8, LANES), jnp.float32)],
        cost_estimate=cost(6),
        compiler_params=params(16),
    )(cell_velocity)
    new_stress = pl.pallas_call(
        unpack_kernel,
        out_shape=pltpu.HBM((3,) + block, jnp.float32),
        in_specs=[SMEM, VMEM, HBM],
        out_specs=HBM,
        scratch_shapes=[
            pltpu.VMEM((3,) + block, jnp.float32),
            pltpu.VMEM((3,) + block, jnp.float32),
            pltpu.VMEM((3, slots * 8, LANES), jnp.float32),
            pltpu.SemaphoreType.DMA((6,)),
        ],
        compiler_params=params(16),
    )(pos, returned, pltpu.with_memory_space_constraint(stress, pltpu.HBM))
    return (new_velocity, new_stress)


def solution(mesh):
    in_specs = (
        P(None, "lon", "lat"),
        P(None, None, None, ("lon", "lat")),
        P(None, None, None, ("lon", "lat")),
        P(None, None, ("lon", "lat")),
        P(None, None, ("lon", "lat")),
        P(),
    )
    out_specs = (P(None, "lon", "lat"), P(None, None, None, ("lon", "lat")))
    return jax.shard_map(
        on_device, mesh=mesh, in_specs=in_specs, out_specs=out_specs, check_vma=False
    )
```

```python
import jax
import jax.numpy as jnp
import numpy as np
from jax import lax
from jax.experimental import pallas as pl
from jax.experimental.pallas import tpu as pltpu
from jax.sharding import PartitionSpec as P

B = 32
BX_DEV = 16
BY_DEV = 16
ITERS = 6
LANES = 128
CORIOLIS = 0.5
HALO = 6
FIELDS = 6
MESSAGE = 2 * FIELDS + 1
EDGE = FIELDS + 2
PER_RIM = 4
ROWS = BX_DEV * B
COLS = BY_DEV * B
LAT_RIM = BX_DEV * 2 + BX_DEV // 8
LON_RIM = 4 * (FIELDS + 2) + BY_DEV // 8
SIDE = BX_DEV + 2
GRID_LANES = -(-SIDE * SIDE // LANES) * LANES


def lane_ids(shape):
    return lax.broadcasted_iota(jnp.int32, shape, len(shape) - 1)


def row_ids(shape):
    return lax.broadcasted_iota(jnp.int32, shape, len(shape) - 2)


def swap_groups(parts):
    lane = lane_ids((8, LANES))
    low = lane < 64
    even = (lane // 32) % 2 == 0
    lo, hi = [], []
    for p in range(2):
        lo.append(jnp.where(low, parts[p], pltpu.roll(parts[p + 2], 64, 1)))
        hi.append(jnp.where(low, pltpu.roll(parts[p], 64, 1), parts[p + 2]))
    out = []
    for pair in (lo, hi):
        out.append(jnp.where(even, pair[0], pltpu.roll(pair[1], 32, 1)))
        out.append(jnp.where(even, pltpu.roll(pair[0], 96, 1), pair[1]))
    return out


def grid_rows(bx, by):
    return pl.ds(pl.multiple_of(((bx + 1) * SIDE + by + 1) * 8, 8), 8)


def grid_row(bx, by):
    return pl.ds(pl.multiple_of(((bx + 1) * SIDE + by + 1) * 8, 8), 1)


def pack_kernel(
    own_ref,
    owner_ref,
    vel_hbm,
    str_hbm,
    mass_hbm,
    strength_hbm,
    send_ref,
    pos_ref,
    vel_ref,
    str_ref,
    mass_ref,
    strength_ref,
    scr_ref,
    edge_ref,
    stage_ref,
    place_ref,
    sems,
):
    slots = vel_ref.shape[-1]
    lon_count = owner_ref.shape[0] // BX_DEV
    lat_count = owner_ref.shape[1] // BY_DEV
    devices = lon_count * lat_count
    fetches = [
        pltpu.make_async_copy(src, dst, sems.at[i])
        for i, (src, dst) in enumerate(
            (
                (vel_hbm, vel_ref),
                (str_hbm, str_ref),
                (mass_hbm, mass_ref),
                (strength_hbm, strength_ref),
            )
        )
    ]
    for fetch in fetches:
        fetch.start()

    half_rows = BX_DEV // 2
    columns = owner_ref.shape[1]

    def dot(x, y):
        return jnp.dot(
            x.astype(jnp.bfloat16), y.astype(jnp.bfloat16), preferred_element_type=jnp.float32
        )

    def square(rows, cols):
        return (
            lax.broadcasted_iota(jnp.int32, (rows, cols), 0),
            lax.broadcasted_iota(jnp.int32, (rows, cols), 1),
        )

    row, col = square(columns, devices)
    of_lat = jnp.where(row // BY_DEV == col % lat_count, 1.0, 0.0)
    iced = jnp.where(owner_ref[...] >= 0, 1.0, 0.0)
    row, col = square(2 * lon_count, owner_ref.shape[0])
    of_half = jnp.where(col // half_rows == row, 1.0, 0.0)
    per_tile = dot(dot(of_half, iced), of_lat)
    row, col = square(2 * lon_count, devices)
    mine = row // 2 == col // lat_count
    counts = [
        jnp.sum(jnp.where(mine & (row % 2 == h), per_tile, 0.0), axis=0, keepdims=True)
        for h in range(2)
    ]
    row, col = square(devices, devices)
    upto = jnp.where(row <= col, 1.0, 0.0)
    both = jnp.broadcast_to(counts[0] + counts[1], (8, devices))
    end_second = dot(both, upto)[:1]
    end_first = end_second - counts[1]
    number = (lax.broadcasted_iota(jnp.int32, (devices, slots), 1) * devices + own_ref[0]).astype(
        jnp.float32
    )
    place = jnp.zeros((1, slots), jnp.float32)
    for end in (end_first, end_second):
        column = jnp.broadcast_to(end, (devices, devices)).T[:, :1]
        place = place + jnp.sum(jnp.where(column <= number, 1.0, 0.0), axis=0, keepdims=True)
    pos_ref[...] = place.astype(jnp.int32)
    to_scalar = pltpu.make_async_copy(pos_ref, place_ref, sems.at[4])
    to_scalar.start()

    def turn(field, planes):
        scr_ref[field, pl.ds(planes[0], slots, stride=8), :] = jnp.concatenate(planes[1], axis=0).T

    def scatter(first, fields, sem):
        def body(slot, carry):
            rows = pl.ds(pl.multiple_of(slot * 8, 8), 8)
            place = place_ref[0, slot]
            pltpu.make_async_copy(
                scr_ref.at[pl.ds(first, fields), rows, :],
                send_ref.at[place >> 1, pl.ds((place & 1) * (FIELDS + 1) + first, fields)],
                sem,
            ).start()
            return carry

        lax.fori_loop(0, slots, body, 0, unroll=8)
        everything = send_ref.at[pl.ds(0, slots), pl.ds(0, fields)]
        return pltpu.make_async_copy(everything, everything, sem)

    first_row = row_ids((B, slots)) == 0

    def south(x):
        return jnp.where(first_row, 0.0, pltpu.roll(x, 1, 0))

    def stresses(ci):
        total, diff = str_ref[0, ci], str_ref[1, ci]
        return 0.5 * (total + diff), 0.5 * (total - diff), str_ref[2, ci]

    fetches[0].wait()
    for c in range(2):
        for s in range(8):
            turn(c, (s, [vel_ref[c, 8 * q + s] for q in range(4)]))
    fetches[1].wait()
    for s in range(8):
        push_x, push_y = [], []
        for q in range(4):
            p, n, shear = stresses(8 * q + s)
            gx = p + (shear - south(shear))
            gy = shear + (n - south(n))
            if q or s:
                p_west, _, shear_west = stresses(8 * q + s - 1)
                gx, gy = gx - p_west, gy - shear_west
            push_x.append(gx)
            push_y.append(gy)
        turn(2, (s, push_x))
        turn(3, (s, push_y))
    p, _, shear = stresses(B - 1)
    shear_top = str_ref[2, :, B - 1, :]
    n_top = 0.5 * (str_ref[0, :, B - 1, :] - str_ref[1, :, B - 1, :])
    edge_ref[...] = jnp.concatenate((p, shear, shear_top, n_top), axis=0).T
    to_scalar.wait()
    waits = [scatter(0, 4, sems.at[5])]

    def stage(slot, carry):
        place = place_ref[0, slot]
        stage_ref[place >> 1, pl.ds(place & 1, 1), :] = edge_ref[pl.ds(slot, 1), :]
        return carry

    lax.fori_loop(0, slots, stage, 0, unroll=8)
    edges = pltpu.make_async_copy(stage_ref, send_ref.at[:, FIELDS], sems.at[7])
    edges.start()
    for field, ref in ((4, mass_ref), (5, strength_ref)):
        fetches[field - 2].wait()
        for s in range(8):
            turn(field, (s, [ref[8 * q + s] for q in range(4)]))
    waits.append(scatter(4, 2, sems.at[6]))
    for wait in waits:
        wait.wait()
    edges.wait()


def fetch_edges(tile_ref, recv_hbm, edge_ref, sem, places):
    count = recv_hbm.shape[0]

    def fetch(i, carry):
        for side, (bx, by) in enumerate(places(i)):
            first = jnp.int32(bx >= BX_DEV // 2) * FIELDS
            block = recv_hbm.at[tile_ref[bx, by] & (count - 1), pl.ds(first, FIELDS + 1)]
            pltpu.make_async_copy(block, edge_ref.at[side * BX_DEV + i], sem).start()
        return carry

    lax.fori_loop(0, BX_DEV, fetch, 0, unroll=4)
    pltpu.make_async_copy(edge_ref, edge_ref, sem).wait()


def lat_kernel(tile_ref, even_ref, recv_hbm, force_ref, near_ref, far_ref, edge_ref, sem):
    in_group = lane_ids((8, LANES)) % 32
    edges = (0, BY_DEV - 1)
    fetch_edges(tile_ref, recv_hbm, edge_ref, sem, lambda i: [(i, by) for by in edges])

    def lat_rims(half):
        def body(bx, carry):
            found = []
            for side, (by, first) in enumerate(zip(edges, (0, B - HALO))):
                place = side * BX_DEV + bx
                iced = tile_ref[bx, by] >= 0
                vectors = []
                for v in range(2):
                    total = jnp.zeros((8, LANES), jnp.float32)
                    for k in range(PER_RIM):
                        field = v * PER_RIM + k
                        if field >= FIELDS:
                            got = force_ref[bx * BY_DEV + by, field - FIELDS]
                        else:
                            got = jnp.where(iced, edge_ref[place, half + field], 0.0)
                        mine = (in_group >= HALO * k) & (in_group < HALO * (k + 1))
                        got = pltpu.roll(got, (HALO * k - first) % LANES, 1)
                        total = jnp.where(mine, got, total)
                    vectors.append(total)
                row = edge_ref[place, FIELDS * (1 - half), half : half + 1, :]
                found.append(vectors + [jnp.where(iced, row, 0.0)])
            even = even_ref[0] == 1
            for ref, kept in ((near_ref, even), (far_ref, jnp.logical_not(even))):
                first_v, second_v, row = [jnp.where(kept, y, x) for x, y in zip(*found)]
                ref[bx * 2] = first_v
                ref[bx * 2 + 1] = second_v
                ref[BX_DEV * 2 + half, pl.ds(bx % 8, 1), :] = row
            return carry

        return body

    lax.fori_loop(0, BX_DEV // 2, lat_rims(0), 0, unroll=2)
    lax.fori_loop(BX_DEV // 2, BX_DEV, lat_rims(1), 0, unroll=2)


def lon_kernel(tile_ref, even_ref, recv_hbm, force_ref, near_ref, far_ref, edge_ref, sem):
    group_of = lane_ids((8, LANES)) // 32
    edges = (0, BX_DEV - 1)
    even = even_ref[0] == 1
    fetch_edges(tile_ref, recv_hbm, edge_ref, sem, lambda i: [(bx, i) for bx in edges])

    def keep(first, last, index):
        near_ref[index] = jnp.where(even, last, first)
        far_ref[index] = jnp.where(even, first, last)

    for part in range(4):
        for field in range(FIELDS + 2):
            found = []
            for side, (bx, group) in enumerate(zip(edges, (0, 3))):
                half = int(bx >= BX_DEV // 2)
                total = jnp.zeros((8, LANES), jnp.float32)
                for p in range(4):
                    by = part * 4 + p
                    if field >= FIELDS:
                        got = force_ref[bx * BY_DEV + by, field - FIELDS]
                    else:
                        got = edge_ref[side * BX_DEV + by, half + field]
                        got = jnp.where(tile_ref[bx, by] >= 0, got, 0.0)
                    turned = pltpu.roll(got, ((p - group) * 32) % LANES, 1) if p != group else got
                    total = jnp.where(group_of == p, turned, total)
                found.append(total)
            keep(*found, field * 4 + part)
    sub = row_ids((8, LANES))
    for v in range(BY_DEV // 8):
        found = []
        for side, bx in enumerate(edges):
            half = int(bx >= BX_DEV // 2)
            total = jnp.zeros((8, LANES), jnp.float32)
            for r in range(8):
                by = v * 8 + r
                row = edge_ref[side * BX_DEV + by, FIELDS * (1 - half), half : half + 1, :]
                row = jnp.where(tile_ref[bx, by] >= 0, row, 0.0)
                total = jnp.where(sub == r, row, total)
            found.append(total)
        keep(*found, 4 * (FIELDS + 2) + v)


def collect_kernel(tile_ref, recv_ref, force_ref, scr_ref):
    count = recv_ref.shape[0]
    rest = SIDE * SIDE * 8
    for field in range(FIELDS + 3):
        scr_ref[field, pl.ds(rest, GRID_LANES * 8 - rest), :] = jnp.zeros(
            (GRID_LANES * 8 - rest, LANES), jnp.float32
        )

    def collect(half):
        def body(bx, carry):
            for by in range(BY_DEV):
                number = tile_ref[bx, by]
                source = number & (count - 1)
                iced = number >= 0
                for field in range(FIELDS):
                    scr_ref[field, grid_rows(bx, by), :] = jnp.where(
                        iced, recv_ref[source, half * (FIELDS + 1) + field], 0.0
                    )
                for c in range(2):
                    scr_ref[FIELDS + c, grid_rows(bx, by), :] = force_ref[bx * BY_DEV + by, c]
                row = recv_ref[source, FIELDS, half : half + 1, :]
                scr_ref[EDGE, grid_row(bx, by), :] = jnp.where(iced, row, 0.0)
            return carry

        return body

    lax.fori_loop(0, BX_DEV // 2, collect(0), 0)
    lax.fori_loop(BX_DEV // 2, BX_DEV, collect(1), 0)


def force_kernel(force_ref, out_ref):
    def body(bx, carry):
        for part in range(4):
            for c in range(2):
                rows = [
                    force_ref[
                        c,
                        pl.ds(pl.multiple_of(bx * B + 8 * q, 8), 8),
                        pl.ds(part * LANES, LANES),
                    ]
                    for q in range(4)
                ]
                for p, block in enumerate(swap_groups(rows)):
                    out_ref[bx * BY_DEV + part * 4 + p, c] = block
        return carry

    lax.fori_loop(0, BX_DEV, body, 0)


def velocity_kernel(vel_ref, out_ref, scr_ref):
    for c in range(2):
        for t in range(GRID_LANES // LANES):
            for s in range(8):
                cells = [vel_ref[c, 8 * q + s, :, pl.ds(t * LANES, LANES)] for q in range(4)]
                scr_ref[c, pl.ds(t * 8 * LANES + s, LANES, stride=8), :] = jnp.concatenate(
                    cells, axis=0
                ).T

    def body(bx, carry):
        for part in range(4):
            for c in range(2):
                blocks = [
                    scr_ref[
                        c,
                        pl.ds(pl.multiple_of(((bx + 1) * SIDE + part * 4 + p + 1) * 8, 8), 8),
                        :,
                    ]
                    for p in range(4)
                ]
                for q, rows in enumerate(swap_groups(blocks)):
                    out_ref[
                        c,
                        pl.ds(pl.multiple_of(bx * B + 8 * q, 8), 8),
                        pl.ds(part * LANES, LANES),
                    ] = rows
        return carry

    lax.fori_loop(0, BX_DEV, body, 0)


def tile_kernel(
    place_ref,
    lat_ref,
    blocks_ref,
    cell_ref,
    near_ref,
    far_ref,
    lon_near_ref,
    lon_far_ref,
    scr_ref,
    vel_out_ref,
    send_out_ref,
    z_ref,
    m_ref,
    p_ref,
    q_ref,
    s_ref,
    a_ref,
    b_ref,
    fx_ref,
    fy_ref,
    w_ref,
    gx_ref,
    gy_ref,
    turn_ref,
    edge_ref,
    send_ref,
    sems,
):
    del blocks_ref
    lane = lane_ids((8, LANES))
    tiles = GRID_LANES // LANES
    fields = FIELDS + 2
    spot = grid_rows
    in_group = lane % 32

    even = lat_ref[2] == 1

    def either(x, y):
        return jnp.where(even, x, y), jnp.where(even, y, x)

    def lat_rim(bx, near, far, near_row, far_row):
        north_row, south_row = either(near_row, far_row)
        for field in range(fields):
            v, k = divmod(field, PER_RIM)
            north, south = either(near(v), far(v))
            got = pltpu.roll(north, (-HALO * k) % LANES, 1)
            scr_ref[field, spot(bx, BY_DEV), :] = jnp.where(in_group < HALO, got, 0.0)
            got = pltpu.roll(south, (B - HALO - HALO * k) % LANES, 1)
            scr_ref[field, spot(bx, -1), :] = jnp.where(in_group >= B - HALO, got, 0.0)
        scr_ref[EDGE, grid_row(bx, BY_DEV), :] = north_row
        scr_ref[EDGE, grid_row(bx, -1), :] = south_row

    def lat_rims(bx, carry):
        lat_rim(
            bx,
            lambda v: near_ref[bx * 2 + v],
            lambda v: far_ref[bx * 2 + v],
            near_ref[BX_DEV * 2 + bx // 8, pl.ds(bx % 8, 1), :],
            far_ref[BX_DEV * 2 + bx // 8, pl.ds(bx % 8, 1), :],
        )
        return carry

    lax.fori_loop(0, BX_DEV, lat_rims, 0)
    lon_even = lat_ref[3] == 1

    def west(i):
        return jnp.where(lon_even, lon_far_ref[i], lon_near_ref[i])

    def east(i):
        return jnp.where(lon_even, lon_near_ref[i], lon_far_ref[i])

    for rim, bx, group, row in ((west, -1, 3, 7), (east, BX_DEV, 0, 0)):
        for field in range(fields):
            for part in range(4):
                whole = rim(field * 4 + part)
                for p in range(4):
                    got = pltpu.roll(whole, ((group - p) * 32) % LANES, 1)
                    scr_ref[field, spot(bx, part * 4 + p), :] = jnp.where(
                        lane // 32 == group, got, 0.0
                    )
        for by in range(BY_DEV):
            scr_ref[EDGE, grid_row(bx, by), :] = rim(fields * 4 + by // 8)[by % 8 : by % 8 + 1]
        lat_rim(
            bx,
            lambda v: rim(LON_RIM + v),
            lambda v: rim(LON_RIM + 2 + v),
            rim(LON_RIM + 4)[row : row + 1],
            rim(LON_RIM + 5)[row : row + 1],
        )

    def turn_edges(t, carry):
        start = pl.multiple_of(t * 8 * LANES, 8 * LANES)
        edge_ref[:, pl.ds(pl.multiple_of(t * LANES, LANES), LANES)] = scr_ref[
            EDGE, pl.ds(start, LANES, stride=8), :
        ].T
        return carry

    lax.fori_loop(0, tiles, turn_edges, 0)
    edge_ref[: 2 * B, :] = pltpu.roll(edge_ref[: 2 * B, :], SIDE, 1)
    edge_ref[2 * B :, :] = pltpu.roll(edge_ref[2 * B :, :], 1, 1)
    top_row = row_ids((8, LANES)) == 0

    def prepare(t, carry):
        cols = pl.ds(pl.multiple_of(t * LANES, LANES), LANES)
        for s in range(8):
            start = pl.multiple_of(t * 8 * LANES, 8 * LANES) + s
            turned = [
                scr_ref[field, pl.ds(start, LANES, stride=8), :].T for field in range(fields)
            ]
            for q in range(4):
                plane = 8 * q + s
                zonal, merid, push_x, push_y, mass, strength, fzonal, fmerid = [
                    x[q * B : (q + 1) * B] for x in turned
                ]

                def less(push, base):
                    row = edge_ref[base + plane : base + plane + 1, cols]
                    top = push[:8] - jnp.where(top_row, row, 0.0)
                    return jnp.concatenate((top, push[8:]), axis=0)

                push_x, push_y = less(push_x, 2 * B), less(push_y, 3 * B)
                if plane == 0:
                    push_x = push_x - edge_ref[:B, cols]
                    push_y = push_y - edge_ref[B : 2 * B, cols]
                drag = jnp.where(mass > 0.0, 0.5 / (mass + 0.5), 0.0)
                z_ref[plane + 1, :, cols] = zonal
                m_ref[plane + 1, :, cols] = merid
                for ref in (p_ref, q_ref, s_ref):
                    ref[plane + 1, :, cols] = jnp.zeros((B, LANES), jnp.float32)
                a_ref[plane, :, cols] = 2.0 * mass * drag
                b_ref[plane, :, cols] = drag
                fx_ref[plane, :, cols] = drag * fzonal
                fy_ref[plane, :, cols] = drag * fmerid
                gx_ref[plane, :, cols] = drag * push_x
                gy_ref[plane, :, cols] = drag * push_y
                w_ref[plane, :, cols] = 0.25 * strength
        return carry

    lax.fori_loop(0, tiles, prepare, 0)

    cell = cell_ref[...] + lat_ref[0] * COLS
    turn_ref[...] = (0.5 * CORIOLIS) * (
        2.0 * (cell.astype(jnp.float32) + 0.5) / (lat_ref[1] * COLS).astype(jnp.float32) - 1.0
    )

    sub = row_ids((8, LANES))
    first_row = sub == 0
    last_row = sub == 7

    def north_of(x, edge):
        top = jnp.where(first_row, edge, x[:8])
        return pltpu.roll(jnp.concatenate((top, x[8:]), axis=0), B - 1, 0)

    def south_of(x, edge):
        bottom = jnp.where(last_row, edge, x[B - 8 :])
        return pltpu.roll(jnp.concatenate((x[: B - 8], bottom), axis=0), 1, 0)

    def stress_plane(k):
        z_edge = pltpu.roll(z_ref[k, pl.ds(0, 8), :], GRID_LANES - 1, 1)
        m_edge = pltpu.roll(m_ref[k, pl.ds(0, 8), :], GRID_LANES - 1, 1)
        for t in range(tiles):
            cols = slice(t * LANES, (t + 1) * LANES)
            z, m, w = z_ref[k, :, cols], m_ref[k, :, cols], w_ref[k - 1, :, cols]
            gx = z_ref[k + 1, :, cols] - z
            hx = m_ref[k + 1, :, cols] - m
            gy = north_of(m, m_edge[:, cols]) - m
            hy = north_of(z, z_edge[:, cols]) - z
            div = gx + gy
            ten = gx - gy
            she = hy + hx
            weight = w * lax.rsqrt(div * div + 0.25 * (ten * ten + she * she) + 0.25)
            quarter = 0.25 * weight
            mean = weight * div - w
            dev = quarter * ten
            p_ref[k, :, cols] = 0.5 * p_ref[k, :, cols] + (mean + dev)
            q_ref[k, :, cols] = 0.5 * q_ref[k, :, cols] + (mean - dev)
            s_ref[k, :, cols] = 0.5 * s_ref[k, :, cols] + quarter * she

    def momentum_plane(k, share):
        s_edge = pltpu.roll(s_ref[k, pl.ds(B - 8, 8), :], 1, 1)
        q_edge = pltpu.roll(q_ref[k, pl.ds(B - 8, 8), :], 1, 1)
        for t in range(tiles):
            cols = slice(t * LANES, (t + 1) * LANES)
            z, m = z_ref[k, :, cols], m_ref[k, :, cols]
            a, b = a_ref[k - 1, :, cols], b_ref[k - 1, :, cols]
            s, q = s_ref[k, :, cols], q_ref[k, :, cols]
            push_x = (p_ref[k, :, cols] - p_ref[k - 1, :, cols]) + (
                s - south_of(s, s_edge[:, cols])
            )
            push_y = (s - s_ref[k - 1, :, cols]) + (q - south_of(q, q_edge[:, cols]))
            turn = turn_ref[:, cols]
            z_ref[k, :, cols] = (
                a * (z + turn * m) + b * push_x + (fx_ref[k - 1, :, cols] + share * gx_ref[k - 1, :, cols])
            )
            m_ref[k, :, cols] = (
                a * (m - turn * z) + b * push_y + (fy_ref[k - 1, :, cols] + share * gy_ref[k - 1, :, cols])
            )

    def sweep(step, share):
        for ref in (z_ref, m_ref):
            ref[B + 1] = pltpu.roll(ref[1], GRID_LANES - SIDE, 1)
        stress_plane(B)
        for ref in (p_ref, s_ref):
            ref[0] = pltpu.roll(ref[B], SIDE, 1)
        stress_plane(1)

        def body(k, carry):
            stress_plane(k + 1)
            momentum_plane(k, share)
            return carry

        lax.fori_loop(1, B - 1, body, 0, unroll=True)
        for k in (B - 1, B):
            momentum_plane(k, share)
        return 0.5 * share

    lax.fori_loop(0, ITERS, sweep, jnp.float32(0.5))
    copies = [
        pltpu.make_async_copy(ref.at[pl.ds(1, B)], vel_out_ref.at[c], sems.at[c])
        for c, ref in enumerate((z_ref, m_ref))
    ]
    for copy in copies:
        copy.start()

    def total(k, cols):
        return p_ref[k, :, cols] + q_ref[k, :, cols]

    def difference(k, cols):
        return p_ref[k, :, cols] - q_ref[k, :, cols]

    def shear(k, cols):
        return s_ref[k, :, cols]

    for c, value in enumerate((total, difference, shear)):
        for t in range(tiles):
            cols = slice(t * LANES, (t + 1) * LANES)
            for s in range(8):
                cells = [value(8 * q + s + 1, cols) for q in range(4)]
                scr_ref[c, pl.ds(t * 8 * LANES + s, LANES, stride=8), :] = jnp.concatenate(
                    cells, axis=0
                ).T

        def deal(bx, carry, c=c):
            for by in range(BY_DEV):
                send_ref[place_ref[bx, by], c] = scr_ref[c, spot(bx, by), :]
            return carry

        lax.fori_loop(0, BX_DEV, deal, 0, unroll=2)
        copies.append(
            pltpu.make_async_copy(
                send_ref.at[pl.ds(0, send_out_ref.shape[0]), c],
                send_out_ref.at[:, c],
                sems.at[2 + c],
            )
        )
        copies[-1].start()
    for copy in copies:
        copy.wait()


def unpack_kernel(pos_ref, recv_ref, stress_hbm, out_hbm, out_ref, stress_ref, scr_ref, sems):
    slots = out_ref.shape[-1]
    old, done = [], []
    for c in range(3):
        old.append(pltpu.make_async_copy(stress_hbm.at[c], stress_ref.at[c], sems.at[c]))
        done.append(pltpu.make_async_copy(out_ref.at[c], out_hbm.at[c], sems.at[3 + c]))
        old[c].start()

    def gather(slot, carry):
        place = pos_ref[0, slot]
        rows = pl.ds(pl.multiple_of(slot * 8, 8), 8)
        for c in range(3):
            scr_ref[c, rows, :] = recv_ref[place, c]
        return carry

    lax.fori_loop(0, slots, gather, 0, unroll=8)
    for c in range(3):
        old[c].wait()
        for s in range(8):
            turned = scr_ref[c, pl.ds(s, slots, stride=8), :].T
            for q in range(4):
                ci = 8 * q + s
                out_ref[c, ci] = turned[q * B : (q + 1) * B] + 0.5**ITERS * stress_ref[c, ci]
        done[c].start()
    for copy in done:
        copy.wait()


VMEM = pl.BlockSpec(memory_space=pltpu.VMEM)
SMEM = pl.BlockSpec(memory_space=pltpu.SMEM)
HBM = pl.BlockSpec(memory_space=pltpu.HBM)


def params(mebibytes):
    return pltpu.CompilerParams(vmem_limit_bytes=mebibytes * 1024 * 1024)


def cost(mebibytes):
    return pl.CostEstimate(flops=10**7, bytes_accessed=mebibytes * 2**20, transcendentals=0)


def f32(*shape):
    return jax.ShapeDtypeStruct(shape, jnp.float32)


def on_device(forcing, velocity, stress, mass, strength, owner):
    lon_count = lax.axis_size("lon")
    lat_count = lax.axis_size("lat")
    devices = lon_count * lat_count
    lat_index = lax.axis_index("lat")
    lon_index = lax.axis_index("lon")
    own_index = lon_index * lat_count + lat_index
    slots = velocity.shape[-1]

    my_tile = lax.dynamic_slice(owner, (lon_index * BX_DEV, lat_index * BY_DEV), (BX_DEV, BY_DEV))

    block = (B, B, slots)
    send, pos = pl.pallas_call(
        pack_kernel,
        out_shape=(
            pltpu.HBM((devices, MESSAGE, 8, LANES), jnp.float32),
            jax.ShapeDtypeStruct((1, slots), jnp.int32),
        ),
        in_specs=[SMEM, VMEM] + [HBM] * 4,
        out_specs=(HBM, VMEM),
        scratch_shapes=[
            pltpu.VMEM((2,) + block, jnp.float32),
            pltpu.VMEM((3,) + block, jnp.float32),
            pltpu.VMEM(block, jnp.float32),
            pltpu.VMEM(block, jnp.float32),
            pltpu.VMEM((FIELDS, slots * 8, LANES), jnp.float32),
            pltpu.VMEM((slots, LANES), jnp.float32),
            pltpu.VMEM((devices, 8, LANES), jnp.float32),
            pltpu.SMEM((1, slots), jnp.int32),
            pltpu.SemaphoreType.DMA((8,)),
        ],
        compiler_params=params(61),
    )(own_index.reshape(1).astype(jnp.int32), owner, velocity, stress, mass, strength)
    recv = lax.all_to_all(send, ("lon", "lat"), 0, 0, tiled=True)

    force_blocks = pl.pallas_call(
        force_kernel,
        out_shape=f32(BX_DEV * BY_DEV, 2, 8, LANES),
        in_specs=[VMEM],
        out_specs=VMEM,
        cost_estimate=cost(4),
        compiler_params=params(12),
    )(forcing)
    edge_scratch = [
        pltpu.VMEM((2 * BX_DEV, FIELDS + 1, 8, LANES), jnp.float32),
        pltpu.SemaphoreType.DMA(()),
    ]
    even = 1 - lat_index % 2
    near, far = pl.pallas_call(
        lat_kernel,
        out_shape=(f32(LAT_RIM, 8, LANES),) * 2,
        in_specs=[SMEM, SMEM, HBM, VMEM],
        out_specs=(VMEM,) * 2,
        scratch_shapes=edge_scratch,
        cost_estimate=cost(4),
        compiler_params=params(8),
    )(my_tile, even.reshape(1).astype(jnp.int32), recv, force_blocks)
    lon_even = 1 - lon_index % 2
    lon_near, lon_far = pl.pallas_call(
        lon_kernel,
        out_shape=(f32(LON_RIM, 8, LANES),) * 2,
        in_specs=[SMEM, SMEM, HBM, VMEM],
        out_specs=(VMEM,) * 2,
        scratch_shapes=edge_scratch,
        cost_estimate=cost(6),
        compiler_params=params(8),
    )(my_tile, lon_even.reshape(1).astype(jnp.int32), recv, force_blocks)
    blocks = pl.pallas_call(
        collect_kernel,
        out_shape=pltpu.VMEM((FIELDS + 3, GRID_LANES * 8, LANES), jnp.float32),
        in_specs=[SMEM, VMEM, VMEM],
        out_specs=VMEM,
        cost_estimate=cost(24),
        compiler_params=params(12),
    )(my_tile, recv, force_blocks)

    def exchange(rim, first):
        pairs = [(j, j + 1) for j in range(first, lat_count - 1, 2)]
        return lax.ppermute(rim, "lat", pairs + [(k, j) for j, k in pairs])

    got_near = exchange(near, 0)
    got_far = exchange(far, 1)
    end = BX_DEV * 2
    rows = BX_DEV // 8

    def with_corners(rim, last):
        pairs = [jnp.where(last, x[end - 2 : end], x[:2]) for x in (got_near, got_far)]
        edge = [jnp.where(last, x[end + rows - 1 :], x[end : end + 1]) for x in (got_near, got_far)]
        return jnp.concatenate([rim] + pairs + edge, axis=0)

    def exchange_lon(rim, first):
        pairs = [(i, (i + 1) % lon_count) for i in range(first, lon_count, 2)]
        return lax.ppermute(rim, "lon", pairs + [(k, i) for i, k in pairs])

    got_lon_near = exchange_lon(with_corners(lon_near, lon_even == 1), 0)
    got_lon_far = exchange_lon(with_corners(lon_far, lon_even == 0), 1)
    grid = np.arange(GRID_LANES) % SIDE - 1
    cells = jnp.asarray(grid[None, :] * B + np.arange(B)[:, None], jnp.int32)
    state = (B + 2, B, GRID_LANES)
    constant = (B, B, GRID_LANES)
    half = (jnp.arange(BX_DEV, dtype=jnp.int32) // (BX_DEV // 2))[:, None]
    places = jnp.where(my_tile >= 0, (my_tile & (devices - 1)) * 2 + half, 2 * devices)
    _, cell_velocity, back = pl.pallas_call(
        tile_kernel,
        out_shape=(
            pltpu.VMEM((FIELDS + 3, GRID_LANES * 8, LANES), jnp.float32),
            pltpu.HBM((2, B, B, GRID_LANES), jnp.float32),
            pltpu.HBM((devices * 2, 3, 8, LANES), jnp.float32),
        ),
        in_specs=[SMEM, SMEM] + [VMEM] * 6,
        out_specs=(VMEM, HBM, HBM),
        input_output_aliases={2: 0},
        scratch_shapes=[pltpu.VMEM(state, jnp.float32)] * 5
        + [pltpu.VMEM(constant, jnp.float32)] * 7
        + [
            pltpu.VMEM((B, GRID_LANES), jnp.float32),
            pltpu.VMEM((4 * B, GRID_LANES), jnp.float32),
            pltpu.VMEM((devices * 2 + 1, 3, 8, LANES), jnp.float32),
            pltpu.SemaphoreType.DMA((5,)),
        ],
        compiler_params=params(26),
    )(
        places,
        jnp.stack((lat_index, lat_count, even, lon_even)).astype(jnp.int32),
        blocks,
        cells,
        got_near,
        got_far,
        got_lon_near,
        got_lon_far,
    )
    returned = lax.all_to_all(
        back.reshape(devices, 6, 8, LANES), ("lon", "lat"), 0, 0, tiled=True
    ).reshape(devices * 2, 3, 8, LANES)
    new_velocity = pl.pallas_call(
        velocity_kernel,
        out_shape=f32(2, ROWS, COLS),
        in_specs=[VMEM],
        out_specs=VMEM,
        scratch_shapes=[pltpu.VMEM((2, GRID_LANES * 8, LANES), jnp.float32)],
        cost_estimate=cost(6),
        compiler_params=params(16),
    )(cell_velocity)
    new_stress = pl.pallas_call(
        unpack_kernel,
        out_shape=pltpu.HBM((3,) + block, jnp.float32),
        in_specs=[SMEM, VMEM, HBM],
        out_specs=HBM,
        scratch_shapes=[
            pltpu.VMEM((3,) + block, jnp.float32),
            pltpu.VMEM((3,) + block, jnp.float32),
            pltpu.VMEM((3, slots * 8, LANES), jnp.float32),
            pltpu.SemaphoreType.DMA((6,)),
        ],
        compiler_params=params(16),
    )(pos, returned, pltpu.with_memory_space_constraint(stress, pltpu.HBM))
    return (new_velocity, new_stress)


def solution(mesh):
    in_specs = (
        P(None, "lon", "lat"),
        P(None, None, None, ("lon", "lat")),
        P(None, None, None, ("lon", "lat")),
        P(None, None, ("lon", "lat")),
        P(None, None, ("lon", "lat")),
        P(),
    )
    out_specs = (P(None, "lon", "lat"), P(None, None, None, ("lon", "lat")))
    return jax.shard_map(
        on_device, mesh=mesh, in_specs=in_specs, out_specs=out_specs, check_vma=False
    )
```

```python
import jax
import jax.numpy as jnp
import numpy as np
from jax import lax
from jax.experimental import pallas as pl
from jax.experimental.pallas import tpu as pltpu
from jax.sharding import PartitionSpec as P

B = 32
BX_DEV = 16
BY_DEV = 16
ITERS = 6
LANES = 128
CORIOLIS = 0.5
HALO = 6
FIELDS = 6
MESSAGE = 2 * FIELDS + 1
EDGE = FIELDS + 2
PER_RIM = 4
ROWS = BX_DEV * B
COLS = BY_DEV * B
LAT_RIM = BX_DEV * 2 + BX_DEV // 8
LON_RIM = 4 * (FIELDS + 2) + BY_DEV // 8
SIDE = BX_DEV + 2
GRID_LANES = -(-SIDE * SIDE // LANES) * LANES


def lane_ids(shape):
    return lax.broadcasted_iota(jnp.int32, shape, len(shape) - 1)


def row_ids(shape):
    return lax.broadcasted_iota(jnp.int32, shape, len(shape) - 2)


def swap_groups(parts):
    lane = lane_ids((8, LANES))
    low = lane < 64
    even = (lane // 32) % 2 == 0
    lo, hi = [], []
    for p in range(2):
        lo.append(jnp.where(low, parts[p], pltpu.roll(parts[p + 2], 64, 1)))
        hi.append(jnp.where(low, pltpu.roll(parts[p], 64, 1), parts[p + 2]))
    out = []
    for pair in (lo, hi):
        out.append(jnp.where(even, pair[0], pltpu.roll(pair[1], 32, 1)))
        out.append(jnp.where(even, pltpu.roll(pair[0], 96, 1), pair[1]))
    return out


def grid_rows(bx, by):
    return pl.ds(pl.multiple_of(((bx + 1) * SIDE + by + 1) * 8, 8), 8)


def grid_row(bx, by):
    return pl.ds(pl.multiple_of(((bx + 1) * SIDE + by + 1) * 8, 8), 1)


def pack_kernel(
    own_ref,
    owner_ref,
    vel_hbm,
    str_hbm,
    mass_hbm,
    strength_hbm,
    send_ref,
    pos_ref,
    vel_ref,
    str_ref,
    mass_ref,
    strength_ref,
    scr_ref,
    edge_ref,
    stage_ref,
    place_ref,
    sems,
):
    slots = vel_ref.shape[-1]
    lon_count = owner_ref.shape[0] // BX_DEV
    lat_count = owner_ref.shape[1] // BY_DEV
    devices = lon_count * lat_count
    fetches = [
        pltpu.make_async_copy(src, dst, sems.at[i])
        for i, (src, dst) in enumerate(
            (
                (vel_hbm, vel_ref),
                (str_hbm, str_ref),
                (mass_hbm, mass_ref),
                (strength_hbm, strength_ref),
            )
        )
    ]
    for fetch in fetches:
        fetch.start()

    half_rows = BX_DEV // 2
    columns = owner_ref.shape[1]

    def dot(x, y):
        return jnp.dot(
            x.astype(jnp.bfloat16), y.astype(jnp.bfloat16), preferred_element_type=jnp.float32
        )

    def square(rows, cols):
        return (
            lax.broadcasted_iota(jnp.int32, (rows, cols), 0),
            lax.broadcasted_iota(jnp.int32, (rows, cols), 1),
        )

    row, col = square(columns, devices)
    of_lat = jnp.where(row // BY_DEV == col % lat_count, 1.0, 0.0)
    iced = jnp.where(owner_ref[...] >= 0, 1.0, 0.0)
    row, col = square(2 * lon_count, owner_ref.shape[0])
    of_half = jnp.where(col // half_rows == row, 1.0, 0.0)
    per_tile = dot(dot(of_half, iced), of_lat)
    row, col = square(2 * lon_count, devices)
    mine = row // 2 == col // lat_count
    counts = [
        jnp.sum(jnp.where(mine & (row % 2 == h), per_tile, 0.0), axis=0, keepdims=True)
        for h in range(2)
    ]
    row, col = square(devices, devices)
    upto = jnp.where(row <= col, 1.0, 0.0)
    both = jnp.broadcast_to(counts[0] + counts[1], (8, devices))
    end_second = dot(both, upto)[:1]
    end_first = end_second - counts[1]
    number = (lax.broadcasted_iota(jnp.int32, (devices, slots), 1) * devices + own_ref[0]).astype(
        jnp.float32
    )
    place = jnp.zeros((1, slots), jnp.float32)
    for end in (end_first, end_second):
        column = jnp.broadcast_to(end, (devices, devices)).T[:, :1]
        place = place + jnp.sum(jnp.where(column <= number, 1.0, 0.0), axis=0, keepdims=True)
    pos_ref[...] = place.astype(jnp.int32)
    to_scalar = pltpu.make_async_copy(pos_ref, place_ref, sems.at[4])
    to_scalar.start()

    def turn(field, planes):
        scr_ref[field, pl.ds(planes[0], slots, stride=8), :] = jnp.concatenate(planes[1], axis=0).T

    def scatter(first, fields, sem):
        def body(slot, carry):
            rows = pl.ds(pl.multiple_of(slot * 8, 8), 8)
            place = place_ref[0, slot]
            pltpu.make_async_copy(
                scr_ref.at[pl.ds(first, fields), rows, :],
                send_ref.at[place >> 1, pl.ds((place & 1) * (FIELDS + 1) + first, fields)],
                sem,
            ).start()
            return carry

        lax.fori_loop(0, slots, body, 0, unroll=8)
        everything = send_ref.at[pl.ds(0, slots), pl.ds(0, fields)]
        return pltpu.make_async_copy(everything, everything, sem)

    first_row = row_ids((B, slots)) == 0

    def south(x):
        return jnp.where(first_row, 0.0, pltpu.roll(x, 1, 0))

    def stresses(ci):
        total, diff = str_ref[0, ci], str_ref[1, ci]
        return 0.5 * (total + diff), 0.5 * (total - diff), str_ref[2, ci]

    fetches[0].wait()
    for c in range(2):
        for s in range(8):
            turn(c, (s, [vel_ref[c, 8 * q + s] for q in range(4)]))
    fetches[1].wait()
    for s in range(8):
        push_x, push_y = [], []
        for q in range(4):
            p, n, shear = stresses(8 * q + s)
            gx = p + (shear - south(shear))
            gy = shear + (n - south(n))
            if q or s:
                p_west, _, shear_west = stresses(8 * q + s - 1)
                gx, gy = gx - p_west, gy - shear_west
            push_x.append(gx)
            push_y.append(gy)
        turn(2, (s, push_x))
        turn(3, (s, push_y))
    p, _, shear = stresses(B - 1)
    shear_top = str_ref[2, :, B - 1, :]
    n_top = 0.5 * (str_ref[0, :, B - 1, :] - str_ref[1, :, B - 1, :])
    edge_ref[...] = jnp.concatenate((p, shear, shear_top, n_top), axis=0).T
    to_scalar.wait()
    waits = [scatter(0, 4, sems.at[5])]

    def stage(slot, carry):
        place = place_ref[0, slot]
        stage_ref[place >> 1, pl.ds(place & 1, 1), :] = edge_ref[pl.ds(slot, 1), :]
        return carry

    lax.fori_loop(0, slots, stage, 0, unroll=8)
    edges = pltpu.make_async_copy(stage_ref, send_ref.at[:, FIELDS], sems.at[7])
    edges.start()
    for field, ref in ((4, mass_ref), (5, strength_ref)):
        fetches[field - 2].wait()
        for s in range(8):
            turn(field, (s, [ref[8 * q + s] for q in range(4)]))
    waits.append(scatter(4, 2, sems.at[6]))
    for wait in waits:
        wait.wait()
    edges.wait()


def start_edges(tile_ref, recv_hbm, edge_ref, sem, places, first, last):
    count = recv_hbm.shape[0]

    def fetch(i, carry):
        for side, (bx, by) in enumerate(places(i)):
            start = jnp.int32(bx >= BX_DEV // 2) * FIELDS
            block = recv_hbm.at[tile_ref[bx, by] & (count - 1), pl.ds(start, FIELDS + 1)]
            pltpu.make_async_copy(block, edge_ref.at[side * BX_DEV + i], sem).start()
        return carry

    lax.fori_loop(first, last, fetch, 0, unroll=4)
    everything = edge_ref.at[pl.ds(0, 2 * (last - first))]
    return pltpu.make_async_copy(everything, everything, sem)


def lat_kernel(tile_ref, even_ref, recv_hbm, force_ref, near_ref, far_ref, edge_ref, sems):
    in_group = lane_ids((8, LANES)) % 32
    edges = (0, BY_DEV - 1)
    middle = BX_DEV // 2
    waits = [
        start_edges(
            tile_ref,
            recv_hbm,
            edge_ref,
            sems.at[half],
            lambda i: [(i, by) for by in edges],
            half * middle,
            (half + 1) * middle,
        )
        for half in range(2)
    ]

    def lat_rims(half):
        def body(bx, carry):
            found = []
            for side, (by, first) in enumerate(zip(edges, (0, B - HALO))):
                place = side * BX_DEV + bx
                iced = tile_ref[bx, by] >= 0
                vectors = []
                for v in range(2):
                    total = jnp.zeros((8, LANES), jnp.float32)
                    for k in range(PER_RIM):
                        field = v * PER_RIM + k
                        if field >= FIELDS:
                            got = force_ref[bx * BY_DEV + by, field - FIELDS]
                        else:
                            got = jnp.where(iced, edge_ref[place, half + field], 0.0)
                        mine = (in_group >= HALO * k) & (in_group < HALO * (k + 1))
                        got = pltpu.roll(got, (HALO * k - first) % LANES, 1)
                        total = jnp.where(mine, got, total)
                    vectors.append(total)
                row = edge_ref[place, FIELDS * (1 - half), half : half + 1, :]
                found.append(vectors + [jnp.where(iced, row, 0.0)])
            even = even_ref[0] == 1
            for ref, kept in ((near_ref, even), (far_ref, jnp.logical_not(even))):
                first_v, second_v, row = [jnp.where(kept, y, x) for x, y in zip(*found)]
                ref[bx * 2] = first_v
                ref[bx * 2 + 1] = second_v
                ref[BX_DEV * 2 + half, pl.ds(bx % 8, 1), :] = row
            return carry

        return body

    waits[0].wait()
    lax.fori_loop(0, middle, lat_rims(0), 0, unroll=2)
    waits[1].wait()
    lax.fori_loop(middle, BX_DEV, lat_rims(1), 0, unroll=2)


def lon_kernel(tile_ref, even_ref, recv_hbm, force_ref, near_ref, far_ref, edge_ref, sem):
    group_of = lane_ids((8, LANES)) // 32
    edges = (0, BX_DEV - 1)
    even = even_ref[0] == 1
    places = lambda i: [(bx, i) for bx in edges]
    start_edges(tile_ref, recv_hbm, edge_ref, sem, places, 0, BY_DEV).wait()

    def keep(first, last, index):
        near_ref[index] = jnp.where(even, last, first)
        far_ref[index] = jnp.where(even, first, last)

    for part in range(4):
        for field in range(FIELDS + 2):
            found = []
            for side, (bx, group) in enumerate(zip(edges, (0, 3))):
                half = int(bx >= BX_DEV // 2)
                total = jnp.zeros((8, LANES), jnp.float32)
                for p in range(4):
                    by = part * 4 + p
                    if field >= FIELDS:
                        got = force_ref[bx * BY_DEV + by, field - FIELDS]
                    else:
                        got = edge_ref[side * BX_DEV + by, half + field]
                        got = jnp.where(tile_ref[bx, by] >= 0, got, 0.0)
                    turned = pltpu.roll(got, ((p - group) * 32) % LANES, 1) if p != group else got
                    total = jnp.where(group_of == p, turned, total)
                found.append(total)
            keep(*found, field * 4 + part)
    sub = row_ids((8, LANES))
    for v in range(BY_DEV // 8):
        found = []
        for side, bx in enumerate(edges):
            half = int(bx >= BX_DEV // 2)
            total = jnp.zeros((8, LANES), jnp.float32)
            for r in range(8):
                by = v * 8 + r
                row = edge_ref[side * BX_DEV + by, FIELDS * (1 - half), half : half + 1, :]
                row = jnp.where(tile_ref[bx, by] >= 0, row, 0.0)
                total = jnp.where(sub == r, row, total)
            found.append(total)
        keep(*found, 4 * (FIELDS + 2) + v)


def collect_kernel(tile_ref, recv_ref, force_ref, scr_ref):
    count = recv_ref.shape[0]
    rest = SIDE * SIDE * 8
    for field in range(FIELDS + 3):
        scr_ref[field, pl.ds(rest, GRID_LANES * 8 - rest), :] = jnp.zeros(
            (GRID_LANES * 8 - rest, LANES), jnp.float32
        )

    def collect(half):
        def body(bx, carry):
            for by in range(BY_DEV):
                number = tile_ref[bx, by]
                source = number & (count - 1)
                iced = number >= 0
                for field in range(FIELDS):
                    scr_ref[field, grid_rows(bx, by), :] = jnp.where(
                        iced, recv_ref[source, half * (FIELDS + 1) + field], 0.0
                    )
                for c in range(2):
                    scr_ref[FIELDS + c, grid_rows(bx, by), :] = force_ref[bx * BY_DEV + by, c]
                row = recv_ref[source, FIELDS, half : half + 1, :]
                scr_ref[EDGE, grid_row(bx, by), :] = jnp.where(iced, row, 0.0)
            return carry

        return body

    lax.fori_loop(0, BX_DEV // 2, collect(0), 0)
    lax.fori_loop(BX_DEV // 2, BX_DEV, collect(1), 0)


def force_kernel(force_ref, out_ref):
    def body(bx, carry):
        for part in range(4):
            for c in range(2):
                rows = [
                    force_ref[
                        c,
                        pl.ds(pl.multiple_of(bx * B + 8 * q, 8), 8),
                        pl.ds(part * LANES, LANES),
                    ]
                    for q in range(4)
                ]
                for p, block in enumerate(swap_groups(rows)):
                    out_ref[bx * BY_DEV + part * 4 + p, c] = block
        return carry

    lax.fori_loop(0, BX_DEV, body, 0)


def velocity_kernel(vel_ref, out_ref, scr_ref):
    for c in range(2):
        for t in range(GRID_LANES // LANES):
            for s in range(8):
                cells = [vel_ref[c, 8 * q + s, :, pl.ds(t * LANES, LANES)] for q in range(4)]
                scr_ref[c, pl.ds(t * 8 * LANES + s, LANES, stride=8), :] = jnp.concatenate(
                    cells, axis=0
                ).T

    def body(bx, carry):
        for part in range(4):
            for c in range(2):
                blocks = [
                    scr_ref[
                        c,
                        pl.ds(pl.multiple_of(((bx + 1) * SIDE + part * 4 + p + 1) * 8, 8), 8),
                        :,
                    ]
                    for p in range(4)
                ]
                for q, rows in enumerate(swap_groups(blocks)):
                    out_ref[
                        c,
                        pl.ds(pl.multiple_of(bx * B + 8 * q, 8), 8),
                        pl.ds(part * LANES, LANES),
                    ] = rows
        return carry

    lax.fori_loop(0, BX_DEV, body, 0)


def tile_kernel(
    place_ref,
    lat_ref,
    blocks_ref,
    cell_ref,
    near_ref,
    far_ref,
    lon_near_ref,
    lon_far_ref,
    scr_ref,
    vel_out_ref,
    send_out_ref,
    z_ref,
    m_ref,
    p_ref,
    q_ref,
    s_ref,
    a_ref,
    b_ref,
    fx_ref,
    fy_ref,
    w_ref,
    gx_ref,
    gy_ref,
    turn_ref,
    edge_ref,
    send_ref,
    sems,
):
    del blocks_ref
    lane = lane_ids((8, LANES))
    tiles = GRID_LANES // LANES
    fields = FIELDS + 2
    spot = grid_rows
    in_group = lane % 32

    even = lat_ref[2] == 1

    def either(x, y):
        return jnp.where(even, x, y), jnp.where(even, y, x)

    def lat_rim(bx, near, far, near_row, far_row):
        north_row, south_row = either(near_row, far_row)
        for field in range(fields):
            v, k = divmod(field, PER_RIM)
            north, south = either(near(v), far(v))
            got = pltpu.roll(north, (-HALO * k) % LANES, 1)
            scr_ref[field, spot(bx, BY_DEV), :] = jnp.where(in_group < HALO, got, 0.0)
            got = pltpu.roll(south, (B - HALO - HALO * k) % LANES, 1)
            scr_ref[field, spot(bx, -1), :] = jnp.where(in_group >= B - HALO, got, 0.0)
        scr_ref[EDGE, grid_row(bx, BY_DEV), :] = north_row
        scr_ref[EDGE, grid_row(bx, -1), :] = south_row

    def lat_rims(bx, carry):
        lat_rim(
            bx,
            lambda v: near_ref[bx * 2 + v],
            lambda v: far_ref[bx * 2 + v],
            near_ref[BX_DEV * 2 + bx // 8, pl.ds(bx % 8, 1), :],
            far_ref[BX_DEV * 2 + bx // 8, pl.ds(bx % 8, 1), :],
        )
        return carry

    lax.fori_loop(0, BX_DEV, lat_rims, 0)
    lon_even = lat_ref[3] == 1

    def west(i):
        return jnp.where(lon_even, lon_far_ref[i], lon_near_ref[i])

    def east(i):
        return jnp.where(lon_even, lon_near_ref[i], lon_far_ref[i])

    for rim, bx, group, row in ((west, -1, 3, 7), (east, BX_DEV, 0, 0)):
        for field in range(fields):
            for part in range(4):
                whole = rim(field * 4 + part)
                for p in range(4):
                    got = pltpu.roll(whole, ((group - p) * 32) % LANES, 1)
                    scr_ref[field, spot(bx, part * 4 + p), :] = jnp.where(
                        lane // 32 == group, got, 0.0
                    )
        for by in range(BY_DEV):
            scr_ref[EDGE, grid_row(bx, by), :] = rim(fields * 4 + by // 8)[by % 8 : by % 8 + 1]
        lat_rim(
            bx,
            lambda v: rim(LON_RIM + v),
            lambda v: rim(LON_RIM + 2 + v),
            rim(LON_RIM + 4)[row : row + 1],
            rim(LON_RIM + 5)[row : row + 1],
        )

    def turn_edges(t, carry):
        start = pl.multiple_of(t * 8 * LANES, 8 * LANES)
        edge_ref[:, pl.ds(pl.multiple_of(t * LANES, LANES), LANES)] = scr_ref[
            EDGE, pl.ds(start, LANES, stride=8), :
        ].T
        return carry

    lax.fori_loop(0, tiles, turn_edges, 0)
    edge_ref[: 2 * B, :] = pltpu.roll(edge_ref[: 2 * B, :], SIDE, 1)
    edge_ref[2 * B :, :] = pltpu.roll(edge_ref[2 * B :, :], 1, 1)
    top_row = row_ids((8, LANES)) == 0

    def prepare(t, carry):
        cols = pl.ds(pl.multiple_of(t * LANES, LANES), LANES)
        for s in range(8):
            start = pl.multiple_of(t * 8 * LANES, 8 * LANES) + s
            turned = [
                scr_ref[field, pl.ds(start, LANES, stride=8), :].T for field in range(fields)
            ]
            for q in range(4):
                plane = 8 * q + s
                zonal, merid, push_x, push_y, mass, strength, fzonal, fmerid = [
                    x[q * B : (q + 1) * B] for x in turned
                ]

                def less(push, base):
                    row = edge_ref[base + plane : base + plane + 1, cols]
                    top = push[:8] - jnp.where(top_row, row, 0.0)
                    return jnp.concatenate((top, push[8:]), axis=0)

                push_x, push_y = less(push_x, 2 * B), less(push_y, 3 * B)
                if plane == 0:
                    push_x = push_x - edge_ref[:B, cols]
                    push_y = push_y - edge_ref[B : 2 * B, cols]
                drag = jnp.where(mass > 0.0, 0.5 / (mass + 0.5), 0.0)
                z_ref[plane + 1, :, cols] = zonal
                m_ref[plane + 1, :, cols] = merid
                for ref in (p_ref, q_ref, s_ref):
                    ref[plane + 1, :, cols] = jnp.zeros((B, LANES), jnp.float32)
                a_ref[plane, :, cols] = 2.0 * mass * drag
                b_ref[plane, :, cols] = drag
                fx_ref[plane, :, cols] = drag * fzonal
                fy_ref[plane, :, cols] = drag * fmerid
                gx_ref[plane, :, cols] = drag * push_x
                gy_ref[plane, :, cols] = drag * push_y
                w_ref[plane, :, cols] = 0.25 * strength
        return carry

    lax.fori_loop(0, tiles, prepare, 0)

    cell = cell_ref[...] + lat_ref[0] * COLS
    turn_ref[...] = (0.5 * CORIOLIS) * (
        2.0 * (cell.astype(jnp.float32) + 0.5) / (lat_ref[1] * COLS).astype(jnp.float32) - 1.0
    )

    sub = row_ids((8, LANES))
    first_row = sub == 0
    last_row = sub == 7

    def north_of(x, edge):
        top = jnp.where(first_row, edge, x[:8])
        return pltpu.roll(jnp.concatenate((top, x[8:]), axis=0), B - 1, 0)

    def south_of(x, edge):
        bottom = jnp.where(last_row, edge, x[B - 8 :])
        return pltpu.roll(jnp.concatenate((x[: B - 8], bottom), axis=0), 1, 0)

    def stress_plane(k):
        z_edge = pltpu.roll(z_ref[k, pl.ds(0, 8), :], GRID_LANES - 1, 1)
        m_edge = pltpu.roll(m_ref[k, pl.ds(0, 8), :], GRID_LANES - 1, 1)
        for t in range(tiles):
            cols = slice(t * LANES, (t + 1) * LANES)
            z, m, w = z_ref[k, :, cols], m_ref[k, :, cols], w_ref[k - 1, :, cols]
            gx = z_ref[k + 1, :, cols] - z
            hx = m_ref[k + 1, :, cols] - m
            gy = north_of(m, m_edge[:, cols]) - m
            hy = north_of(z, z_edge[:, cols]) - z
            div = gx + gy
            ten = gx - gy
            she = hy + hx
            weight = w * lax.rsqrt(div * div + 0.25 * (ten * ten + she * she) + 0.25)
            quarter = 0.25 * weight
            mean = weight * div - w
            dev = quarter * ten
            p_ref[k, :, cols] = 0.5 * p_ref[k, :, cols] + (mean + dev)
            q_ref[k, :, cols] = 0.5 * q_ref[k, :, cols] + (mean - dev)
            s_ref[k, :, cols] = 0.5 * s_ref[k, :, cols] + quarter * she

    def momentum_plane(k, share):
        s_edge = pltpu.roll(s_ref[k, pl.ds(B - 8, 8), :], 1, 1)
        q_edge = pltpu.roll(q_ref[k, pl.ds(B - 8, 8), :], 1, 1)
        for t in range(tiles):
            cols = slice(t * LANES, (t + 1) * LANES)
            z, m = z_ref[k, :, cols], m_ref[k, :, cols]
            a, b = a_ref[k - 1, :, cols], b_ref[k - 1, :, cols]
            s, q = s_ref[k, :, cols], q_ref[k, :, cols]
            push_x = (p_ref[k, :, cols] - p_ref[k - 1, :, cols]) + (
                s - south_of(s, s_edge[:, cols])
            )
            push_y = (s - s_ref[k - 1, :, cols]) + (q - south_of(q, q_edge[:, cols]))
            turn = turn_ref[:, cols]
            z_ref[k, :, cols] = (
                a * (z + turn * m) + b * push_x + (fx_ref[k - 1, :, cols] + share * gx_ref[k - 1, :, cols])
            )
            m_ref[k, :, cols] = (
                a * (m - turn * z) + b * push_y + (fy_ref[k - 1, :, cols] + share * gy_ref[k - 1, :, cols])
            )

    def sweep(step, share):
        for ref in (z_ref, m_ref):
            ref[B + 1] = pltpu.roll(ref[1], GRID_LANES - SIDE, 1)
        stress_plane(B)
        for ref in (p_ref, s_ref):
            ref[0] = pltpu.roll(ref[B], SIDE, 1)
        stress_plane(1)

        def body(k, carry):
            stress_plane(k + 1)
            momentum_plane(k, share)
            return carry

        lax.fori_loop(1, B - 1, body, 0, unroll=True)
        for k in (B - 1, B):
            momentum_plane(k, share)
        return 0.5 * share

    lax.fori_loop(0, ITERS, sweep, jnp.float32(0.5))
    copies = [
        pltpu.make_async_copy(ref.at[pl.ds(1, B)], vel_out_ref.at[c], sems.at[c])
        for c, ref in enumerate((z_ref, m_ref))
    ]
    for copy in copies:
        copy.start()

    def total(k, cols):
        return p_ref[k, :, cols] + q_ref[k, :, cols]

    def difference(k, cols):
        return p_ref[k, :, cols] - q_ref[k, :, cols]

    def shear(k, cols):
        return s_ref[k, :, cols]

    for c, value in enumerate((total, difference, shear)):
        for t in range(tiles):
            cols = slice(t * LANES, (t + 1) * LANES)
            for s in range(8):
                cells = [value(8 * q + s + 1, cols) for q in range(4)]
                scr_ref[c, pl.ds(t * 8 * LANES + s, LANES, stride=8), :] = jnp.concatenate(
                    cells, axis=0
                ).T

        def deal(bx, carry, c=c):
            for by in range(BY_DEV):
                send_ref[place_ref[bx, by], c] = scr_ref[c, spot(bx, by), :]
            return carry

        lax.fori_loop(0, BX_DEV, deal, 0, unroll=2)
        copies.append(
            pltpu.make_async_copy(
                send_ref.at[pl.ds(0, send_out_ref.shape[0]), c],
                send_out_ref.at[:, c],
                sems.at[2 + c],
            )
        )
        copies[-1].start()
    for copy in copies:
        copy.wait()


def unpack_kernel(pos_ref, recv_ref, stress_hbm, out_hbm, out_ref, stress_ref, scr_ref, sems):
    slots = out_ref.shape[-1]
    old, done = [], []
    for c in range(3):
        old.append(pltpu.make_async_copy(stress_hbm.at[c], stress_ref.at[c], sems.at[c]))
        done.append(pltpu.make_async_copy(out_ref.at[c], out_hbm.at[c], sems.at[3 + c]))
        old[c].start()

    def gather(slot, carry):
        place = pos_ref[0, slot]
        rows = pl.ds(pl.multiple_of(slot * 8, 8), 8)
        for c in range(3):
            scr_ref[c, rows, :] = recv_ref[place, c]
        return carry

    lax.fori_loop(0, slots, gather, 0, unroll=8)
    for c in range(3):
        old[c].wait()
        for s in range(8):
            turned = scr_ref[c, pl.ds(s, slots, stride=8), :].T
            for q in range(4):
                ci = 8 * q + s
                out_ref[c, ci] = turned[q * B : (q + 1) * B] + 0.5**ITERS * stress_ref[c, ci]
        done[c].start()
    for copy in done:
        copy.wait()


VMEM = pl.BlockSpec(memory_space=pltpu.VMEM)
SMEM = pl.BlockSpec(memory_space=pltpu.SMEM)
HBM = pl.BlockSpec(memory_space=pltpu.HBM)


def params(mebibytes):
    return pltpu.CompilerParams(vmem_limit_bytes=mebibytes * 1024 * 1024)


def cost(mebibytes):
    return pl.CostEstimate(flops=10**7, bytes_accessed=mebibytes * 2**20, transcendentals=0)


def f32(*shape):
    return jax.ShapeDtypeStruct(shape, jnp.float32)


def on_device(forcing, velocity, stress, mass, strength, owner):
    lon_count = lax.axis_size("lon")
    lat_count = lax.axis_size("lat")
    devices = lon_count * lat_count
    lat_index = lax.axis_index("lat")
    lon_index = lax.axis_index("lon")
    own_index = lon_index * lat_count + lat_index
    slots = velocity.shape[-1]

    my_tile = lax.dynamic_slice(owner, (lon_index * BX_DEV, lat_index * BY_DEV), (BX_DEV, BY_DEV))

    block = (B, B, slots)
    send, pos = pl.pallas_call(
        pack_kernel,
        out_shape=(
            pltpu.HBM((devices, MESSAGE, 8, LANES), jnp.float32),
            jax.ShapeDtypeStruct((1, slots), jnp.int32),
        ),
        in_specs=[SMEM, VMEM] + [HBM] * 4,
        out_specs=(HBM, VMEM),
        scratch_shapes=[
            pltpu.VMEM((2,) + block, jnp.float32),
            pltpu.VMEM((3,) + block, jnp.float32),
            pltpu.VMEM(block, jnp.float32),
            pltpu.VMEM(block, jnp.float32),
            pltpu.VMEM((FIELDS, slots * 8, LANES), jnp.float32),
            pltpu.VMEM((slots, LANES), jnp.float32),
            pltpu.VMEM((devices, 8, LANES), jnp.float32),
            pltpu.SMEM((1, slots), jnp.int32),
            pltpu.SemaphoreType.DMA((8,)),
        ],
        compiler_params=params(61),
    )(own_index.reshape(1).astype(jnp.int32), owner, velocity, stress, mass, strength)
    recv = lax.all_to_all(send, ("lon", "lat"), 0, 0, tiled=True)

    force_blocks = pl.pallas_call(
        force_kernel,
        out_shape=f32(BX_DEV * BY_DEV, 2, 8, LANES),
        in_specs=[VMEM],
        out_specs=VMEM,
        cost_estimate=cost(4),
        compiler_params=params(12),
    )(forcing)
    edge_scratch = [
        pltpu.VMEM((2 * BX_DEV, FIELDS + 1, 8, LANES), jnp.float32),
        pltpu.SemaphoreType.DMA(()),
    ]
    even = 1 - lat_index % 2
    near, far = pl.pallas_call(
        lat_kernel,
        out_shape=(f32(LAT_RIM, 8, LANES),) * 2,
        in_specs=[SMEM, SMEM, HBM, VMEM],
        out_specs=(VMEM,) * 2,
        scratch_shapes=[edge_scratch[0], pltpu.SemaphoreType.DMA((2,))],
        cost_estimate=cost(4),
        compiler_params=params(8),
    )(my_tile, even.reshape(1).astype(jnp.int32), recv, force_blocks)
    lon_even = 1 - lon_index % 2
    lon_near, lon_far = pl.pallas_call(
        lon_kernel,
        out_shape=(f32(LON_RIM, 8, LANES),) * 2,
        in_specs=[SMEM, SMEM, HBM, VMEM],
        out_specs=(VMEM,) * 2,
        scratch_shapes=edge_scratch,
        cost_estimate=cost(6),
        compiler_params=params(8),
    )(my_tile, lon_even.reshape(1).astype(jnp.int32), recv, force_blocks)
    blocks = pl.pallas_call(
        collect_kernel,
        out_shape=pltpu.VMEM((FIELDS + 3, GRID_LANES * 8, LANES), jnp.float32),
        in_specs=[SMEM, VMEM, VMEM],
        out_specs=VMEM,
        cost_estimate=cost(24),
        compiler_params=params(12),
    )(my_tile, recv, force_blocks)

    def exchange(rim, first):
        pairs = [(j, j + 1) for j in range(first, lat_count - 1, 2)]
        return lax.ppermute(rim, "lat", pairs + [(k, j) for j, k in pairs])

    got_near = exchange(near, 0)
    got_far = exchange(far, 1)
    end = BX_DEV * 2
    rows = BX_DEV // 8

    def with_corners(rim, last):
        pairs = [jnp.where(last, x[end - 2 : end], x[:2]) for x in (got_near, got_far)]
        edge = [jnp.where(last, x[end + rows - 1 :], x[end : end + 1]) for x in (got_near, got_far)]
        return jnp.concatenate([rim] + pairs + edge, axis=0)

    def exchange_lon(rim, first):
        pairs = [(i, (i + 1) % lon_count) for i in range(first, lon_count, 2)]
        return lax.ppermute(rim, "lon", pairs + [(k, i) for i, k in pairs])

    got_lon_near = exchange_lon(with_corners(lon_near, lon_even == 1), 0)
    got_lon_far = exchange_lon(with_corners(lon_far, lon_even == 0), 1)
    grid = np.arange(GRID_LANES) % SIDE - 1
    cells = jnp.asarray(grid[None, :] * B + np.arange(B)[:, None], jnp.int32)
    state = (B + 2, B, GRID_LANES)
    constant = (B, B, GRID_LANES)
    half = (jnp.arange(BX_DEV, dtype=jnp.int32) // (BX_DEV // 2))[:, None]
    places = jnp.where(my_tile >= 0, (my_tile & (devices - 1)) * 2 + half, 2 * devices)
    _, cell_velocity, back = pl.pallas_call(
        tile_kernel,
        out_shape=(
            pltpu.VMEM((FIELDS + 3, GRID_LANES * 8, LANES), jnp.float32),
            pltpu.HBM((2, B, B, GRID_LANES), jnp.float32),
            pltpu.HBM((devices * 2, 3, 8, LANES), jnp.float32),
        ),
        in_specs=[SMEM, SMEM] + [VMEM] * 6,
        out_specs=(VMEM, HBM, HBM),
        input_output_aliases={2: 0},
        scratch_shapes=[pltpu.VMEM(state, jnp.float32)] * 5
        + [pltpu.VMEM(constant, jnp.float32)] * 7
        + [
            pltpu.VMEM((B, GRID_LANES), jnp.float32),
            pltpu.VMEM((4 * B, GRID_LANES), jnp.float32),
            pltpu.VMEM((devices * 2 + 1, 3, 8, LANES), jnp.float32),
            pltpu.SemaphoreType.DMA((5,)),
        ],
        compiler_params=params(26),
    )(
        places,
        jnp.stack((lat_index, lat_count, even, lon_even)).astype(jnp.int32),
        blocks,
        cells,
        got_near,
        got_far,
        got_lon_near,
        got_lon_far,
    )
    returned = lax.all_to_all(
        back.reshape(devices, 6, 8, LANES), ("lon", "lat"), 0, 0, tiled=True
    ).reshape(devices * 2, 3, 8, LANES)
    new_velocity = pl.pallas_call(
        velocity_kernel,
        out_shape=f32(2, ROWS, COLS),
        in_specs=[VMEM],
        out_specs=VMEM,
        scratch_shapes=[pltpu.VMEM((2, GRID_LANES * 8, LANES), jnp.float32)],
        cost_estimate=cost(6),
        compiler_params=params(16),
    )(cell_velocity)
    new_stress = pl.pallas_call(
        unpack_kernel,
        out_shape=pltpu.HBM((3,) + block, jnp.float32),
        in_specs=[SMEM, VMEM, HBM],
        out_specs=HBM,
        scratch_shapes=[
            pltpu.VMEM((3,) + block, jnp.float32),
            pltpu.VMEM((3,) + block, jnp.float32),
            pltpu.VMEM((3, slots * 8, LANES), jnp.float32),
            pltpu.SemaphoreType.DMA((6,)),
        ],
        compiler_params=params(16),
    )(pos, returned, pltpu.with_memory_space_constraint(stress, pltpu.HBM))
    return (new_velocity, new_stress)


def solution(mesh):
    in_specs = (
        P(None, "lon", "lat"),
        P(None, None, None, ("lon", "lat")),
        P(None, None, None, ("lon", "lat")),
        P(None, None, ("lon", "lat")),
        P(None, None, ("lon", "lat")),
        P(),
    )
    out_specs = (P(None, "lon", "lat"), P(None, None, None, ("lon", "lat")))
    return jax.shard_map(
        on_device, mesh=mesh, in_specs=in_specs, out_specs=out_specs, check_vma=False
    )
```
